32 devices in a mesh: section: 2 (over core), dp: 16 (over z, y, x).
Axes of the slice: x: 2, y: 2, z: 4, core: 2. Of those that a mesh axis runs over, the one named last changes fastest.
Arguments:
- features: bfloat16 [50176, 1024], P('dp')
- image_group: int32 [256], replicated, may hold values from 0 to 511, as said below
- token_ids: int32 [8192], P('dp'), may hold values from 0 to 31999
- text_lengths: int32 [16, 32], P('dp'), may hold values from 1 to 32, 512 in all within a row
- cotangent: float32 [8192, 768], P('dp'), may hold values from -6 to 6
- table_master: float32 [32000, 768], P(('section', 'dp')), may hold values from -6 to 6
- table_momentum: float32 [32000, 768], P(('section', 'dp')), may hold values from -1.5 to 1.5
- table_average: float32 [32000, 768], P(('section', 'dp')), may hold values from -6 to 6
- block_master: float32 [768, 9216], P(('section', 'dp'))
- block_momentum: float32 [768, 9216], P(('section', 'dp')), may hold values from -28 to 28
- block_average: float32 [768, 9216], P(('section', 'dp')), may hold values from -0.21875 to 0.21875
- project_master: float32 [4096, 768], P(('section', 'dp')), may hold values from -0.109375 to 0.109375
- project_momentum: float32 [4096, 768], P(('section', 'dp')), may hold values from -28 to 28
- project_average: float32 [4096, 768], P(('section', 'dp')), may hold values from -0.109375 to 0.109375
- vector_master: float32 [11264], P(('section', 'dp'))
- vector_momentum: float32 [11264], P(('section', 'dp')), may hold values from -28 to 28
- vector_average: float32 [11264], P(('section', 'dp')), may hold values from 0.5 to 1.5
Outputs:
- block_out: bfloat16 [8192, 768], P('dp', 'section')
- feature_grad: float32 [50176, 1024], P('dp', 'section')
- table_grad: float32 [32000, 768], P(('section', 'dp'))
- table_momentum_new: float32 [32000, 768], P(('section', 'dp'))
- table_average_new: float32 [32000, 768], P(('section', 'dp'))
- table_master_new: float32 [32000, 768], P(('section', 'dp'))
- table_copy: bfloat16 [32000, 768], P(('section', 'dp'))
- block_grad: float32 [768, 9216], P(('section', 'dp'))
- block_momentum_new: float32 [768, 9216], P(('section', 'dp'))
- block_average_new: float32 [768, 9216], P(('section', 'dp'))
- block_master_new: float32 [768, 9216], P(('section', 'dp'))
- block_copy: bfloat16 [768, 9216], P(('section', 'dp'))
- project_grad: float32 [4096, 768], P(('section', 'dp'))
- project_momentum_new: float32 [4096, 768], P(('section', 'dp'))
- project_average_new: float32 [4096, 768], P(('section', 'dp'))
- project_master_new: float32 [4096, 768], P(('section', 'dp'))
- project_copy: bfloat16 [4096, 768], P(('section', 'dp'))
- vector_grad: float32 [11264], P(('section', 'dp'))
- vector_momentum_new: float32 [11264], P(('section', 'dp'))
- vector_average_new: float32 [11264], P(('section', 'dp'))
- vector_master_new: float32 [11264], P(('section', 'dp'))
- vector_copy: bfloat16 [11264], P(('section', 'dp'))
The draws below stay inside these ranges and needn't reach their ends.
Inputs may be any that keep to these rules, and one draw needn't show every extreme that they name: `image_group`: no group is named twice, so some groups are named by no image. Of the 16 images of one stem device at most 2 name groups of one text device, and exactly 2 do for some pair; some text device has all its 32 groups named. `text_lengths`: each row sums to 512, and its largest entry is 32.
All inputs are finite; a program needn't handle non-finite values.
Results may differ from the reference program's by a relative error of at most 0.015.
Values may be sent and summed in bfloat16 or wider, within the bound.
No kernel may reach another device: no remote copies, remote signals or barrier semaphores. Data moves between devices by JAX's collectives and lax.ppermute only.
A program may use at most 448 MiB of HBM per device.

```python
import math
import jax
import jax.numpy as jnp
import numpy as np
from jax import lax

D = 768
HEADS = 12
HEAD_DIM = 64
FF = 3072
VOCAB = 32000
CH = 1024
PATCH = 196
TOK_DEV = 512
IMG_DEV = 16
GROUPS_DEV = 32
LONGEST = 32
PATCH_DEV = 3136
IMAGES = 256
TOKENS = 8192
PATCHES = 50176
N_DP = 16


def draw_features(key, part):
    key = jax.random.fold_in(key, 11)
    first, second, third, fourth = jax.random.split(key, 4)
    device_place = (jnp.arange(PATCHES) // PATCH_DEV).astype(jnp.float32) / max(N_DP - 1, 1)
    base = jax.random.normal(first, (PATCHES, CH), jnp.float32)
    device_scale = 10.0 ** (0.5 * device_place)
    row_scale = 10.0 ** jax.random.uniform(fourth, (PATCHES,), jnp.float32, 0.0, 1.0)
    column_scale = 10.0 ** jax.random.uniform(second, (CH,), jnp.float32, 0.0, 1.0)
    offset = jax.random.uniform(third, (CH,), jnp.float32, 0.5, 1.5)
    scales = device_scale * row_scale
    values = column_scale[None, :] * scales[:, None] * (base + offset[None, :])
    return values.astype(jnp.bfloat16)


def draw_block_master(key, part):
    key = jax.random.fold_in(key, 23)
    values = jax.random.normal(key, (D, 8 * D + FF), jnp.float32) * D ** (-0.5)
    columns = jnp.arange(8 * D + FF)
    larger = (columns >= 3 * D) & (columns < 4 * D) | (columns >= 7 * D) & (columns < 8 * D)
    return values * jnp.where(larger, 4.0, 1.0)[None, :]


def draw_vector_master(key, part):
    key = jax.random.fold_in(key, 37)
    first, second = jax.random.split(key)
    places = jnp.arange(2 * CH + 8 * D + FF)
    offset = 2 * CH + D
    gains = (places < CH) | (places >= offset) & (places < offset + D) | (places >= offset + 2 * D) & (places < offset + 3 * D) | (places >= offset + 4 * D) & (places < offset + 5 * D)
    gain_values = jax.random.uniform(first, places.shape, jnp.float32, 0.5, 1.5)
    bias_values = jax.random.uniform(second, places.shape, jnp.float32, -0.5, 0.5)
    return jnp.where(gains, gain_values, bias_values)


def relabel(values, first, second):
    return jnp.where(values == first, second, jnp.where(values == second, first, values))


def draw_image_group(key, part):
    key = jax.random.fold_in(key, 5)
    keys = jax.random.split(key, 5)
    pairs = N_DP // 2
    order = jax.random.permutation(keys[0], N_DP)
    first_share = jax.random.randint(keys[1], (pairs,), 0, 2 * IMG_DEV + 1)
    forced = jax.random.randint(keys[2], (), 0, pairs)
    first_share = jnp.where(jnp.arange(pairs) == forced, 2 * IMG_DEV, first_share)
    pair_counts = jnp.stack([first_share, 2 * IMG_DEV - first_share], axis=1).reshape(N_DP)
    counts = jnp.zeros((N_DP,), jnp.int32).at[order].set(pair_counts.astype(jnp.int32))
    ends = jnp.cumsum(counts)
    starts = ends - counts
    places = jnp.arange(IMAGES, dtype=jnp.int32)
    target = jnp.sum((places[:, None] >= ends[None, :]).astype(jnp.int32), axis=1).astype(jnp.int32)
    within = places - starts[target]
    shift = jax.random.randint(keys[4], (), 0, IMAGES).astype(jnp.int32)
    first_place = (N_DP - shift % N_DP) % N_DP
    owner_first = target[first_place]
    last_places = (N_DP - 1 - shift) % N_DP + N_DP * jnp.arange(IMG_DEV, dtype=jnp.int32)
    last_targets = target[last_places]
    pick = jnp.argmax((last_targets != owner_first).astype(jnp.int32))
    owner_last = last_targets[pick]
    target = relabel(target, owner_first, N_DP - 1)
    owner_last = jnp.where(owner_last == N_DP - 1, owner_first, owner_last)
    target = relabel(target, owner_last, 0)
    group_order = jax.vmap(lambda one: jax.random.permutation(one, GROUPS_DEV))(jax.random.split(keys[3], N_DP))
    chosen = target * GROUPS_DEV + group_order[target, within]
    turned = (places + shift) % IMAGES
    image_index = turned % N_DP * IMG_DEV + turned // N_DP
    return jnp.zeros((IMAGES,), jnp.int32).at[image_index].set(chosen.astype(jnp.int32))


def set_ends(array, own_key, low, top_value):
    longest = array.shape.index(max(array.shape))
    spots = []
    for shift in (0, 1):
        where = [jax.random.randint(jax.random.fold_in(own_key, axis), (), 0, length) for axis, length in enumerate(array.shape)]
        where[longest] = (where[longest] + shift) % array.shape[longest]
        spots.append(tuple(where))
    return array.at[spots[0]].set(low).at[spots[1]].set(top_value)


def steps_of(rng, dims, cuts, low, high):
    gain, own = 1.0, jax.random.fold_in(rng, 6)
    for position, blocks in cuts:
        heights = jnp.exp(jax.random.uniform(jax.random.fold_in(own, position), (blocks,), jnp.float32, low / len(cuts), high / len(cuts)))
        gain = gain * jnp.repeat(heights, dims[position] // blocks).reshape([-1 if axis == position else 1 for axis in range(len(dims))])
    return gain


def rank_bounds(amount, lean):
    weights = [(1 << 20) // math.isqrt(grade ** lean) + 1 for grade in range(1, amount + 1)]
    scale = 1 + sum(weights) // (1 << 30)
    return np.cumsum(np.array([max(1, weight // scale) for weight in weights]))


def ranked(rng, extent, count, lean):
    grid = rank_bounds(count, lean)
    ticket = jax.random.randint(jax.random.fold_in(rng, 1), extent, 0, int(grid[count - 1]))
    standing = jnp.searchsorted(jnp.asarray(grid, jnp.int32), ticket, side="right")
    return jax.random.permutation(jax.random.fold_in(rng, 2), count)[standing].astype(jnp.int32)


def length_profile(count, total, most, slope):
    weights = [(1 << 20) // math.isqrt(rank ** slope) + 1 for rank in range(2, count + 1)]
    surplus, given = total - most - (count - 1), [1] * (count - 1)
    while surplus > 0:
        free = [i for i in range(count - 1) if given[i] < most]
        pool, budget = sum([weights[i] for i in free]), surplus
        for i in free:
            more = min(most - given[i], max(1, budget * weights[i] // pool), surplus)
            given[i] = given[i] + more
            surplus = surplus - more
    return np.array([most] + given)


def uneven_parts(own_key, number_of, total, limit, slope):
    if number_of == 2:
        one = jax.random.randint(own_key, (), max(1, total - limit), min(limit, total - 1) + 1)
        return jnp.stack([one, total - one])
    lengths = jnp.asarray(length_profile(number_of, total, limit, slope), jnp.int32)
    pairs = (number_of - 1) // 2
    giver, receiver = lengths[1:1 + 2 * pairs:2], lengths[2:2 + 2 * pairs:2]
    margin = jnp.minimum(giver - 1, limit - receiver)
    passed = jax.random.randint(jax.random.fold_in(own_key, 1), (pairs,), 0, 1 << 20) % (margin + 1)
    lengths = lengths.at[1:1 + 2 * pairs:2].set(giver - passed).at[2:2 + 2 * pairs:2].set(receiver + passed)
    return lengths[jax.random.permutation(jax.random.fold_in(own_key, 2), number_of)]


def gaussian(rng, shape, scale, limit, cuts=(), held_as=jnp.bfloat16):
    loudness = steps_of(rng, shape, cuts, -0.22, 0.18) if cuts else 1.0
    array = jax.random.normal(rng, shape, jnp.float32) * scale * loudness
    return jnp.minimum(jnp.maximum(array, -limit), limit).astype(held_as)


def setup_inputs(seed: int = 0) -> dict:
    seeds = jax.random.split(jax.random.key(seed), 18)
    return {
        "features": draw_features(jax.random.fold_in(seeds[17], 71), 0),
        "image_group": draw_image_group(jax.random.fold_in(seeds[17], 71), 0),
        "token_ids": set_ends(ranked(seeds[2], (TOKENS,), VOCAB, 2), jax.random.fold_in(seeds[2], 3), 0, VOCAB - 1).astype(jnp.int32),
        "text_lengths": jax.vmap(lambda own: uneven_parts(own, GROUPS_DEV, TOK_DEV, LONGEST, 2))(jax.random.split(seeds[3], N_DP)).reshape((N_DP, GROUPS_DEV)).astype(jnp.int32),
        "cotangent": gaussian(seeds[4], (TOKENS, D), 1.0, 6.0, ((0, 16),), jnp.float32),
        "table_master": gaussian(seeds[5], (VOCAB, D), 1.0, 6.0, ((0, 32),), jnp.float32),
        "table_momentum": gaussian(seeds[6], (VOCAB, D), 0.1, 1.5, ((0, 32),), jnp.float32),
        "table_average": gaussian(seeds[7], (VOCAB, D), 1.0, 6.0, ((0, 32),), jnp.float32),
        "block_master": draw_block_master(jax.random.fold_in(seeds[17], 71), 0),
        "block_momentum": gaussian(seeds[9], (D, 8 * D + FF), (0.05 * TOKENS ** 0.5), 28.0, ((0, 32),), jnp.float32),
        "block_average": gaussian(seeds[10], (D, 8 * D + FF), D ** -0.5, 0.21875, ((0, 32),), jnp.float32),
        "project_master": gaussian(seeds[11], (CH + FF, D), FF ** -0.5, 0.109375, ((0, 32),), jnp.float32),
        "project_momentum": gaussian(seeds[12], (CH + FF, D), (0.05 * TOKENS ** 0.5), 28.0, ((0, 32),), jnp.float32),
        "project_average": gaussian(seeds[13], (CH + FF, D), FF ** -0.5, 0.109375, ((0, 32),), jnp.float32),
        "vector_master": draw_vector_master(jax.random.fold_in(seeds[17], 71), 0),
        "vector_momentum": gaussian(seeds[15], (2 * CH + 8 * D + FF,), (0.05 * TOKENS ** 0.5), 28.0, ((0, 32),), jnp.float32),
        "vector_average": jnp.clip(1.0 + 0.1 * jax.random.normal(seeds[16], (2 * CH + 8 * D + FF,), jnp.float32), 0.5, 1.5),
    }


@jax.custom_vjp
def low(v):
    return lax.optimization_barrier(v.astype(jnp.bfloat16)).astype(jnp.float32)

@jax.custom_vjp
def low_back(v):
    return v

def low_keep(v):
    return (low(v), None)

def low_pass(kept, grad):
    return (grad,)

def back_keep(v):
    return (v, None)

def back_low(kept, grad):
    return (low(grad),)
low.defvjp(low_keep, low_pass)
low_back.defvjp(back_keep, back_low)

def matmul(left, right):
    return jnp.dot(left, right, precision=lax.Precision.HIGHEST, preferred_element_type=jnp.float32)

def gelu_tanh(values):
    return jax.nn.gelu(values, approximate=True)

def layer_norm(values, gain_vec, bias_vec):
    center = lax.optimization_barrier(jnp.mean(values, axis=-1, keepdims=True))
    shifted = values - center
    spread = lax.optimization_barrier(jnp.mean(shifted * shifted, axis=-1, keepdims=True))
    return shifted * lax.rsqrt(spread + 1e-05) * gain_vec + bias_vec

def split_vector(vector):
    offset = 2 * CH + D
    return (vector[:CH], vector[CH:2 * CH], vector[2 * CH:offset], vector[offset:offset + D], vector[offset + D:offset + 2 * D], vector[offset + 2 * D:offset + 3 * D], vector[offset + 3 * D:offset + 4 * D], vector[offset + 4 * D:offset + 5 * D], vector[offset + 5 * D:offset + 6 * D], vector[offset + 6 * D:offset + 6 * D + FF], vector[offset + 6 * D + FF:])

def attention(queries, key_rows, value_rows, allowed, row_weight):
    heads_q = queries.reshape(queries.shape[0], HEADS, HEAD_DIM)
    heads_k = key_rows.reshape(key_rows.shape[0], HEADS, HEAD_DIM)
    heads_v = value_rows.reshape(value_rows.shape[0], HEADS, HEAD_DIM)
    scores = jnp.einsum('thc,shc->hts', heads_q, heads_k, precision=lax.Precision.HIGHEST) * HEAD_DIM ** (-0.5)
    scores = low_back(scores)
    scores = jnp.where(allowed[None], scores, -1e+30)
    highest = lax.optimization_barrier(jnp.max(scores, axis=-1, keepdims=True))
    weights = jnp.exp(scores - highest)
    shares = low(weights / lax.optimization_barrier(jnp.sum(weights, axis=-1, keepdims=True))) * row_weight[None, :, None]
    mixed_rows = jnp.einsum('hts,shc->thc', shares, heads_v, precision=lax.Precision.HIGHEST)
    return mixed_rows.reshape(queries.shape[0], HEADS * HEAD_DIM)

def forward(table_f, block_f, project_f, vector_f, features_f, token_ids, segments, group_image, group_has):
    table_w = low(table_f)
    block_w = low(block_f)
    project_w = low(project_f)
    bn_gain, bn_bias, patch_bias, gain_one, bias_one, gain_two, bias_two, gain_three, bias_three, up_bias, down_bias = split_vector(low(vector_f))
    w_qkv = block_w[:, :3 * D]
    w_out = block_w[:, 3 * D:4 * D]
    w_cross_q = block_w[:, 4 * D:5 * D]
    w_cross_kv = block_w[:, 5 * D:7 * D]
    w_cross_out = block_w[:, 7 * D:8 * D]
    w_up = block_w[:, 8 * D:]
    w_patch = project_w[:CH]
    w_down = project_w[CH:]
    center = lax.optimization_barrier(jnp.mean(features_f, axis=0))
    shifted = features_f - center
    spread = lax.optimization_barrier(jnp.mean(shifted * shifted, axis=0))
    stem_pre = shifted * lax.rsqrt(spread + 1e-05) * bn_gain + bn_bias
    stem_hidden = low(gelu_tanh(stem_pre))
    patches = low_back(low(matmul(stem_hidden, w_patch) + patch_bias))
    cross_kv = low_back(low(matmul(patches, w_cross_kv))).reshape(IMAGES, PATCH, 2 * D)
    embedded = low_back(jnp.take(table_w, token_ids, axis=0))
    places = jnp.arange(TOK_DEV, dtype=jnp.int32)
    earlier_ok = places[:, None] >= places[None, :]
    key_group = jnp.repeat(jnp.arange(GROUPS_DEV, dtype=jnp.int32), PATCH)
    every_row = jnp.ones((TOK_DEV,), jnp.float32)

    def one_device(inputs):
        resid_zero, segment, image_rows, has_rows = inputs
        causal = (segment[:, None] == segment[None, :]) & earlier_ok
        group_kv = jnp.take(cross_kv, image_rows, axis=0).reshape(GROUPS_DEV * PATCH, 2 * D)
        visible = segment[:, None] == key_group[None, :]
        attends = jnp.take(has_rows, segment)
        normed_one = low(layer_norm(resid_zero, gain_one, bias_one))
        qkv_rows = low_back(low(matmul(normed_one, w_qkv)))
        self_mix = low_back(low(attention(qkv_rows[:, :D], qkv_rows[:, D:2 * D], qkv_rows[:, 2 * D:], causal, every_row)))
        resid_one = resid_zero + low_back(matmul(self_mix, w_out))
        normed_two = low(layer_norm(resid_one, gain_two, bias_two))
        cross_q = low_back(low(matmul(normed_two, w_cross_q)))
        cross_mix = low_back(low(attention(cross_q, group_kv[:, :D], group_kv[:, D:], visible, attends)))
        resid_two = resid_one + low_back(matmul(cross_mix, w_cross_out))
        normed_three = low(layer_norm(resid_two, gain_three, bias_three))
        up_rows = low_back(matmul(normed_three, w_up) + up_bias)
        up_act = low(gelu_tanh(up_rows))
        return resid_two + low_back(matmul(up_act, w_down)) + down_bias
    outputs = lax.map(jax.checkpoint(one_device), (embedded.reshape(N_DP, TOK_DEV, D), segments, group_image, group_has))
    return outputs.reshape(N_DP * TOK_DEV, D)

def sgd_update(gradient, momentum, master, average, step_rate):
    new_momentum = 0.9 * momentum + gradient
    new_master = master - step_rate * (gradient + 0.9 * new_momentum)
    new_average = 0.8 * average + 0.2 * new_master
    return (gradient, new_momentum, new_average, new_master, new_master.astype(jnp.bfloat16))

def reference(features, image_group, token_ids, text_lengths, cotangent, table_master, table_momentum, table_average, block_master, block_momentum, block_average, project_master, project_momentum, project_average, vector_master, vector_momentum, vector_average):
    places = jnp.arange(TOK_DEV, dtype=jnp.int32)
    group_ends = jnp.cumsum(text_lengths, axis=1).astype(jnp.int32)
    segments = lax.optimization_barrier(jnp.sum((places[None, :, None] >= group_ends[:, None, :]).astype(jnp.int32), axis=-1)).astype(jnp.int32)
    group_ids = jnp.arange(N_DP * GROUPS_DEV, dtype=jnp.int32).reshape(N_DP, GROUPS_DEV)
    image_index = jnp.arange(IMAGES, dtype=jnp.int32)
    match = image_group[None, None, :] == group_ids[:, :, None]
    group_has = jnp.any(match, axis=-1).astype(jnp.float32)
    group_image = lax.optimization_barrier(jnp.sum(jnp.where(match, image_index[None, None, :], 0), axis=-1)).astype(jnp.int32)

    def wrapped(table_f, block_f, project_f, vector_f, features_f):
        return forward(table_f, block_f, project_f, vector_f, features_f, token_ids, segments, group_image, group_has)
    block_out, pullback = jax.vjp(wrapped, table_master, block_master, project_master, vector_master, features.astype(jnp.float32))
    table_grad, block_grad, project_grad, vector_grad, feature_grad = pullback(cotangent)
    root_tokens = (TOK_DEV * N_DP) ** 0.5
    table_new = sgd_update(table_grad, table_momentum, table_master, table_average, 0.05)
    block_new = sgd_update(block_grad, block_momentum, block_master, block_average, 0.5 * D ** (-0.5) / root_tokens)
    project_new = sgd_update(project_grad, project_momentum, project_master, project_average, 0.5 * FF ** (-0.5) / root_tokens)
    vector_new = sgd_update(vector_grad, vector_momentum, vector_master, vector_average, 0.1 / root_tokens)
    return (block_out.astype(jnp.bfloat16), feature_grad, table_new[0], table_new[1], table_new[2], table_new[3], table_new[4], block_new[0], block_new[1], block_new[2], block_new[3], block_new[4], project_new[0], project_new[1], project_new[2], project_new[3], project_new[4], vector_new[0], vector_new[1], vector_new[2], vector_new[3], vector_new[4])
```

```python
import functools
import math

import jax
import jax.numpy as jnp
from jax import lax
from jax.experimental import pallas as pl
from jax.experimental.pallas import tpu as pltpu
from jax.sharding import PartitionSpec as P

D = 768
HEADS = 12
HEAD_DIM = 64
QUAD = 4 * HEAD_DIM
QUADS = HEADS // 4
FF = 3072
CH = 1024
PATCH = 196
WINDOW = 208
IMG_DEV = 16
GROUPS_DEV = 32
LONGEST = 32
HALF_ROWS = LONGEST // 2
BLOCK = 128
SPAN = BLOCK + LONGEST
SCALE = HEAD_DIM ** (-0.5)
EPS = 1e-05
NEG = -1e30
BOTH = ("section", "dp")
VMEM_BYTES = 58 * 1024 * 1024
bf16 = jnp.bfloat16
f32 = jnp.float32
i32 = jnp.int32


def mm(left, right):
    return jnp.dot(left, right, preferred_element_type=f32)


def mm_rt(left, right):
    return lax.dot_general(left, right, (((1,), (1,)), ((), ())), preferred_element_type=f32)


def mm_lt(left, right):
    return lax.dot_general(left, right, (((0,), (0,)), ((), ())), preferred_element_type=f32)


def normalise(values):
    shifted = values - jnp.mean(values, axis=-1, keepdims=True)
    factor = lax.rsqrt(jnp.mean(shifted * shifted, axis=-1, keepdims=True) + EPS)
    return shifted * factor, factor


def norm_back(incoming, unit, factor, gain):
    scaled = incoming * gain
    mean_grad = jnp.mean(scaled, axis=-1, keepdims=True)
    mean_cross = jnp.mean(scaled * unit, axis=-1, keepdims=True)
    return factor * (scaled - mean_grad - unit * mean_cross)


GELU_C = math.sqrt(2.0 / math.pi)


def gelu_parts(values):
    square = values * values
    bend = jnp.tanh(GELU_C * values * (1.0 + 0.044715 * square))
    half = 0.5 * (1.0 + bend)
    slope = half + 0.5 * values * (1.0 - bend * bend) * (GELU_C * (1.0 + 3 * 0.044715 * square))
    return values * half, slope


def gelu_only(values):
    bend = jnp.tanh(GELU_C * values * (1.0 + 0.044715 * (values * values)))
    return 0.5 * values * (1.0 + bend)


def head_masks(dtype):
    lanes = lax.broadcasted_iota(i32, (1, QUAD), 1) // HEAD_DIM
    return [jnp.where(lanes == h, 1.0, 0.0).astype(dtype) for h in range(4)]


def spread_heads(rows, masks):
    return jnp.concatenate([rows * m for m in masks], axis=0)


def join_heads(stacked, masks):
    count = stacked.shape[0] // 4
    total = stacked[:count] * masks[0]
    for h in range(1, 4):
        total = total + stacked[h * count : (h + 1) * count] * masks[h]
    return total


def softmax(scores, allowed):
    scores = jnp.where(allowed, scores * SCALE, NEG)
    weights = jnp.exp(scores - jnp.max(scores, axis=-1, keepdims=True))
    return weights * (1.0 / jnp.sum(weights, axis=-1, keepdims=True))


def one_hot_cols(index_col, width):
    places = lax.broadcasted_iota(i32, (index_col.shape[0], width), 1)
    return jnp.where(places == index_col, 1.0, 0.0).astype(bf16)


def one_hot_rows(index_row, height, offset=0):
    places = lax.broadcasted_iota(i32, (height, index_row.shape[1]), 0) + offset
    return jnp.where(places == index_row, 1.0, 0.0).astype(bf16)


def join_halves(target, low_ref, high_ref):
    count = low_ref.shape[0]
    target[:count, :] = low_ref[...]
    target[count : 2 * count, :] = high_ref[...]


def self_allowed(start_rows, first):
    rows = lax.broadcasted_iota(i32, (BLOCK, SPAN), 0) + first
    keys = lax.broadcasted_iota(i32, (BLOCK, SPAN), 1) + (first - LONGEST)
    allowed = (keys <= rows) & (keys >= start_rows)
    return jnp.concatenate([jnp.where(allowed, 1, 0)] * 4, axis=0) > 0


def text_first(
    embed, start, pack_a, pack_b, vecs,
    qkv_lo, qkv_hi, out_lo, out_hi, cq_lo, cq_hi,
    qkv_rows, mix_rows, resid_one, slots_a, slots_b,
    w_qkv, w_out, w_cq, padded,
):
    tokens = embed.shape[0]
    join_halves(w_qkv, qkv_lo, qkv_hi)
    join_halves(w_out, out_lo, out_hi)
    join_halves(w_cq, cq_lo, cq_hi)
    values = embed[...].astype(f32)
    unit, _ = normalise(values)
    normed = (unit * vecs[0:1, :] + vecs[1:2, :]).astype(bf16)
    for third in range(3):
        columns = slice(third * D, (third + 1) * D)
        qkv_rows[:, columns] = mm(normed, w_qkv[:, columns]).astype(bf16)
    padded[:LONGEST, :] = jnp.zeros((LONGEST, 2 * D), bf16)
    padded[LONGEST : LONGEST + tokens, :] = qkv_rows[:, D:]
    masks = head_masks(bf16)
    masks_f = head_masks(f32)

    def block(index, carry):
        first = pl.multiple_of(index * BLOCK, BLOCK)
        allowed = self_allowed(start[pl.ds(first, BLOCK), :], first)
        for quad in range(QUADS):
            lanes = slice(quad * QUAD, (quad + 1) * QUAD)
            later = slice(D + quad * QUAD, D + (quad + 1) * QUAD)
            queries = spread_heads(qkv_rows[pl.ds(first, BLOCK), lanes], masks)
            shares = softmax(mm_rt(queries, padded[pl.ds(first, SPAN), lanes]), allowed)
            mixed = mm(shares.astype(bf16), padded[pl.ds(first, SPAN), later])
            mix_rows[pl.ds(first, BLOCK), lanes] = join_heads(mixed, masks_f).astype(bf16)
        return carry

    lax.fori_loop(0, tokens // BLOCK, block, 0)
    resid = values + mm(mix_rows[...], w_out[...])
    resid_one[...] = resid
    unit, _ = normalise(resid)
    normed = (unit * vecs[2:3, :] + vecs[3:4, :]).astype(bf16)
    queries = mm(normed, w_cq[...]).astype(bf16)
    slots_a[...] = mm(one_hot_cols(pack_a[...], tokens), queries).astype(bf16)
    slots_b[...] = mm(one_hot_cols(pack_b[...], tokens), queries).astype(bf16)


def text_middle(
    mix_a, mix_b, take_a, take_b, pack_a, pack_b, resid_one, cotangent, vecs, up_bias,
    cout_lo, cout_hi, up_lo, up_hi, w_down,
    block_out, grad_two, grad_up_w, grad_down_w, grad_cout_w, slots_a, slots_b,
    vec_grad, up_bias_grad,
    w_cout, w_up, mixed, normed, normed_t, unit_s, factor_s, total, back, grad_down,
):
    step = pl.program_id(0)
    tokens = resid_one.shape[0]

    @pl.when(step == 0)
    def _():
        join_halves(w_cout, cout_lo, cout_hi)
        rows = mm(one_hot_rows(take_a[...], tokens), mix_a[...])
        rows = rows + mm(one_hot_rows(take_b[...], tokens), mix_b[...])
        mixed[...] = rows.astype(bf16)
        resid_two = resid_one[...] + mm(mixed[...], w_cout[...])
        unit, factor = normalise(resid_two)
        unit_s[...] = unit
        factor_s[...] = factor
        rows = unit * vecs[0:1, :] + vecs[1:2, :]
        normed[...] = rows.astype(bf16)
        normed_t[...] = rows.astype(bf16).T
        total[...] = resid_two + vecs[2:3, :]
        back[...] = jnp.zeros_like(back)
        grad_down[...] = cotangent[...].astype(bf16)
        vec_grad[2:3, :] = jnp.sum(cotangent[...], axis=0, keepdims=True)

    join_halves(w_up, up_lo, up_hi)
    up = mm(normed[...], w_up[...]) + up_bias[...]
    act, slope = gelu_parts(up)
    act = act.astype(bf16)
    total[...] += mm(act, w_down[...])
    grad_up_f = mm_rt(grad_down[...], w_down[...]) * slope
    grad_up = grad_up_f.astype(bf16)
    up_bias_grad[...] = jnp.sum(grad_up.astype(f32), axis=0, keepdims=True)
    grad_down_w[...] = mm_lt(act, grad_down[...]).astype(bf16)
    grad_up_w[...] = mm(normed_t[...], grad_up).astype(bf16)
    back[...] += mm_rt(grad_up, w_up[...])

    @pl.when(step == pl.num_programs(0) - 1)
    def _():
        block_out[...] = total[...].astype(bf16)
        incoming, unit = back[...], unit_s[...]
        vec_grad[0:1, :] = jnp.sum(incoming * unit, axis=0, keepdims=True)
        vec_grad[1:2, :] = jnp.sum(incoming, axis=0, keepdims=True)
        grad = cotangent[...] + norm_back(incoming, unit, factor_s[...], vecs[0:1, :])
        grad_two[...] = grad
        grad = grad.astype(bf16)
        grad_cout_w[...] = mm_lt(mixed[...], grad).astype(bf16)
        grad = mm_rt(grad, w_cout[...]).astype(bf16)
        slots_a[...] = mm(one_hot_cols(pack_a[...], tokens), grad).astype(bf16)
        slots_b[...] = mm(one_hot_cols(pack_b[...], tokens), grad).astype(bf16)


def text_last(
    grad_a, grad_b, take_a, take_b, place, grad_two, resid_one, embed, qkv_rows, mix_rows, start, vecs,
    qkv_lo, qkv_hi, out_lo, out_hi, cq_lo, cq_hi,
    grad_embed, rows_a, rows_b, grad_w, vec_grad,
    w_qkv, w_out, w_cq, padded, grad_mix, grad_qkv, total,
):
    tokens = embed.shape[0]
    join_halves(w_qkv, qkv_lo, qkv_hi)
    join_halves(w_out, out_lo, out_hi)
    join_halves(w_cq, cq_lo, cq_hi)
    grad_q = mm(one_hot_rows(take_a[...], tokens), grad_a[...])
    grad_q = (grad_q + mm(one_hot_rows(take_b[...], tokens), grad_b[...])).astype(bf16)
    unit, factor = normalise(resid_one[...])
    normed = (unit * vecs[2:3, :] + vecs[3:4, :]).astype(bf16)
    grad_w[:, 4 * D : 5 * D] = mm_lt(normed, grad_q).astype(bf16)
    incoming = mm_rt(grad_q, w_cq[...])
    vec_grad[2:3, :] = jnp.sum(incoming * unit, axis=0, keepdims=True)
    vec_grad[3:4, :] = jnp.sum(incoming, axis=0, keepdims=True)
    grad_one = grad_two[...] + norm_back(incoming, unit, factor, vecs[2:3, :])
    grad_low = grad_one.astype(bf16)
    grad_w[:, 3 * D : 4 * D] = mm_lt(mix_rows[...], grad_low).astype(bf16)
    grad_mix[...] = mm_rt(grad_low, w_out[...]).astype(bf16)
    padded[:LONGEST, :] = jnp.zeros((LONGEST, 2 * D), bf16)
    padded[LONGEST : LONGEST + tokens, :] = qkv_rows[:, D:]
    total[...] = jnp.zeros_like(total)
    masks = head_masks(bf16)
    masks_f = head_masks(f32)

    def block(index, carry):
        first = pl.multiple_of(index * BLOCK, BLOCK)
        allowed = self_allowed(start[pl.ds(first, BLOCK), :], first)
        for quad in range(QUADS):
            lanes = slice(quad * QUAD, (quad + 1) * QUAD)
            later = slice(D + quad * QUAD, D + (quad + 1) * QUAD)
            queries = spread_heads(qkv_rows[pl.ds(first, BLOCK), lanes], masks)
            grads = spread_heads(grad_mix[pl.ds(first, BLOCK), lanes], masks)
            keys = padded[pl.ds(first, SPAN), lanes]
            shares = softmax(mm_rt(queries, keys), allowed)
            grad_shares = mm_rt(grads, padded[pl.ds(first, SPAN), later])
            inner = jnp.sum(grad_shares * shares, axis=-1, keepdims=True)
            grad_scores = (shares * (grad_shares - inner)).astype(bf16)
            grad_queries = join_heads(mm(grad_scores, keys), masks_f) * SCALE
            grad_qkv[pl.ds(first, BLOCK), lanes] = grad_queries.astype(bf16)
            total[pl.ds(first, SPAN), lanes] += mm_lt(grad_scores, queries) * SCALE
            total[pl.ds(first, SPAN), later] += mm_lt(shares.astype(bf16), grads)
        return carry

    lax.fori_loop(0, tokens // BLOCK, block, 0)
    grad_qkv[:, D:] = total[LONGEST : LONGEST + tokens, :].astype(bf16)
    unit, factor = normalise(embed[...].astype(f32))
    normed = (unit * vecs[0:1, :] + vecs[1:2, :]).astype(bf16)
    for third in range(3):
        columns = slice(third * D, (third + 1) * D)
        grad_w[:, columns] = mm_lt(normed, grad_qkv[:, columns]).astype(bf16)
    incoming = mm_rt(grad_qkv[...], w_qkv[...])
    vec_grad[0:1, :] = jnp.sum(incoming * unit, axis=0, keepdims=True)
    vec_grad[1:2, :] = jnp.sum(incoming, axis=0, keepdims=True)
    grad_low = (grad_one + norm_back(incoming, unit, factor, vecs[0:1, :])).astype(bf16)
    grad_embed[...] = grad_low
    count = rows_a.shape[0]
    rows_a[...] = mm(one_hot_rows(place[...], count), grad_low).astype(bf16)
    rows_b[...] = mm(one_hot_rows(place[...], count, count), grad_low).astype(bf16)


def unpack_rows(rows_a, rows_b, place, embed):
    count = rows_a.shape[0]
    total = mm(one_hot_cols(place[...], count), rows_a[...])
    total = total + mm(one_hot_cols(place[...] - count, count), rows_b[...])
    embed[...] = total.astype(bf16)


def stem_forward(
    features, bn, w_patch, patch_bias, kv_lo0, kv_hi0, kv_lo1, kv_hi1, patches, kv, w_kv
):
    @pl.when(pl.program_id(0) == 0)
    def _():
        join_halves(w_kv.at[:, :D], kv_lo0, kv_hi0)
        join_halves(w_kv.at[:, D:], kv_lo1, kv_hi1)

    normed = (features[...].astype(f32) - bn[0:1, :]) * bn[1:2, :]
    hidden = gelu_only(normed * bn[2:3, :] + bn[3:4, :]).astype(bf16)
    rows = (mm(hidden, w_patch[...]) + patch_bias[...]).astype(bf16)
    patches[...] = rows
    kv[...] = mm(rows, w_kv[...]).astype(bf16)


def image_window(image):
    first = image * PATCH
    aligned = pl.multiple_of(first // 16 * 16, 16)
    lanes = lax.broadcasted_iota(i32, (1, WINDOW), 1) + (aligned - first)
    return aligned, (lanes >= 0) & (lanes < PATCH)


def cross_forward(slot, q_a, q_b, kv, mix_a, mix_b):
    mix_a[...] = jnp.zeros_like(mix_a)
    mix_b[...] = jnp.zeros_like(mix_b)
    masks = head_masks(bf16)
    masks_f = head_masks(f32)

    def image(index, carry):
        aligned, allowed = image_window(index)
        place = pl.ds(pl.multiple_of(slot[index] * HALF_ROWS, HALF_ROWS), HALF_ROWS)
        for quad in range(QUADS):
            lanes = slice(quad * QUAD, (quad + 1) * QUAD)
            later = slice(D + quad * QUAD, D + (quad + 1) * QUAD)
            rows = jnp.concatenate([q_a[place, lanes], q_b[place, lanes]], axis=0)
            scores = mm_rt(spread_heads(rows, masks), kv[pl.ds(aligned, WINDOW), lanes])
            shares = softmax(scores, allowed).astype(bf16)
            mixed = join_heads(mm(shares, kv[pl.ds(aligned, WINDOW), later]), masks_f).astype(bf16)
            mix_a[place, lanes] = mixed[:HALF_ROWS]
            mix_b[place, lanes] = mixed[HALF_ROWS:]
        return carry

    lax.fori_loop(0, IMG_DEV, image, 0)


def cross_backward(slot, q_a, q_b, g_a, g_b, kv, grad_a, grad_b, grad_kv):
    grad_a[...] = jnp.zeros_like(grad_a)
    grad_b[...] = jnp.zeros_like(grad_b)
    grad_kv[...] = jnp.zeros_like(grad_kv)
    masks = head_masks(bf16)
    masks_f = head_masks(f32)

    def image(index, carry):
        aligned, allowed = image_window(index)
        place = pl.ds(pl.multiple_of(slot[index] * HALF_ROWS, HALF_ROWS), HALF_ROWS)
        window = pl.ds(aligned, WINDOW)
        for quad in range(QUADS):
            lanes = slice(quad * QUAD, (quad + 1) * QUAD)
            later = slice(D + quad * QUAD, D + (quad + 1) * QUAD)
            rows = jnp.concatenate([q_a[place, lanes], q_b[place, lanes]], axis=0)
            queries = spread_heads(rows, masks)
            rows = jnp.concatenate([g_a[place, lanes], g_b[place, lanes]], axis=0)
            grads = spread_heads(rows, masks)
            keys = kv[window, lanes]
            shares = softmax(mm_rt(queries, keys), allowed)
            grad_shares = mm_rt(grads, kv[window, later])
            inner = jnp.sum(grad_shares * shares, axis=-1, keepdims=True)
            grad_scores = (shares * (grad_shares - inner)).astype(bf16)
            back = (join_heads(mm(grad_scores, keys), masks_f) * SCALE).astype(bf16)
            grad_a[place, lanes] = back[:HALF_ROWS]
            grad_b[place, lanes] = back[HALF_ROWS:]
            grad_kv[window, lanes] += (mm_lt(grad_scores, queries) * SCALE).astype(bf16)
            grad_kv[window, later] += mm_lt(shares.astype(bf16), grads).astype(bf16)
        return carry

    lax.fori_loop(0, IMG_DEV, image, 0)


def stem_backward(
    features, bn, w_patch, kv_lo0, kv_hi0, kv_lo1, kv_hi1, patches, grad_kv,
    grad_lo, grad_hi, grad_kv_w, grad_patch_w, sums, bias_sum,
    w_kv, kv_acc, patch_acc,
):
    step = pl.program_id(0)

    @pl.when(step == 0)
    def _():
        join_halves(w_kv.at[:, :D], kv_lo0, kv_hi0)
        join_halves(w_kv.at[:, D:], kv_lo1, kv_hi1)
        kv_acc[...] = jnp.zeros_like(kv_acc)
        patch_acc[...] = jnp.zeros_like(patch_acc)
        sums[...] = jnp.zeros_like(sums)
        bias_sum[...] = jnp.zeros_like(bias_sum)

    normed = (features[...].astype(f32) - bn[0:1, :]) * bn[1:2, :]
    hidden, slope = gelu_parts(normed * bn[2:3, :] + bn[3:4, :])
    grad_rows = mm_rt(grad_kv[...], w_kv[...]).astype(bf16)
    bias_sum[...] += jnp.sum(grad_rows.astype(f32), axis=0, keepdims=True)
    kv_acc[...] += mm_lt(patches[...], grad_kv[...])
    patch_acc[...] += mm_lt(hidden.astype(bf16), grad_rows)
    grad_pre = mm_rt(grad_rows, w_patch[...]) * slope
    sums[0:1, :] += jnp.sum(grad_pre * normed, axis=0, keepdims=True)
    sums[1:2, :] += jnp.sum(grad_pre, axis=0, keepdims=True)
    grad_low = grad_pre.astype(bf16)
    grad_lo[...] = grad_low[:, : CH // 2]
    grad_hi[...] = grad_low[:, CH // 2 :]

    @pl.when(step == pl.num_programs(0) - 1)
    def _():
        grad_kv_w[...] = kv_acc[...].astype(bf16)
        grad_patch_w[...] = patch_acc[...].astype(bf16)


def shape(dims, dtype):
    return jax.ShapeDtypeStruct(dims, dtype)


def whole(array):
    zeros = (0,) * array.ndim
    return pl.BlockSpec(array.shape, lambda *_: zeros)


def at(dims, *index):
    return pl.BlockSpec(dims, lambda *_: index)


def call(kernel, steps, in_specs, out_specs, outs, scratch, flops):
    return pl.pallas_call(
        kernel,
        grid=(steps,),
        in_specs=in_specs,
        out_specs=out_specs,
        out_shape=outs,
        scratch_shapes=scratch,
        compiler_params=pltpu.CompilerParams(vmem_limit_bytes=VMEM_BYTES),
        cost_estimate=pl.CostEstimate(flops=flops, bytes_accessed=flops // 500, transcendentals=0),
    )


def simple(kernel, inputs, outs, scratch, flops):
    return call(
        kernel,
        1,
        [whole(a) for a in inputs],
        [at(o.shape, *(0,) * len(o.shape)) for o in outs],
        outs,
        scratch,
        flops,
    )(*inputs)


def blank(outs):
    return pl.pallas_call(
        lambda *refs: None,
        out_shape=outs,
        out_specs=[pl.BlockSpec(memory_space=pl.ANY) for _ in outs],
    )()


def doubled(state, axis, count, merge):
    step = 1
    while step < count:
        other = lax.ppermute(state, axis, [(i, i ^ step) for i in range(count)])
        state = merge(state, other, step)
        step *= 2
    return state


def sgd_update(gradient, momentum, master, average, step_rate):
    new_momentum = 0.9 * momentum + gradient
    new_master = master - step_rate * (gradient + 0.9 * new_momentum)
    new_average = 0.8 * average + 0.2 * new_master
    return (gradient, new_momentum, new_average, new_master, new_master.astype(bf16))


def per_device(
    features,
    image_group,
    token_ids,
    text_lengths,
    cotangent,
    table_master,
    table_momentum,
    table_average,
    block_master,
    block_momentum,
    block_average,
    project_master,
    project_momentum,
    project_average,
    vector_master,
    vector_momentum,
    vector_average,
):
    dp = lax.axis_size("dp")
    group = lax.axis_size(BOTH)
    dp_index = lax.axis_index("dp")
    section = lax.axis_index("section")
    is_stem = section == 0
    me = section * dp + dp_index
    tokens = token_ids.shape[0]
    image_rows = features.shape[0]
    every_patch = image_rows * dp
    table_rows = table_master.shape[0]
    images = image_group.shape[0]

    block_full = lax.all_gather(block_master.astype(bf16), BOTH, axis=0, tiled=True)
    project_full = lax.all_gather(project_master.astype(bf16), BOTH, axis=0, tiled=True)

    capacity = (2 * IMG_DEV + dp - 1) // dp
    slots = dp * capacity
    half_slots = slots * HALF_ROWS
    destination = image_group // GROUPS_DEV
    by_source = destination.reshape(dp, IMG_DEV)
    order = jnp.arange(IMG_DEV, dtype=i32)
    earlier = order[None, :] < order[:, None]
    rank_all = jnp.sum(
        ((by_source[:, :, None] == by_source[:, None, :]) & earlier[None]).astype(i32), axis=2
    ).reshape(images)
    my_dest = lax.dynamic_slice_in_dim(destination, dp_index * IMG_DEV, IMG_DEV)
    my_rank = lax.dynamic_slice_in_dim(rank_all, dp_index * IMG_DEV, IMG_DEV)
    stem_slot = my_dest * capacity + my_rank
    slot_of_image = jnp.where(
        destination == dp_index,
        jnp.arange(images, dtype=i32) // IMG_DEV * capacity + rank_all,
        -1,
    )
    lengths = text_lengths[0]
    group_ends = jnp.cumsum(lengths)
    group_starts = group_ends - lengths
    places = jnp.arange(tokens, dtype=i32)
    start = jnp.max(
        jnp.where(group_starts[None, :] <= places[:, None], group_starts[None, :], 0), axis=1
    )
    match = slot_of_image[None, :] == jnp.arange(slots, dtype=i32)[:, None]
    slot_group = jnp.max(jnp.where(match, (image_group % GROUPS_DEV)[None, :], -1), axis=1)
    group_hit = slot_group[:, None] == jnp.arange(GROUPS_DEV, dtype=i32)[None, :]
    slot_start = jnp.sum(jnp.where(group_hit, group_starts[None, :], 0), axis=1)
    slot_length = jnp.sum(jnp.where(group_hit, lengths[None, :], 0), axis=1)
    within = jnp.arange(LONGEST, dtype=i32)
    slot_rows = jnp.where(
        within[None, :] < slot_length[:, None], slot_start[:, None] + within[None, :], -1
    )
    rows_a = slot_rows[:, :HALF_ROWS].reshape(half_slots)
    rows_b = slot_rows[:, HALF_ROWS:].reshape(half_slots)
    pack_a, pack_b = rows_a[:, None], rows_b[:, None]
    take_a, take_b = rows_a[None, :], rows_b[None, :]
    start = start[:, None]

    room = max(16, 2 * tokens // group)
    owner = token_ids // table_rows
    before = places[None, :] < places[:, None]
    same = token_ids[:, None] == token_ids[None, :]
    is_first = ~jnp.any(same & before, axis=1)
    rank = jnp.sum(
        ((owner[:, None] == owner[None, :]) & before & is_first[None, :]).astype(i32), axis=1
    )
    crowded = jnp.any(is_first & (rank >= room))
    first_place = jnp.where(is_first, owner * room + rank, -1)
    place = jnp.max(jnp.where(same, first_place[None, :], -1), axis=1)
    half_room = dp * room
    asked = lax.dynamic_slice_in_dim(
        jnp.max(
            jnp.where(
                first_place[None, :] == jnp.arange(group * room, dtype=i32)[:, None],
                (token_ids % table_rows)[None, :],
                -1,
            ),
            axis=1,
        ),
        section * half_room,
        half_room,
    )
    asked = lax.all_to_all(
        asked.reshape(dp, room), "dp", split_axis=0, concat_axis=0, tiled=True
    ).reshape(half_room)
    table_low = table_master.astype(bf16)
    table_hit = (asked[:, None] == jnp.arange(table_rows, dtype=i32)[None, :]).astype(bf16)
    served = mm(table_hit, table_low).astype(bf16)
    served = lax.all_to_all(
        served.reshape(dp, room, D), "dp", split_axis=0, concat_axis=0, tiled=True
    ).reshape(half_room, D)
    served_low = lax.ppermute(served, "section", [(0, 1)])

    rows_f = features.astype(f32)
    local_center = jnp.mean(rows_f, axis=0)
    local_square = jnp.sum(jnp.square(rows_f - local_center), axis=0)
    vector_own = lax.dynamic_update_slice(
        jnp.zeros((vector_master.shape[0] * group,), f32),
        vector_master.astype(bf16).astype(f32),
        (me * vector_master.shape[0],),
    ).reshape(-1, CH)
    state = jnp.concatenate(
        [
            local_center[None],
            local_square[None],
            jnp.broadcast_to(crowded.astype(f32), (1, CH)),
            vector_own,
        ]
    )

    def merge(mine, other, step):
        delta = other[0] - mine[0]
        squares = mine[1] + other[1] + delta * delta * (0.5 * image_rows * step)
        return jnp.concatenate(
            [(0.5 * (mine[0] + other[0]))[None], squares[None], mine[2:] + other[2:]]
        )

    state = doubled(state, "dp", dp, merge)
    center = state[0]
    factor = lax.rsqrt(state[1] / every_patch + EPS)
    any_crowded = state[2, 0] > 0.5
    vector_full = state[3:] + lax.ppermute(state[3:], "section", [(0, 1), (1, 0)])
    bn_gain, bn_bias = vector_full[0], vector_full[1]
    flat = vector_full.reshape(-1)
    offset = 2 * CH + D
    patch_bias = flat[2 * CH : offset].reshape(1, D)
    ln_vecs = flat[offset : offset + 6 * D].reshape(6, D)
    up_bias = flat[offset + 6 * D : offset + 6 * D + FF].reshape(1, FF)
    down_bias = flat[offset + 6 * D + FF :].reshape(1, D)
    vecs_outer = ln_vecs[:4]
    vecs_three = jnp.concatenate([ln_vecs[4:], down_bias])
    bn = jnp.stack([center, factor, bn_gain, bn_bias])

    def embed_packed():
        return simple(
            unpack_rows,
            [served_low, served, place[:, None]],
            [shape((tokens, D), bf16)],
            [],
            4 * tokens * half_room * D,
        )[0]

    def embed_gathered():
        table_full = lax.all_gather(table_low, BOTH, axis=0, tiled=True)
        return jnp.take(table_full, token_ids, axis=0)

    embed = lax.cond(any_crowded, embed_gathered, embed_packed)

    half = D // 2

    def halves(width, column):
        return [at((half, width), 0, column), at((half, width), 1, column)]

    qkv_specs = halves(3 * D, 0) + halves(D, 3) + halves(D, 4)
    kv_specs = halves(D, 5) + halves(D, 6)
    patch_spec = at((CH, D), 0, 0)
    blocks = 4
    per_block = image_rows // blocks
    qkv_scratch = [
        pltpu.VMEM((D, 3 * D), bf16),
        pltpu.VMEM((D, D), bf16),
        pltpu.VMEM((D, D), bf16),
        pltpu.VMEM((LONGEST + tokens, 2 * D), bf16),
    ]

    def rows_spec(width):
        return pl.BlockSpec((per_block, width), lambda step: (step, 0))

    slot_shape = shape((half_slots, D), bf16)

    text_saved = [
        shape((tokens, 3 * D), bf16),
        shape((tokens, D), bf16),
        shape((tokens, D), f32),
        slot_shape,
        slot_shape,
    ]
    stem_saved = [shape((image_rows, D), bf16), shape((image_rows, 2 * D), bf16)]

    def first_text():
        inputs = [embed, start, pack_a, pack_b, vecs_outer]
        done = call(
            text_first,
            1,
            [whole(a) for a in inputs] + qkv_specs,
            [at(o.shape, 0, 0) for o in text_saved],
            text_saved,
            qkv_scratch,
            2 * tokens * D * 5 * D,
        )(*inputs, *[block_full] * 6)
        return (*done, *blank(stem_saved))

    def first_stem():
        done = call(
            stem_forward,
            blocks,
            [rows_spec(CH), whole(bn), patch_spec, whole(patch_bias)] + kv_specs,
            [rows_spec(D), rows_spec(2 * D)],
            stem_saved,
            [pltpu.VMEM((D, 2 * D), bf16)],
            2 * image_rows * D * (CH + 2 * D),
        )(features, bn, project_full, patch_bias, *[block_full] * 4)
        return (*blank(text_saved), *done)

    qkv_rows, mix_rows, resid_one, q_a, q_b, patches, kv = lax.cond(is_stem, first_stem, first_text)

    def exchange(block):
        return lax.all_to_all(
            block.reshape(dp, capacity * HALF_ROWS, D), "dp", split_axis=0, concat_axis=0, tiled=True
        ).reshape(half_slots, D)

    def to_stem(block_a, block_b):
        moved = lax.ppermute(block_a, "section", [(1, 0)])
        got = exchange(jnp.where(is_stem, moved, block_b))
        return got, lax.ppermute(got, "section", [(1, 0)])

    def to_text(block_a, block_b):
        moved = lax.ppermute(block_b, "section", [(0, 1)])
        got = exchange(jnp.where(is_stem, block_a, moved))
        return lax.ppermute(got, "section", [(0, 1)]), got

    q_a, q_b = to_stem(q_a, q_b)
    slot_spec = pl.BlockSpec(memory_space=pltpu.SMEM)

    def cross_stem():
        return call(
            cross_forward,
            1,
            [slot_spec, whole(q_a), whole(q_b), whole(kv)],
            [whole(q_a), whole(q_b)],
            [slot_shape, slot_shape],
            [],
            4 * IMG_DEV * BLOCK * WINDOW * D,
        )(stem_slot, q_a, q_b, kv)

    mix_a, mix_b = lax.cond(is_stem, cross_stem, lambda: blank([slot_shape, slot_shape]))
    mix_a, mix_b = to_text(mix_a, mix_b)

    chunks = 3
    wide = FF // chunks
    middle_shapes = [
        shape((tokens, D), bf16),
        shape((tokens, D), f32),
        shape((D, FF), bf16),
        shape((FF, D), bf16),
        shape((D, D), bf16),
        slot_shape,
        slot_shape,
        shape((3, D), f32),
        shape((1, FF), f32),
    ]

    def middle_text():
        inputs = [mix_a, mix_b, take_a, take_b, pack_a, pack_b, resid_one, cotangent, vecs_three]
        first_up = 8 * D // wide
        outs = [at(o.shape, *(0,) * len(o.shape)) for o in middle_shapes]
        outs[2] = pl.BlockSpec((D, wide), lambda step: (0, step))
        outs[3] = pl.BlockSpec((wide, D), lambda step: (step, 0))
        outs[8] = pl.BlockSpec((1, wide), lambda step: (0, step))
        return call(
            text_middle,
            chunks,
            [whole(a) for a in inputs]
            + [pl.BlockSpec((1, wide), lambda step: (0, step))]
            + halves(D, 7)
            + [
                pl.BlockSpec((half, wide), lambda step: (0, first_up + step)),
                pl.BlockSpec((half, wide), lambda step: (1, first_up + step)),
                pl.BlockSpec((wide, D), lambda step: (CH // wide + step, 0)),
            ],
            outs,
            middle_shapes,
            [
                pltpu.VMEM((D, D), bf16),
                pltpu.VMEM((D, wide), bf16),
                pltpu.VMEM((tokens, D), bf16),
                pltpu.VMEM((tokens, D), bf16),
                pltpu.VMEM((D, tokens), bf16),
                pltpu.VMEM((tokens, D), f32),
                pltpu.VMEM((tokens, 1), f32),
                pltpu.VMEM((tokens, D), f32),
                pltpu.VMEM((tokens, D), f32),
                pltpu.VMEM((tokens, D), bf16),
            ],
            12 * tokens * D * FF,
        )(*inputs, up_bias, *[block_full] * 4, project_full)

    (
        block_out, grad_two, grad_up_w, grad_down_w, grad_cout_w, g_a, g_b, grads_three, grad_up_bias,
    ) = lax.cond(is_stem, lambda: blank(middle_shapes), middle_text)
    g_a, g_b = to_stem(g_a, g_b)

    def cross_stem_back():
        return call(
            cross_backward,
            1,
            [slot_spec] + [whole(q_a)] * 4 + [whole(kv)],
            [whole(q_a)] * 2 + [whole(kv)],
            [slot_shape, slot_shape, shape(kv.shape, bf16)],
            [],
            10 * IMG_DEV * BLOCK * WINDOW * D,
        )(stem_slot, q_a, q_b, g_a, g_b, kv)

    grad_a, grad_b, grad_kv = lax.cond(
        is_stem, cross_stem_back, lambda: blank([slot_shape, slot_shape, shape(kv.shape, bf16)])
    )
    grad_a, grad_b = to_text(grad_a, grad_b)

    row_shape = shape((half_room, D), bf16)
    text_last_shapes = [
        shape((tokens, D), bf16),
        row_shape,
        row_shape,
        shape((D, 5 * D), bf16),
        shape((4, D), f32),
    ]
    half_channels = CH // 2
    stem_last_shapes = [
        shape((image_rows, half_channels), bf16),
        shape((image_rows, half_channels), bf16),
        shape((D, 2 * D), bf16),
        shape((CH, D), bf16),
        shape((2, CH), f32),
        shape((1, D), f32),
    ]

    def last_text():
        inputs = [
            grad_a, grad_b, take_a, take_b, place[None, :], grad_two, resid_one, embed,
            qkv_rows, mix_rows, start, vecs_outer,
        ]
        done = call(
            text_last,
            1,
            [whole(a) for a in inputs] + qkv_specs,
            [at(o.shape, 0, 0) for o in text_last_shapes],
            text_last_shapes,
            qkv_scratch
            + [
                pltpu.VMEM((tokens, D), bf16),
                pltpu.VMEM((tokens, 3 * D), bf16),
                pltpu.VMEM((LONGEST + tokens, 2 * D), f32),
            ],
            4 * tokens * D * 5 * D,
        )(*inputs, *[block_full] * 6)
        return (*done, *blank(stem_last_shapes))

    def last_stem():
        done = call(
            stem_backward,
            blocks,
            [rows_spec(CH), whole(bn), patch_spec] + kv_specs + [rows_spec(D), rows_spec(2 * D)],
            [rows_spec(half_channels)] * 2
            + [at(o.shape, *(0,) * len(o.shape)) for o in stem_last_shapes[2:]],
            stem_last_shapes,
            [
                pltpu.VMEM((D, 2 * D), bf16),
                pltpu.VMEM((D, 2 * D), f32),
                pltpu.VMEM((CH, D), f32),
            ],
            4 * image_rows * D * (CH + 2 * D),
        )(features, bn, project_full, *[block_full] * 4, patches, grad_kv)
        return (*blank(text_last_shapes), *done)

    (
        grad_embed, rows_low, rows_high, grad_w, grads_outer,
        grad_lo, grad_hi, grad_kv_w, grad_patch_w, bn_sums, patch_bias_sum,
    ) = lax.cond(is_stem, last_stem, last_text)

    def term_stem():
        return (
            jnp.concatenate(
                [jnp.zeros((D, 5 * D), bf16), grad_kv_w, jnp.zeros((D, D + FF), bf16)], axis=1
            ),
            jnp.concatenate([grad_patch_w, jnp.zeros((FF, D), bf16)]),
        )

    def term_text():
        return (
            jnp.concatenate([grad_w, jnp.zeros((D, 2 * D), bf16), grad_cout_w, grad_up_w], axis=1),
            jnp.concatenate([jnp.zeros((CH, D), bf16), grad_down_w]),
        )

    block_term, project_term = lax.cond(is_stem, term_stem, term_text)
    block_grad = lax.psum_scatter(block_term, BOTH, scatter_dimension=0, tiled=True).astype(f32)
    project_grad = lax.psum_scatter(project_term, BOTH, scatter_dimension=0, tiled=True).astype(f32)

    gone = jnp.zeros((), f32)
    vector_term = jnp.concatenate(
        [
            jnp.where(is_stem, bn_sums.reshape(-1), gone),
            jnp.where(is_stem, patch_bias_sum.reshape(-1), gone),
            jnp.where(
                is_stem,
                gone,
                jnp.concatenate(
                    [
                        grads_outer.reshape(-1),
                        grads_three[:2].reshape(-1),
                        grad_up_bias.reshape(-1),
                        grads_three[2],
                    ]
                ),
            ),
        ]
    ).reshape(-1, CH)
    vector_total = doubled(vector_term, "dp", dp, lambda mine, other, step: mine + other)
    vector_total = vector_total + lax.ppermute(vector_total, "section", [(0, 1), (1, 0)])
    vector_grad = lax.dynamic_slice_in_dim(
        vector_total.reshape(-1), me * vector_master.shape[0], vector_master.shape[0]
    )

    got_hi = lax.ppermute(grad_hi, "section", [(0, 1)])
    own_pre = jnp.where(is_stem, grad_lo, got_hi).astype(f32)
    first_channel = section * half_channels

    def own_half(array):
        return lax.dynamic_slice_in_dim(array, first_channel, half_channels, axis=array.ndim - 1)

    own_normed = (own_half(features).astype(f32) - own_half(center)) * own_half(factor)
    own_gain = own_half(bn_gain)
    feature_grad = own_half(factor) * (
        own_pre * own_gain
        - own_gain * own_half(vector_total[1]) / every_patch
        - own_normed * (own_gain * own_half(vector_total[0]) / every_patch)
    )

    def table_packed():
        moved = lax.ppermute(rows_low, "section", [(1, 0)])
        sent = jnp.where(is_stem, moved, rows_high).reshape(dp, room, D)
        got = lax.all_to_all(sent, "dp", split_axis=0, concat_axis=0, tiled=True)
        hit = (jnp.arange(table_rows, dtype=i32)[:, None] == asked[None, :]).astype(bf16)
        return mm(hit, got.reshape(half_room, D))

    def table_gathered():
        rows = jnp.where(is_stem, lax.ppermute(grad_embed, "section", [(1, 0)]), grad_embed)
        rows = lax.all_gather(rows, "dp", axis=0, tiled=True).astype(f32)
        spot = lax.all_gather(token_ids, "dp", axis=0, tiled=True) - me * table_rows
        spot = jnp.where((spot >= 0) & (spot < table_rows), spot, table_rows)
        return jnp.zeros((table_rows, D), f32).at[spot].add(rows, mode="drop")

    table_grad = lax.cond(any_crowded, table_gathered, table_packed)

    root_tokens = math.sqrt(tokens * dp)
    table_new = sgd_update(table_grad, table_momentum, table_master, table_average, 0.05)
    block_new = sgd_update(
        block_grad, block_momentum, block_master, block_average, 0.5 * D ** (-0.5) / root_tokens
    )
    project_new = sgd_update(
        project_grad,
        project_momentum,
        project_master,
        project_average,
        0.5 * FF ** (-0.5) / root_tokens,
    )
    vector_new = sgd_update(
        vector_grad, vector_momentum, vector_master, vector_average, 0.1 / root_tokens
    )
    half_width = D // 2
    got_out = lax.ppermute(block_out[:, :half_width], "section", [(1, 0)])
    block_piece = jnp.where(is_stem, got_out, block_out[:, half_width:])
    return (block_piece, feature_grad, *table_new, *block_new, *project_new, *vector_new)


def solution(mesh):
    rows = P(BOTH, None)
    flat = P(BOTH)
    placed = (
        (P("dp", None), P(), P("dp"), P("dp", None), P("dp", None))
        + (rows,) * 9
        + (flat,) * 3
    )
    return jax.shard_map(
        per_device,
        mesh=mesh,
        in_specs=placed,
        out_specs=(P("dp", "section"), P("dp", "section")) + (rows,) * 15 + (flat,) * 5,
        check_vma=False,
    )
```

```python
import math

import jax
import jax.numpy as jnp
from jax import lax
from jax.experimental import pallas as pl
from jax.experimental.pallas import tpu as pltpu
from jax.sharding import PartitionSpec as P

D = 768
HEADS = 12
HEAD_DIM = 64
QUAD = 4 * HEAD_DIM
QUADS = HEADS // 4
FF = 3072
CH = 1024
PATCH = 196
WINDOW = 208
IMG_DEV = 16
GROUPS_DEV = 32
LONGEST = 32
HALF = D // 2
ROWS = 256
BLOCK = 128
SPAN = BLOCK + LONGEST
SCALE = HEAD_DIM ** (-0.5)
EPS = 1e-05
NEG = -1e30
BOTH = ("section", "dp")
VMEM_BYTES = 58 * 1024 * 1024
bf16 = jnp.bfloat16
f32 = jnp.float32
i32 = jnp.int32


def mm(left, right):
    return jnp.dot(left, right, preferred_element_type=f32)


def mm_rt(left, right):
    return lax.dot_general(left, right, (((1,), (1,)), ((), ())), preferred_element_type=f32)


def mm_lt(left, right):
    return lax.dot_general(left, right, (((0,), (0,)), ((), ())), preferred_element_type=f32)


def normalise(values):
    shifted = values - jnp.mean(values, axis=-1, keepdims=True)
    factor = lax.rsqrt(jnp.mean(shifted * shifted, axis=-1, keepdims=True) + EPS)
    return shifted * factor, factor


def norm_back(incoming, unit, factor, gain):
    scaled = incoming * gain
    mean_grad = jnp.mean(scaled, axis=-1, keepdims=True)
    mean_cross = jnp.mean(scaled * unit, axis=-1, keepdims=True)
    return factor * (scaled - mean_grad - unit * mean_cross)


GELU_C = math.sqrt(2.0 / math.pi)


def gelu_parts(values):
    square = values * values
    bend = jnp.tanh(GELU_C * values * (1.0 + 0.044715 * square))
    half = 0.5 * (1.0 + bend)
    slope = half + 0.5 * values * (1.0 - bend * bend) * (GELU_C * (1.0 + 3 * 0.044715 * square))
    return values * half, slope


def gelu_only(values):
    bend = jnp.tanh(GELU_C * values * (1.0 + 0.044715 * (values * values)))
    return 0.5 * values * (1.0 + bend)


def head_masks(dtype, width=QUAD):
    lanes = lax.broadcasted_iota(i32, (1, width), 1) // HEAD_DIM
    return [jnp.where(lanes == h, 1.0, 0.0).astype(dtype) for h in range(width // HEAD_DIM)]


def spread_heads(rows, masks):
    return jnp.concatenate([rows * m for m in masks], axis=0)


def join_heads(stacked, masks):
    count = stacked.shape[0] // len(masks)
    total = stacked[:count] * masks[0]
    for h in range(1, len(masks)):
        total = total + stacked[h * count : (h + 1) * count] * masks[h]
    return total


def softmax(scores, allowed):
    scores = jnp.where(allowed, scores * SCALE, NEG)
    weights = jnp.exp(scores - jnp.max(scores, axis=-1, keepdims=True))
    return weights * (1.0 / jnp.sum(weights, axis=-1, keepdims=True))


def one_hot_cols(index_col, width):
    places = lax.broadcasted_iota(i32, (index_col.shape[0], width), 1)
    return jnp.where(places == index_col, 1.0, 0.0).astype(bf16)


def one_hot_rows(index_row, height, offset=0):
    places = lax.broadcasted_iota(i32, (height, index_row.shape[1]), 0) + offset
    return jnp.where(places == index_row, 1.0, 0.0).astype(bf16)


def join_halves(target, low_ref, high_ref):
    count = low_ref.shape[0]
    target[:count, :] = low_ref[...]
    target[count : 2 * count, :] = high_ref[...]


def key_span(first):
    return pl.multiple_of(jnp.maximum(first - LONGEST, 0), LONGEST)


def self_allowed(start_rows, first, key_first):
    rows = lax.broadcasted_iota(i32, (BLOCK, SPAN), 0) + first
    keys = lax.broadcasted_iota(i32, (BLOCK, SPAN), 1) + key_first
    allowed = (keys <= rows) & (keys >= start_rows)
    return jnp.concatenate([jnp.where(allowed, 1, 0)] * 4, axis=0) > 0


def chunks_of(count, size, body):
    def step(index, carry):
        body(pl.multiple_of(index * size, size))
        return carry

    lax.fori_loop(0, count, step, 0)


def text_first(
    blocks, embed, start, pack, vecs,
    qkv_lo, qkv_hi, out_lo, out_hi, cq_lo, cq_hi,
    qkv_rows, mix_rows, resid_one, slots_a, slots_b,
    w_qkv, w_out, w_cq, queries,
):
    count = blocks[0]
    join_halves(w_qkv, qkv_lo, qkv_hi)
    join_halves(w_out, out_lo, out_hi)
    join_halves(w_cq, cq_lo, cq_hi)
    queries[...] = jnp.zeros_like(queries)
    masks = head_masks(bf16)
    masks_f = head_masks(f32)

    def project(first):
        rows = pl.ds(first, ROWS)
        unit, _ = normalise(embed[rows, :].astype(f32))
        normed = (unit * vecs[0:1, :] + vecs[1:2, :]).astype(bf16)
        for third in range(3):
            columns = slice(third * D, (third + 1) * D)
            qkv_rows[rows, columns] = mm(normed, w_qkv[:, columns]).astype(bf16)

    def attend(first):
        rows = pl.ds(first, BLOCK)
        key_first = key_span(first)
        span = pl.ds(key_first, SPAN)
        allowed = self_allowed(start[rows, :], first, key_first)
        for quad in range(QUADS):
            lanes, keys, values = quad_lanes(quad)
            query = spread_heads(qkv_rows[rows, lanes], masks)
            shares = softmax(mm_rt(query, qkv_rows[span, keys]), allowed)
            mixed = mm(shares.astype(bf16), qkv_rows[span, values])
            mix_rows[rows, lanes] = join_heads(mixed, masks_f).astype(bf16)

    def finish(first):
        rows = pl.ds(first, ROWS)
        resid = embed[rows, :].astype(f32) + mm(mix_rows[rows, :], w_out[...])
        resid_one[rows, :] = resid
        unit, _ = normalise(resid)
        normed = (unit * vecs[2:3, :] + vecs[3:4, :]).astype(bf16)
        queries[rows, :] = mm(normed, w_cq[...]).astype(bf16)

    chunks_of(count, ROWS, project)
    chunks_of(count * (ROWS // BLOCK), BLOCK, attend)
    chunks_of(count, ROWS, finish)
    packed = mm(one_hot_cols(pack[...], queries.shape[0]), queries[...]).astype(bf16)
    slots_a[...] = packed[:, :HALF]
    slots_b[...] = packed[:, HALF:]


def quad_lanes(quad):
    return [slice(part * D + quad * QUAD, part * D + (quad + 1) * QUAD) for part in range(3)]


def text_middle(
    blocks, mix_a, mix_b, take, pack, resid_one, cotangent, vecs, up_bias,
    cout_lo, cout_hi, up_lo, up_hi, down_part,
    block_out, grad_two, late_lo, late_hi, slots_a, slots_b,
    vec_grad, up_bias_grad,
    w_cout, w_up, mixed, normed, normed_t, factor_s, total, back, grad_down_t,
    up_sum, down_sum, up_buffer, down_buffer, w_down_t, sems,
):
    step = pl.program_id(0)
    last = pl.num_programs(0) - 1
    count = blocks[0]
    wide = w_up.shape[1]
    by_owner = down_buffer.shape[1] != D

    def copies(chunk):
        slot = chunk % 2
        place = (chunk + 1) % 4
        columns = slice(chunk * wide, (chunk + 1) * wide)
        pairs = [
            (up_buffer.at[slot, :HALF, :], late_lo.at[:, columns]),
            (up_buffer.at[slot, HALF:, :], late_hi.at[:, columns]),
        ]
        if by_owner:
            height = down_buffer.shape[1]
            rows = slice(place % 2 * height, (place % 2 + 1) * height)
            target = late_lo if place < 2 else late_hi
            pairs.append((down_buffer.at[slot], target.at[rows, CH + FF :]))
        else:
            columns = slice(CH + FF + place * wide, CH + FF + (place + 1) * wide)
            pairs.append((down_buffer.at[slot, :HALF, :], late_lo.at[:, columns]))
            pairs.append((down_buffer.at[slot, HALF:, :], late_hi.at[:, columns]))
        return [
            pltpu.make_async_copy(source, target, sems.at[slot, i])
            for i, (source, target) in enumerate(pairs)
        ]

    for chunk in (0, 1):

        @pl.when(step == chunk + 2)
        def _():
            for copy in copies(chunk):
                copy.wait()

    @pl.when(step == 0)
    def _():
        w_cout[:HALF, :] = cout_lo[:, :D]
        w_cout[HALF:, :] = cout_hi[:, :D]
        normed[...] = jnp.zeros_like(normed)
        block_out[...] = jnp.zeros_like(block_out)
        vec_grad[...] = jnp.zeros_like(vec_grad)

        def begin(first):
            rows = pl.ds(first, ROWS)
            places = lax.broadcasted_iota(i32, (ROWS, take.shape[1]), 0) + first
            hit = jnp.where(places == take[...], 1.0, 0.0).astype(bf16)
            mixed[rows, :HALF] = mm(hit, mix_a[...]).astype(bf16)
            mixed[rows, HALF:] = mm(hit, mix_b[...]).astype(bf16)
            resid_two = resid_one[rows, :] + mm(mixed[rows, :], w_cout[...])
            unit, factor = normalise(resid_two)
            grad_two[rows, :] = unit
            factor_s[rows, :] = factor
            low = (unit * vecs[0:1, :] + vecs[1:2, :]).astype(bf16)
            normed[rows, :] = low
            normed_t[:, rows] = low.T
            total[rows, :] = resid_two + vecs[2:3, :]
            back[rows, :] = jnp.zeros((ROWS, D), f32)
            grad_down_t[:, rows] = cotangent[rows, :].T

        chunks_of(count, ROWS, begin)

    @pl.when(step < last)
    def _():
        join_halves(w_up, up_lo, up_hi)
        parts = wide // 128
        if by_owner:
            height = down_buffer.shape[1] // parts
            for i in range(0, parts, 2):
                pair = down_part[i * height : (i + 2) * height, :].astype(f32)
                for h in range(2):
                    one = pair[h * height : (h + 1) * height]
                    one = jnp.concatenate([one[:, j : j + 128] for j in range(0, CH + FF, 128)], axis=0)
                    w_down_t[:, (i + h) * 128 : (i + h + 1) * 128] = one.astype(bf16)
        else:
            w_down_t[...] = down_part[...]
        up_sum[...] = jnp.zeros_like(up_sum)
        down_sum[...] = jnp.zeros_like(down_sum)
        up_bias_grad[...] = jnp.zeros_like(up_bias_grad)

        def forward_back(first):
            rows = pl.ds(first, ROWS)
            act, slope = gelu_parts(mm(normed[rows, :], w_up[...]) + up_bias[...])
            act = act.astype(bf16)
            total[rows, :] += mm_rt(act, w_down_t[...])
            grad_up = (mm(cotangent[rows, :], w_down_t[...]) * slope).astype(bf16)
            up_bias_grad[...] += jnp.sum(grad_up.astype(f32), axis=0, keepdims=True)
            up_sum[...] += mm(normed_t[:, rows], grad_up)
            down_sum[...] += mm(grad_down_t[:, rows], act)
            back[rows, :] += mm_rt(grad_up, w_up[...])

        chunks_of(count, ROWS, forward_back)
        slot = step % 2
        up_buffer[slot] = up_sum[...].astype(bf16)
        if by_owner:
            pieces = [
                jnp.concatenate(
                    [down_sum[j : j + height, first : first + 128] for j in range(0, D, height)],
                    axis=1,
                )
                for first in range(0, wide, 128)
            ]
            for i in range(0, parts, 2):
                pair = jnp.concatenate(pieces[i : i + 2], axis=0).astype(bf16)
                down_buffer[slot, i * height : (i + 2) * height, :] = pair
        else:
            down_buffer[slot] = down_sum[...].astype(bf16)

    for chunk in range(3):

        @pl.when(step == chunk)
        def _():
            for copy in copies(chunk):
                copy.start()

    @pl.when(step == last)
    def _():
        up_sum[:, :D] = jnp.zeros((D, D), f32)

        def end(first):
            rows = pl.ds(first, ROWS)
            block_out[rows, :] = total[rows, :].astype(bf16)
            incoming, unit = back[rows, :], grad_two[rows, :]
            vec_grad[0:1, :] += jnp.sum(incoming * unit, axis=0, keepdims=True)
            vec_grad[1:2, :] += jnp.sum(incoming, axis=0, keepdims=True)
            grad = norm_back(incoming, unit, factor_s[rows, :], vecs[0:1, :])
            grad = cotangent[rows, :].astype(f32) + grad
            grad_two[rows, :] = grad
            grad = grad.astype(bf16)
            up_sum[:, :D] += mm_lt(mixed[rows, :], grad)
            normed[rows, :] = mm_rt(grad, w_cout[...]).astype(bf16)

        chunks_of(count, ROWS, end)
        slot = step % 2
        up_buffer[slot, :, :D] = up_sum[:, :D].astype(bf16)
        up_buffer[slot, :, D:] = jnp.zeros((D, wide - D), bf16)
        down_buffer[slot] = jnp.zeros(down_buffer.shape[1:], bf16)
        for copy in copies(3):
            copy.start()
        packed = mm(one_hot_cols(pack[...], normed.shape[0]), normed[...]).astype(bf16)
        slots_a[...] = packed[:, :HALF]
        slots_b[...] = packed[:, HALF:]
        for chunk in (2, 3):
            for copy in copies(chunk):
                copy.wait()


def text_last(
    blocks, grad_a, grad_b, take, place, grad_two, resid_one, embed, qkv_rows, mix_rows, start, vecs,
    qkv_lo, qkv_hi, out_lo, out_hi, cq_lo, cq_hi,
    grad_embed, rows_a, rows_b, grad_lo, grad_hi, vec_grad,
    grad_mix, grad_queries, total, sums, grad_one,
):
    count = blocks[0]

    def keep(first, value):
        low = value.astype(bf16)
        width = value.shape[1]
        grad_lo[:, first : first + width] = low[:HALF]
        grad_hi[:, first : first + width] = low[HALF:]

    def turned_back(rows, lo, hi):
        return jnp.concatenate([mm_rt(rows, lo[...]), mm_rt(rows, hi[...])], axis=1)

    masks = head_masks(bf16)
    masks_f = head_masks(f32)
    vec_grad[...] = jnp.zeros_like(vec_grad)
    total[...] = jnp.zeros_like(total)
    sums[...] = jnp.zeros_like(sums)
    grad_embed[...] = jnp.zeros_like(grad_embed)

    def begin(first):
        rows = pl.ds(first, ROWS)
        places = lax.broadcasted_iota(i32, (ROWS, take.shape[1]), 0) + first
        hit = jnp.where(places == take[...], 1.0, 0.0).astype(bf16)
        grad_q = jnp.concatenate([mm(hit, grad_a[...]), mm(hit, grad_b[...])], axis=1).astype(bf16)
        unit, factor = normalise(resid_one[rows, :])
        normed = (unit * vecs[2:3, :] + vecs[3:4, :]).astype(bf16)
        sums[:, :D] += mm_lt(normed, grad_q)
        incoming = turned_back(grad_q, cq_lo, cq_hi)
        vec_grad[2:3, :] += jnp.sum(incoming * unit, axis=0, keepdims=True)
        vec_grad[3:4, :] += jnp.sum(incoming, axis=0, keepdims=True)
        grad = grad_two[rows, :] + norm_back(incoming, unit, factor, vecs[2:3, :])
        grad_one[rows, :] = grad
        grad = grad.astype(bf16)
        sums[:, D : 2 * D] += mm_lt(mix_rows[rows, :], grad)
        grad_mix[rows, :] = turned_back(grad, out_lo, out_hi).astype(bf16)

    def attend(first):
        rows = pl.ds(first, BLOCK)
        key_first = key_span(first)
        span = pl.ds(key_first, SPAN)
        allowed = self_allowed(start[rows, :], first, key_first)
        for quad in range(QUADS):
            lanes, keys, values = quad_lanes(quad)
            query = spread_heads(qkv_rows[rows, lanes], masks)
            grad = spread_heads(grad_mix[rows, lanes], masks)
            key_rows = qkv_rows[span, keys]
            shares = softmax(mm_rt(query, key_rows), allowed)
            grad_shares = mm_rt(grad, qkv_rows[span, values])
            inner = jnp.sum(grad_shares * shares, axis=-1, keepdims=True)
            grad_scores = (shares * (grad_shares - inner)).astype(bf16)
            back = join_heads(mm(grad_scores, key_rows), masks_f) * SCALE
            grad_queries[rows, lanes] = back.astype(bf16)
            later = slice(D + quad * QUAD, D + (quad + 1) * QUAD)
            total[span, lanes] += mm_lt(grad_scores, query) * SCALE
            total[span, later] += mm_lt(shares.astype(bf16), grad)

    def end(first):
        rows = pl.ds(first, ROWS)
        unit, factor = normalise(embed[rows, :].astype(f32))
        normed = (unit * vecs[0:1, :] + vecs[1:2, :]).astype(bf16)
        grad = jnp.concatenate([grad_queries[rows, :], total[rows, :].astype(bf16)], axis=1)
        for third in range(3):
            columns = slice(third * D, (third + 1) * D)
            sums[:, columns] += mm_lt(normed, grad[:, columns])
        incoming = turned_back(grad, qkv_lo, qkv_hi)
        vec_grad[0:1, :] += jnp.sum(incoming * unit, axis=0, keepdims=True)
        vec_grad[1:2, :] += jnp.sum(incoming, axis=0, keepdims=True)
        grad = grad_one[rows, :] + norm_back(incoming, unit, factor, vecs[0:1, :])
        grad_embed[rows, :] = grad.astype(bf16)

    chunks_of(count, ROWS, begin)
    keep(4 * D, sums[:, :D])
    keep(3 * D, sums[:, D : 2 * D])
    chunks_of(count * (ROWS // BLOCK), BLOCK, attend)
    sums[...] = jnp.zeros_like(sums)
    chunks_of(count, ROWS, end)
    keep(0, sums[...])
    half = rows_a.shape[0]
    rows_a[...] = mm(one_hot_rows(place[...], half), grad_embed[...]).astype(bf16)
    rows_b[...] = mm(one_hot_rows(place[...], half, half), grad_embed[...]).astype(bf16)


def unpack_rows(rows_a, rows_b, place, embed):
    count = rows_a.shape[0]
    total = mm(one_hot_cols(place[...], count), rows_a[...])
    total = total + mm(one_hot_cols(place[...] - count, count), rows_b[...])
    embed[...] = total.astype(bf16)


def pack_half(index, rows, packed):
    packed[...] = mm(one_hot_cols(index[...], rows.shape[0]), rows[...].astype(bf16)).astype(bf16)


def join_cotangent(arrival, own, slots_a, slots_b, rows, joined):
    height = joined.shape[0]
    low = mm(one_hot_rows(own[...], height), rows[...].astype(bf16))
    hit = one_hot_rows(arrival[...], height)
    joined[:, :HALF] = (low[:, :HALF] + mm(hit, slots_a[...])).astype(bf16)
    joined[:, HALF:] = (low[:, HALF:] + mm(hit, slots_b[...])).astype(bf16)


def join_output(slot_rows, own, slots, rows, joined):
    height = joined.shape[0]
    total = mm(one_hot_rows(slot_rows[...], height), slots[...])
    total = total + mm(one_hot_cols(own[...], rows.shape[0]), rows[...])
    joined[...] = total.astype(bf16)


def join_kv(w_kv, k_lo, k_hi, v_lo, v_hi):
    for first, (lo, hi) in enumerate(((k_lo, k_hi), (v_lo, v_hi))):
        for part in range(2):
            columns = slice((2 * part + first) * HALF, (2 * part + first + 1) * HALF)
            w_kv[:HALF, columns] = lo[:, part * HALF : (part + 1) * HALF]
            w_kv[HALF:, columns] = hi[:, part * HALF : (part + 1) * HALF]


def stem_forward(
    features, bn, w_patch, patch_bias, k_lo, k_hi, v_lo, v_hi, patches, kv_lo, kv_hi, w_kv
):
    @pl.when(pl.program_id(0) == 0)
    def _():
        join_kv(w_kv, k_lo, k_hi, v_lo, v_hi)

    normed = (features[...].astype(f32) - bn[0:1, :]) * bn[1:2, :]
    hidden = gelu_only(normed * bn[2:3, :] + bn[3:4, :]).astype(bf16)
    rows = (mm(hidden, w_patch[...]) + patch_bias[...]).astype(bf16)
    patches[...] = rows
    kv_lo[...] = mm(rows, w_kv[:, :D]).astype(bf16)
    kv_hi[...] = mm(rows, w_kv[:, D:]).astype(bf16)


def image_window(image):
    first = image * PATCH
    aligned = pl.multiple_of(first // 16 * 16, 16)
    lanes = lax.broadcasted_iota(i32, (1, WINDOW), 1) + (aligned - first)
    return aligned, (lanes >= 0) & (lanes < PATCH)


def cross_forward(queries, kv, mixed):
    masks = head_masks(bf16, HALF)
    masks_f = head_masks(f32, HALF)

    def image(index, carry):
        aligned, allowed = image_window(index)
        window = pl.ds(aligned, WINDOW)
        place = pl.ds(pl.multiple_of(index * LONGEST, LONGEST), LONGEST)
        scores = mm_rt(spread_heads(queries[place, :], masks), kv[window, :HALF])
        shares = softmax(scores, allowed).astype(bf16)
        mixed[place, :] = join_heads(mm(shares, kv[window, HALF:]), masks_f).astype(bf16)
        return carry

    lax.fori_loop(0, IMG_DEV, image, 0, unroll=4)


def cross_backward(queries, grads, kv, grad_q, grad_kv):
    grad_kv[...] = jnp.zeros_like(grad_kv)
    masks = head_masks(bf16, HALF)
    masks_f = head_masks(f32, HALF)

    def image(index, carry):
        aligned, allowed = image_window(index)
        window = pl.ds(aligned, WINDOW)
        place = pl.ds(pl.multiple_of(index * LONGEST, LONGEST), LONGEST)
        query = spread_heads(queries[place, :], masks)
        grad = spread_heads(grads[place, :], masks)
        keys = kv[window, :HALF]
        shares = softmax(mm_rt(query, keys), allowed)
        grad_shares = mm_rt(grad, kv[window, HALF:])
        inner = jnp.sum(grad_shares * shares, axis=-1, keepdims=True)
        grad_scores = (shares * (grad_shares - inner)).astype(bf16)
        grad_q[place, :] = (join_heads(mm(grad_scores, keys), masks_f) * SCALE).astype(bf16)
        grad_kv[window, :HALF] += (mm_lt(grad_scores, query) * SCALE).astype(bf16)
        grad_kv[window, HALF:] += mm_lt(shares.astype(bf16), grad).astype(bf16)
        return carry

    lax.fori_loop(0, IMG_DEV, image, 0, unroll=4)


def stem_backward_kv(
    k_lo, k_hi, v_lo, v_hi, patches, grad_kv_lo, grad_kv_hi,
    grad_rows, grad_lo, grad_hi, bias_sum,
    w_kv, total,
):
    step = pl.program_id(0)

    @pl.when(step == 0)
    def _():
        join_kv(w_kv, k_lo, k_hi, v_lo, v_hi)
        total[...] = jnp.zeros_like(total)
        bias_sum[...] = jnp.zeros_like(bias_sum)

    rows = mm_rt(grad_kv_lo[...], w_kv[:, :D]) + mm_rt(grad_kv_hi[...], w_kv[:, D:])
    rows = rows.astype(bf16)
    grad_rows[...] = rows
    bias_sum[...] += jnp.sum(rows.astype(f32), axis=0, keepdims=True)
    turned = patches[...].T
    total[:, :D] += mm(turned, grad_kv_lo[...])
    total[:, D:] += mm(turned, grad_kv_hi[...])

    @pl.when(step == pl.num_programs(0) - 1)
    def _():
        for first in range(2):
            for part in range(2):
                source = slice((2 * part + first) * HALF, (2 * part + first + 1) * HALF)
                target = slice((2 * first + part) * HALF, (2 * first + part + 1) * HALF)
                grad_lo[:, target] = total[:HALF, source].astype(bf16)
                grad_hi[:, target] = total[HALF:, source].astype(bf16)


def stem_backward(
    features, bn, w_patch, grad_rows, grad_lo, grad_hi, grad_patch_w, sums, patch_acc
):
    step = pl.program_id(0)

    @pl.when(step == 0)
    def _():
        patch_acc[...] = jnp.zeros_like(patch_acc)
        sums[...] = jnp.zeros_like(sums)

    normed = (features[...].astype(f32) - bn[0:1, :]) * bn[1:2, :]
    hidden, slope = gelu_parts(normed * bn[2:3, :] + bn[3:4, :])
    patch_acc[...] += mm_lt(hidden.astype(bf16), grad_rows[...])
    grad_pre = mm_rt(grad_rows[...], w_patch[...]) * slope
    sums[0:1, :] += jnp.sum(grad_pre * normed, axis=0, keepdims=True)
    sums[1:2, :] += jnp.sum(grad_pre, axis=0, keepdims=True)
    grad_low = grad_pre.astype(bf16)
    grad_lo[...] = grad_low[:, : CH // 2]
    grad_hi[...] = grad_low[:, CH // 2 :]

    @pl.when(step == pl.num_programs(0) - 1)
    def _():
        grad_patch_w[...] = patch_acc[...].astype(bf16)


def place_pieces(where_, two, four, two_other, four_other, out, sems):
    dp_index, section = where_[0], where_[1]
    copies = []
    for core, sources in ((1 - section, (two_other, four_other)), (section, (two, four))):
        for z in range(4):
            for far, turn, bits in ((0, 0, 0), (0, 1, 1 + core), (1, 0, 2 - core), (1, 1, 3)):
                target = dp_index ^ (4 * z) ^ bits
                copies.append((sources[far].at[turn, z], out.at[core, target]))
    started = [
        pltpu.make_async_copy(source, target, sems.at[i])
        for i, (source, target) in enumerate(copies)
    ]
    for copy in started:
        copy.start()
    for copy in started:
        copy.wait()


def shape(dims, dtype):
    return jax.ShapeDtypeStruct(dims, dtype)


def whole(array):
    zeros = (0,) * len(array.shape)
    return pl.BlockSpec(array.shape, lambda *_: zeros, pipeline_mode=pl.Buffered(1))


def at(dims, *index):
    return pl.BlockSpec(dims, lambda *_: index)


def call(kernel, steps, in_specs, out_specs, outs, scratch, flops):
    return pl.pallas_call(
        kernel,
        grid=(steps,),
        in_specs=in_specs,
        out_specs=out_specs,
        out_shape=outs,
        scratch_shapes=scratch,
        compiler_params=pltpu.CompilerParams(vmem_limit_bytes=VMEM_BYTES),
        cost_estimate=pl.CostEstimate(flops=flops, bytes_accessed=0, transcendentals=0),
    )


def simple(kernel, inputs, outs, scratch, flops):
    return call(
        kernel,
        1,
        [whole(a) for a in inputs],
        [at(o.shape, *(0,) * len(o.shape)) for o in outs],
        outs,
        scratch,
        flops,
    )(*inputs)


def blank(outs):
    return pl.pallas_call(
        lambda *refs: None,
        out_shape=outs,
        out_specs=[pl.BlockSpec(memory_space=pl.ANY) for _ in outs],
    )()


barrier = lax.optimization_barrier


class Lines:
    def __init__(self, dp, dp_index, section):
        self.dp, self.dp_index, self.section = dp, dp_index, section
        self.is_stem = section == 0
        self.by_hand = dp == 16
        self.x, self.y, self.z = dp_index & 1, dp_index // 2 & 1, dp_index // 4

    def across(self, array, low, high):
        count = self.dp
        pairs = [(d, d ^ low) for d in range(count)]
        pairs += [(count + d, count + (d ^ high)) for d in range(count)]
        return lax.ppermute(array, BOTH, pairs)

    def swap(self, array):
        return lax.ppermute(array, "section", [(0, 1), (1, 0)])

    def gather_line(self, shard):
        return jnp.stack([shard] + [self.across(shard, 4 * k, 4 * k) for k in (1, 2, 3)])

    def gather_first(self, line):
        return jnp.stack([line, self.across(line, 1, 2)])

    def gather_second(self, two):
        return two, self.across(two, 2, 1)

    def gather_place(self, two, four):
        inputs = [two, four, self.swap(two), self.swap(four)]
        any_spec = pl.BlockSpec(memory_space=pl.ANY)
        rows, width = two.shape[2:]
        count = 2 * self.dp
        placed = pl.pallas_call(
            place_pieces,
            in_specs=[pl.BlockSpec(memory_space=pltpu.SMEM)] + [any_spec] * 4,
            out_specs=pl.BlockSpec(memory_space=pltpu.VMEM),
            out_shape=shape((2, self.dp, rows, width), bf16),
            scratch_shapes=[pltpu.SemaphoreType.DMA((count,))],
            compiler_params=pltpu.CompilerParams(vmem_limit_bytes=VMEM_BYTES),
        )(jnp.stack([self.dp_index, self.section]), *inputs)
        return placed.reshape(count * rows, width)

    def share_patch(self, project_low):
        count = self.dp // 2
        half = project_low.shape[0] // 2
        moved = lax.ppermute(project_low[half:], BOTH, [(d, d + count) for d in range(count)])
        mine = jnp.where(self.z < 2, project_low[:half], moved)
        moved = lax.ppermute(mine[half // 2 :], "section", [(0, 1)])
        return jnp.where(self.is_stem, mine[: half // 2], moved)

    def fold_patch(self, part, rows):
        rest = part.shape[0] - rows
        width = D * rest // rows
        tail = [part[rows:, first : first + width] for first in range(0, D, width)]
        return jnp.concatenate([part[:rows], jnp.concatenate(tail)], axis=1)

    def unfold_patch(self, parts):
        count, rows, width = parts.shape
        rest = rows * (width - D) // D
        tail = [parts[:, first : first + rest, D:] for first in range(0, rows, rest)]
        parts = jnp.concatenate([parts[:, :, :D], jnp.concatenate(tail, axis=2)], axis=1)
        parts = parts.reshape(2, 2, self.dp // 2, rows + rest, D)
        return parts.transpose(2, 1, 0, 3, 4).reshape(-1, D)

    def pick(self, places, axis, place):
        return lax.dynamic_index_in_dim(places, place, axis, keepdims=False)

    def first_half(self, terms, flip):
        along_y = [self.pick(stem, 1, self.y ^ flip) for stem, _ in terms]
        along_x = [self.pick(text, 2, self.x ^ flip) for _, text in terms]
        parts = [jnp.where(self.is_stem, *both) for both in zip(along_y, along_x)]
        return jnp.concatenate(parts, axis=-1)

    def second_half(self, terms, got, flip):
        place = jnp.where(self.is_stem, self.x, self.y) ^ flip
        kept = self.pick(self.first_half(terms, 0), 1, place).astype(f32)
        return (kept + self.pick(got, 1, place).astype(f32)).astype(bf16)

    def sum_first(self, terms):
        return self.across(self.first_half(terms, 1), 2, 1)

    def sum_second(self, terms, got):
        return self.across(self.second_half(terms, got, 1), 1, 2)

    def line_of(self, terms, got, got_two):
        kept = self.second_half(terms, got, 0).astype(f32)
        return (kept + got_two.astype(f32)).astype(bf16)

    def sum_line(self, line):
        parts = [self.pick(line, 0, self.z ^ k) for k in (1, 2, 3)]
        return [self.across(p, 4 * k, 4 * k) for k, p in zip((1, 2, 3), parts)]

    def line_total(self, line, parts):
        return self.pick(line, 0, self.z).astype(f32) + sum(part.astype(f32) for part in parts)

    def sum_low_first(self, line):
        return self.across(line, 8, 8)

    def sum_low_last(self, line, got):
        line = (line.astype(f32) + got.astype(f32)).astype(bf16)
        low = self.z & 1
        got = self.across(self.pick(line, 0, 1 - low), 4, 4)
        return self.pick(line, 0, low).astype(f32) + got.astype(f32)

    def scatter_plain(self, w_lo, w_hi, kv_lo, kv_hi, patch):
        def total(term):
            return lax.psum_scatter(term, BOTH, scatter_dimension=0, tiled=True).astype(f32)

        own_w = jnp.concatenate([w_lo, w_hi])
        own_kv = jnp.concatenate([kv_lo, kv_hi])
        own_patch = jnp.concatenate([patch, jnp.zeros((FF, D), bf16)])
        return (
            total(
                jnp.concatenate(
                    [
                        jnp.where(self.is_stem, jnp.zeros_like(own_w), own_w),
                        jnp.where(self.is_stem, own_kv, jnp.zeros_like(own_kv)),
                    ],
                    axis=1,
                )
            ),
            total(jnp.where(self.is_stem, own_patch, jnp.zeros_like(own_patch))),
        )


def sgd_update(gradient, momentum, master, average, step_rate):
    new_momentum = 0.9 * momentum + gradient
    new_master = master - step_rate * (gradient + 0.9 * new_momentum)
    new_average = 0.8 * average + 0.2 * new_master
    return (gradient, new_momentum, new_average, new_master, new_master.astype(bf16))


def per_device(
    features,
    image_group,
    token_ids,
    text_lengths,
    cotangent,
    table_master,
    table_momentum,
    table_average,
    block_master,
    block_momentum,
    block_average,
    project_master,
    project_momentum,
    project_average,
    vector_master,
    vector_momentum,
    vector_average,
):
    dp = lax.axis_size("dp")
    group = lax.axis_size(BOTH)
    dp_index = lax.axis_index("dp")
    section = lax.axis_index("section")
    is_stem = section == 0
    me = section * dp + dp_index
    tokens = token_ids.shape[0]
    image_rows = features.shape[0]
    every_patch = image_rows * dp
    table_rows = table_master.shape[0]
    images = image_group.shape[0]

    lines = Lines(dp, dp_index, section)
    block_low = block_master.astype(bf16)
    project_low = project_master.astype(bf16)
    early = block_low[:, : 7 * D]
    late_low = jnp.concatenate(
        [
            block_low[:, 8 * D :],
            block_low[:, 7 * D : 8 * D],
            jnp.zeros((block_low.shape[0], CH - D), bf16),
        ],
        axis=1,
    )
    project_rows = project_master.shape[0]
    if lines.by_hand:
        patch_part = lines.share_patch(project_low)
        rows = late_low.shape[0]
        down_low = project_low.T.reshape(-1, rows, 128).transpose(1, 0, 2).reshape(rows, CH + FF)
        late_low = jnp.concatenate([down_low, late_low], axis=1)

    def send(block):
        return lax.all_to_all(block, "dp", split_axis=0, concat_axis=0, tiled=True)

    capacity = (2 * IMG_DEV + dp - 1) // dp
    slots = dp * capacity
    destination = image_group // GROUPS_DEV
    by_source = destination.reshape(dp, IMG_DEV)
    order = jnp.arange(IMG_DEV, dtype=i32)
    earlier = order[None, :] < order[:, None]
    rank_all = jnp.sum(
        ((by_source[:, :, None] == by_source[:, None, :]) & earlier[None]).astype(i32), axis=2
    ).reshape(images)
    my_dest = lax.dynamic_slice_in_dim(destination, dp_index * IMG_DEV, IMG_DEV)
    my_rank = lax.dynamic_slice_in_dim(rank_all, dp_index * IMG_DEV, IMG_DEV)
    stem_slot = my_dest * capacity + my_rank
    slot_of_image = jnp.where(
        destination == dp_index,
        jnp.arange(images, dtype=i32) // IMG_DEV * capacity + rank_all,
        -1,
    )
    lengths = text_lengths[0]
    group_ends = jnp.cumsum(lengths)
    group_starts = group_ends - lengths
    places = jnp.arange(tokens, dtype=i32)
    groups = jnp.arange(GROUPS_DEV, dtype=i32)
    named = jnp.any(image_group[None, :] == (dp_index * GROUPS_DEV + groups)[:, None], axis=1)
    within_group = (group_starts[None, :] <= places[:, None]) & (
        places[:, None] < group_ends[None, :]
    )
    token_start = jnp.sum(jnp.where(within_group, group_starts[None, :], 0), axis=1)
    token_named = jnp.any(within_group & named[None, :], axis=1)
    match = slot_of_image[None, :] == jnp.arange(slots, dtype=i32)[:, None]
    slot_group = jnp.max(jnp.where(match, (image_group % GROUPS_DEV)[None, :], -1), axis=1)
    group_hit = slot_group[:, None] == groups[None, :]
    slot_start = jnp.sum(jnp.where(group_hit, group_starts[None, :], 0), axis=1)
    slot_length = jnp.sum(jnp.where(group_hit, lengths[None, :], 0), axis=1)
    within = jnp.arange(LONGEST, dtype=i32)
    slot_rows = jnp.where(
        within[None, :] < slot_length[:, None], slot_start[:, None] + within[None, :], -1
    ).reshape(slots * LONGEST)
    slot_ids = jnp.max(
        jnp.where(slot_rows[:, None] == places[None, :], token_ids[None, :], -1), axis=1
    )

    if lines.by_hand:
        patch_part, slot_ids = barrier((patch_part, slot_ids))
        patch_part = lines.gather_line(lines.fold_patch(patch_part, early.shape[0]))
        early = jnp.concatenate([lines.gather_line(early), patch_part], axis=2)
    got_ids = send(slot_ids.reshape(dp, capacity * LONGEST)).reshape(slots, LONGEST)
    slot_hit = stem_slot[:, None] == jnp.arange(slots, dtype=i32)[None, :]
    image_ids = jnp.max(jnp.where(slot_hit[:, :, None], got_ids[None], -1), axis=1)
    ids = jnp.concatenate([image_ids.reshape(-1), jnp.where(token_named, -1, token_ids)])
    height = ids.shape[0]
    here = ids >= 0
    candidates = jnp.arange(height, dtype=i32)
    before = candidates[None, :] < candidates[:, None]
    row = jnp.sum((before & here[None, :]).astype(i32), axis=1)
    row = jnp.where(here, row, -1)
    row_count = jnp.sum(here.astype(i32))
    row_blocks = ((row_count + ROWS - 1) // ROWS).reshape(1)
    depth = jnp.concatenate(
        [jnp.tile(within, IMG_DEV), places - token_start]
    )
    image_row, own_row = row[: IMG_DEV * LONGEST], row[IMG_DEV * LONGEST :]
    arrival_row = jnp.max(
        jnp.where(slot_hit[:, :, None], image_row.reshape(IMG_DEV, 1, LONGEST), -1), axis=0
    ).reshape(slots * LONGEST)
    chosen = row[None, :] == candidates[:, None]
    start = jnp.max(jnp.where(chosen, (row - depth)[None, :], -1), axis=1)
    start = jnp.where(candidates < row_count, start, candidates)[:, None]

    room = max(16, (2 * tokens + 2 * tokens // 4) // group)
    half_room = dp * room
    owner = ids // table_rows
    same = (ids[:, None] == ids[None, :]) & here[None, :]
    is_first = here & ~jnp.any(same & before, axis=1)
    rank = jnp.sum(
        ((owner[:, None] == owner[None, :]) & before & is_first[None, :]).astype(i32), axis=1
    )
    rounds_here = jnp.max(jnp.where(is_first, rank, 0)) // room + 1
    table_low = table_master.astype(bf16)

    def round_of(turn):
        turn_rank = rank - turn * room
        first_place = jnp.where(
            is_first & (turn_rank >= 0) & (turn_rank < room), owner * room + turn_rank, -1
        )
        place = jnp.max(jnp.where(same, first_place[None, :], -1), axis=1)
        place = jnp.max(jnp.where(chosen, place[None, :], -1), axis=1)
        slot = jnp.arange(half_room, dtype=i32) + section * half_room
        asked = jnp.max(
            jnp.where(first_place[None, :] == slot[:, None], (ids % table_rows)[None, :], -1),
            axis=1,
        )
        return place, asked.reshape(dp, room)

    def serve(asked):
        hit = (asked[:, None] == jnp.arange(table_rows, dtype=i32)[None, :]).astype(bf16)
        served = mm(hit, table_low).astype(bf16)
        return send(served.reshape(dp, room, D)).reshape(half_room, D)

    def unpacked(place, served, served_low):
        return simple(
            unpack_rows,
            [served_low, served, place[:, None]],
            [shape((height, D), bf16)],
            [],
            4 * 10**9,
        )[0]

    rows_f = features.astype(f32)
    local_center = jnp.mean(rows_f, axis=0)
    local_square = jnp.sum(jnp.square(rows_f - local_center), axis=0)
    vector_own = lax.dynamic_update_slice(
        jnp.zeros((vector_master.shape[0] * group,), f32),
        lax.reduce_precision(vector_master, 8, 7),
        (me * vector_master.shape[0],),
    ).reshape(-1, CH)
    state = jnp.concatenate([local_center[None], local_square[None], vector_own])

    def merge(mine, other, step):
        delta = other[0] - mine[0]
        squares = mine[1] + other[1] + delta * delta * (0.5 * image_rows * step)
        return jnp.concatenate(
            [(0.5 * (mine[0] + other[0]))[None], squares[None], mine[2:] + other[2:]]
        )

    def merged(state, first, last, merge):
        step = first
        while step < last:
            other = lax.ppermute(state, "dp", [(i, i ^ step) for i in range(dp)])
            state = merge(state, other, step)
            step *= 2
        return state

    def merge_all(mine, other, step):
        return jnp.concatenate(
            [merge(mine[:-1], other[:-1], step), jnp.maximum(mine[-1:], other[-1:])]
        )

    state = merged(state, 1, 4, merge)
    if lines.by_hand:
        got_ids, state, early = barrier((got_ids, state, early))
        early = lines.gather_first(early)
    place, asked = round_of(0)
    rounds_row = jnp.broadcast_to(rounds_here.astype(f32), (1, CH))
    asked = send(asked).reshape(half_room)
    state = merged(jnp.concatenate([state, rounds_row]), 4, dp, merge_all)
    if lines.by_hand:
        asked, state, early = barrier((asked, state, early))
        early = lines.gather_second(early)
    served = serve(asked)
    served_low = lax.ppermute(served, "section", [(0, 1)])
    rounds_row = merged(state[-1:, :128], 1, 4, lambda mine, other, step: jnp.maximum(mine, other))
    vectors = state[2:-1]
    vector_full = vectors + lax.ppermute(vectors, "section", [(0, 1), (1, 0)])
    arrival_shape = shape((slots * LONGEST, HALF), bf16)
    cot_sent = simple(
        pack_half,
        [slot_rows[:, None], lax.dynamic_slice_in_dim(cotangent, section * HALF, HALF, axis=1)],
        [arrival_shape],
        [],
        3 * 10**9,
    )[0]
    if lines.by_hand:
        served, served_low, state, vector_full, early, rounds_row, cot_sent, late_low = barrier(
            (served, served_low, state, vector_full, early, rounds_row, cot_sent, late_low)
        )
        w_late = w_down = lax.all_gather(late_low, BOTH, axis=0, tiled=True)
    else:
        w_late = lax.all_gather(late_low, BOTH, axis=0, tiled=True)
        project_full = lax.all_gather(project_low, BOTH, axis=0, tiled=True)
        w_down = project_full.T
    center = state[0]
    factor = lax.rsqrt(state[1] / every_patch + EPS)
    rounds = rounds_row[0, 0].astype(i32)
    bn_gain, bn_bias = vector_full[0], vector_full[1]
    flat = vector_full.reshape(-1)
    offset = 2 * CH + D
    patch_bias = flat[2 * CH : offset].reshape(1, D)
    ln_vecs = flat[offset : offset + 6 * D].reshape(6, D)
    up_bias = flat[offset + 6 * D : offset + 6 * D + FF].reshape(1, FF)
    down_bias = flat[offset + 6 * D + FF :].reshape(1, D)
    vecs_outer = ln_vecs[:4]
    vecs_three = jnp.concatenate([ln_vecs[4:], down_bias])
    bn = jnp.stack([center, factor, bn_gain, bn_bias])

    def embed_more(turn, embed):
        place, asked = round_of(turn)
        served = serve(send(asked).reshape(half_room))
        return embed + unpacked(place, served, lax.ppermute(served, "section", [(0, 1)]))

    cot_b = send(cot_sent.reshape(dp, capacity * LONGEST, HALF)).reshape(slots * LONGEST, HALF)
    embed = lax.fori_loop(1, rounds, embed_more, unpacked(place, served, served_low))

    if lines.by_hand:
        w_early = lines.gather_place(*early)
        w_patch = w_early[:, 7 * D :].reshape(2 * dp, -1, w_early.shape[1] - 7 * D)
        w_patch = lines.unfold_patch(w_patch)
        w_early, w_patch, embed, cot_b = barrier((w_early, w_patch, embed, cot_b))
    else:
        w_early, w_patch = lax.all_gather(early, BOTH, axis=0, tiled=True), project_full

    def halves(width, column):
        return [at((HALF, width), 0, column), at((HALF, width), 1, column)]

    qkv_specs = halves(3 * D, 0) + halves(D, 3) + halves(D, 4)
    qkv_inputs = [w_early] * 6
    kv_specs = halves(D, 5) + halves(D, 6)
    kv_inputs = [w_early] * 4
    patch_spec = at((CH, D), 0, 0)
    blocks = 7
    per_block = image_rows // blocks
    qkv_scratch = [
        pltpu.VMEM((D, 3 * D), bf16),
        pltpu.VMEM((D, D), bf16),
        pltpu.VMEM((D, D), bf16),
        pltpu.VMEM((height, D), bf16),
    ]

    def rows_spec(width):
        return pl.BlockSpec((per_block, width), lambda step: (step, 0))

    slot_shape = shape((IMG_DEV * LONGEST, HALF), bf16)
    blocks_spec = pl.BlockSpec(memory_space=pltpu.SMEM)
    pack, take = image_row[:, None], image_row[None, :]
    rows_shape = shape((image_rows, D), bf16)

    text_saved = [
        shape((height, 3 * D), bf16),
        shape((height, D), bf16),
        shape((height, D), f32),
        slot_shape,
        slot_shape,
    ]
    stem_saved = [rows_shape] * 3

    def first_text():
        inputs = [embed, start, pack, vecs_outer]
        done = call(
            text_first,
            1,
            [blocks_spec] + [whole(a) for a in inputs] + qkv_specs,
            [whole(o) for o in text_saved],
            text_saved,
            qkv_scratch,
            15 * 10**9,
        )(row_blocks, *inputs, *qkv_inputs)
        return (*done, *blank(stem_saved))

    def first_stem():
        done = call(
            stem_forward,
            blocks,
            [rows_spec(CH), whole(bn), patch_spec, whole(patch_bias)] + kv_specs,
            [rows_spec(D)] * 3,
            stem_saved,
            [pltpu.VMEM((D, 2 * D), bf16)],
            23 * 10**9,
        )(features, bn, w_patch, patch_bias, *kv_inputs)
        return (*blank(text_saved), *done)

    qkv_rows, mix_rows, resid_one, q_a, q_b, patches, kv_lo, kv_hi = lax.cond(
        is_stem, first_stem, first_text
    )

    kv_moved = lax.ppermute(kv_hi, "section", [(0, 1)])

    def to_cores(block_a, block_b):
        return jnp.where(is_stem, lax.ppermute(block_a, "section", [(1, 0)]), block_b)

    q_here = to_cores(q_a, q_b)
    def cross(kv):
        return call(
            cross_forward,
            1,
            [whole(q_here), whole(kv)],
            [whole(q_here)],
            [slot_shape],
            [],
            8 * 10**9,
        )(q_here, kv)[0]

    mix_b = lax.cond(is_stem, lambda: cross(kv_lo), lambda: cross(kv_moved))

    mix_a = lax.ppermute(mix_b, "section", [(0, 1)])
    cot_a = lax.ppermute(cot_b, "section", [(0, 1)])
    grad_out = simple(
        join_cotangent,
        [arrival_row[None, :], own_row[None, :], cot_a, cot_b, cotangent],
        [shape((height, D), bf16)],
        [],
        4 * 10**9,
    )[0]

    chunks = 3
    wide = FF // chunks
    middle_shapes = [
        shape((height, D), bf16),
        shape((height, D), f32),
        shape((HALF, 2 * (CH + FF)), bf16),
        shape((HALF, 2 * (CH + FF)), bf16),
        slot_shape,
        slot_shape,
        shape((2, D), f32),
        shape((1, FF), f32),
    ]

    def middle_text():
        inputs = [mix_a, mix_b, take, pack, resid_one, grad_out, vecs_three]

        def chunk(step):
            return jnp.minimum(step, chunks - 1)

        if lines.by_hand:
            first_up = (CH + FF) // wide
            down_rows = D // (chunks + 1)
            down_spec = pl.BlockSpec((down_rows, CH + FF), lambda step: (1 + chunk(step), 0))
        else:
            first_up = 0
            down_rows = D
            down_spec = pl.BlockSpec((D, wide), lambda step: (0, 1 + chunk(step)))
        down_width = wide * D // down_rows
        outs = [whole(o) for o in middle_shapes]
        outs[2] = outs[3] = pl.BlockSpec(memory_space=pl.ANY)
        outs[7] = pl.BlockSpec((1, wide), lambda step: (0, chunk(step)))
        return call(
            text_middle,
            chunks + 1,
            [blocks_spec]
            + [whole(a) for a in inputs]
            + [pl.BlockSpec((1, wide), lambda step: (0, chunk(step)))]
            + halves(wide, first_up + chunks)
            + [
                pl.BlockSpec((HALF, wide), lambda step: (0, first_up + chunk(step))),
                pl.BlockSpec((HALF, wide), lambda step: (1, first_up + chunk(step))),
                down_spec,
            ],
            outs,
            middle_shapes,
            [
                pltpu.VMEM((D, D), bf16),
                pltpu.VMEM((D, wide), bf16),
                pltpu.VMEM((height, D), bf16),
                pltpu.VMEM((height, D), bf16),
                pltpu.VMEM((D, height), bf16),
                pltpu.VMEM((height, 1), f32),
                pltpu.VMEM((height, D), f32),
                pltpu.VMEM((height, D), f32),
                pltpu.VMEM((D, height), bf16),
                pltpu.VMEM((D, wide), f32),
                pltpu.VMEM((D, wide), f32),
                pltpu.VMEM((2, D, wide), bf16),
                pltpu.VMEM((2, down_rows, down_width), bf16),
                pltpu.VMEM((D, wide), bf16),
                pltpu.SemaphoreType.DMA((2, 4)),
            ],
            29 * 10**9,
        )(row_blocks, *inputs, up_bias, *[w_late] * 4, w_down)

    (
        block_out, grad_two, late_w_lo, late_w_hi, g_a, g_b, grads_three, grad_up_bias,
    ) = lax.cond(is_stem, lambda: tuple(blank(middle_shapes)), middle_text)
    g_here = to_cores(g_a, g_b)
    g_here, late_w_lo = barrier((g_here, late_w_lo))
    if lines.by_hand:
        late_sum = (lax.ppermute(late_w_lo, "section", [(1, 0)]), late_w_hi)
        late_sum = tuple(w.reshape(4, 2, 2, HALF // dp, w.shape[1]) for w in late_sum)
    else:
        late_term = jnp.concatenate([late_w_lo, late_w_hi])
        late_term = jnp.where(is_stem, jnp.zeros_like(late_term), late_term)
        late_grad = lax.psum_scatter(
            late_term[:, : CH + FF], BOTH, scatter_dimension=0, tiled=True
        )
        down_turned = lax.psum_scatter(
            late_term[:, CH + FF :], BOTH, scatter_dimension=1, tiled=True
        )
    out_here = to_cores(block_out[:, :HALF], block_out[:, HALF:])
    sent = simple(pack_half, [arrival_row[:, None], out_here], [arrival_shape], [], 3 * 10**9)[0]
    g_here, sent = barrier((g_here, sent))
    got_out = send(sent.reshape(dp, capacity * LONGEST, HALF)).reshape(slots * LONGEST, HALF)

    def cross_back(kv):
        return tuple(
            call(
                cross_backward,
                1,
                [whole(q_here), whole(g_here), whole(kv)],
                [whole(q_here), whole(kv)],
                [slot_shape, rows_shape],
                [],
                17 * 10**9,
            )(q_here, g_here, kv)
        )

    grad_here, grad_kv = lax.cond(is_stem, lambda: cross_back(kv_lo), lambda: cross_back(kv_moved))
    if lines.by_hand:
        grad_here, grad_kv, late_sum, got_out = barrier((grad_here, grad_kv, late_sum, got_out))
        late_got = lines.sum_first([late_sum])
    grad_kv_moved = lax.ppermute(grad_kv, "section", [(1, 0)])

    stem_kv_shapes = [
        rows_shape,
        shape((HALF, 2 * D), bf16),
        shape((HALF, 2 * D), bf16),
        shape((1, D), f32),
    ]

    def stem_kv():
        return tuple(
            call(
                stem_backward_kv,
                blocks,
                kv_specs + [rows_spec(D)] * 3,
                [rows_spec(D)] + [at(o.shape, 0, 0) for o in stem_kv_shapes[1:]],
                stem_kv_shapes,
                [pltpu.VMEM((D, 2 * D), bf16), pltpu.VMEM((D, 2 * D), f32)],
                23 * 10**9,
            )(*kv_inputs, patches, grad_kv, grad_kv_moved)
        )

    grad_b = grad_here
    grad_rows, kv_w_lo, kv_w_hi, patch_bias_sum = lax.cond(
        is_stem, stem_kv, lambda: tuple(blank(stem_kv_shapes))
    )
    grad_a = lax.ppermute(grad_b, "section", [(0, 1)])
    grad_a, grad_rows = barrier((grad_a, grad_rows))

    row_shape = shape((half_room, D), bf16)
    text_last_shapes = [
        shape((height, D), bf16),
        row_shape,
        row_shape,
        shape((HALF, 5 * D), bf16),
        shape((HALF, 5 * D), bf16),
        shape((4, D), f32),
    ]
    half_channels = CH // 2
    stem_last_shapes = [
        shape((image_rows, half_channels), bf16),
        shape((image_rows, half_channels), bf16),
        shape((CH, D), bf16),
        shape((2, CH), f32),
    ]

    def last_text():
        inputs = [
            grad_a, grad_b, take, place[None, :], grad_two, resid_one, embed,
            qkv_rows, mix_rows, start, vecs_outer,
        ]
        done = call(
            text_last,
            1,
            [blocks_spec] + [whole(a) for a in inputs] + qkv_specs,
            [whole(o) for o in text_last_shapes],
            text_last_shapes,
            [
                pltpu.VMEM((height, D), bf16),
                pltpu.VMEM((height, D), bf16),
                pltpu.VMEM((height, 2 * D), f32),
                pltpu.VMEM((D, 3 * D), f32),
                pltpu.VMEM((height, D), f32),
            ],
            25 * 10**9,
        )(row_blocks, *inputs, *qkv_inputs)
        return (*done, *blank(stem_last_shapes))

    def last_stem():
        done = call(
            stem_backward,
            blocks,
            [rows_spec(CH), whole(bn), patch_spec, rows_spec(D)],
            [rows_spec(half_channels)] * 2 + [at(o.shape, 0, 0) for o in stem_last_shapes[2:]],
            stem_last_shapes,
            [pltpu.VMEM((CH, D), f32)],
            22 * 10**9,
        )(features, bn, w_patch, grad_rows)
        return (*blank(text_last_shapes), *done)

    (
        grad_embed, rows_low, rows_high, grad_w_lo, grad_w_hi, grads_outer,
        grad_lo, grad_hi, grad_patch_w, bn_sums,
    ) = lax.cond(is_stem, last_stem, last_text)

    gone = jnp.zeros((), f32)
    vector_term = jnp.concatenate(
        [
            jnp.where(is_stem, bn_sums.reshape(-1), gone),
            jnp.where(is_stem, patch_bias_sum.reshape(-1), gone),
            jnp.where(
                is_stem,
                gone,
                jnp.concatenate(
                    [
                        grads_outer.reshape(-1),
                        grads_three.reshape(-1),
                        grad_up_bias.reshape(-1),
                        jnp.sum(cotangent, axis=0),
                    ]
                ),
            ),
        ]
    ).reshape(-1, CH)

    def summed(vector, first, last):
        step = first
        while step < last:
            vector = vector + lax.ppermute(vector, "dp", [(i, i ^ step) for i in range(dp)])
            step *= 2
        return vector

    grad_w_lo, grad_w_hi, kv_w_lo, kv_w_hi = barrier(
        (grad_w_lo, grad_w_hi, kv_w_lo, kv_w_hi)
    )
    if lines.by_hand:
        late_got, grad_w_lo = barrier((late_got, grad_w_lo))
    moved_rows = lax.ppermute(rows_low, "section", [(1, 0)])
    got_hi = lax.ppermute(grad_hi, "section", [(0, 1)])
    block_piece = simple(
        join_output,
        [slot_rows[None, :], own_row[:, None], got_out, out_here],
        [shape((tokens, HALF), bf16)],
        [],
        3 * 10**9,
    )[0]

    def sent_rows():
        return send(jnp.where(is_stem, moved_rows, rows_high).reshape(dp, room, D))

    if lines.by_hand:
        owners = CH // project_rows
        parts = grad_patch_w.reshape(owners, 2, project_rows // 2, D)
        terms = [
            (lax.ppermute(grad_w_lo, "section", [(1, 0)]), grad_w_hi),
            (kv_w_lo, lax.ppermute(kv_w_hi, "section", [(0, 1)])),
        ]
        terms = [
            tuple(w.reshape(4, 2, 2, HALF // dp, w.shape[1]) for w in term) for term in terms
        ]
        patch = (parts[:, 0], lax.ppermute(parts[:, 1], "section", [(0, 1)]))
        patch = [tuple(w.reshape(2, 2, 2, project_rows // 2, D) for w in patch)]
        late_got_two = lines.sum_second([late_sum], late_got)
        terms, patch, moved_rows = barrier((terms, patch, moved_rows))
        got = lines.sum_first(terms)
        patch_got = lines.sum_first(patch)
        got_rows = sent_rows()
        vector_total = summed(vector_term, 1, dp)
        late_line = lines.line_of([late_sum], late_got, late_got_two)
        late_parts = lines.sum_line(late_line)
        got, patch_got, vector_total = barrier((got, patch_got, vector_total))
        got_two = lines.sum_second(terms, got)
        patch_got_two = lines.sum_second(patch, patch_got)
        got_two, patch_got_two, late_parts = barrier((got_two, patch_got_two, late_parts))
        line = lines.line_of(terms, got, got_two)
        line_parts = lines.sum_line(line)
        patch_line = lines.line_of(patch, patch_got, patch_got_two)
        patch_got = lines.sum_low_first(patch_line)
        late_grad = lines.line_total(late_line, late_parts)
        tail_grad = lines.line_total(line, line_parts)
        patch_low = lines.sum_low_last(patch_line, patch_got)
        patch_high = lax.ppermute(patch_low, "section", [(1, 0)])
        down_grad = late_grad[:, CH + FF :].astype(f32).reshape(late_grad.shape[0], -1, 128)
        down_grad = down_grad.transpose(1, 0, 2).reshape(D, 128).T
        project_grad = down_grad + jnp.where(
            is_stem & (dp_index < owners), jnp.concatenate([patch_low, patch_high]), 0.0
        )
    else:
        vector_total = summed(vector_term, 1, dp)
        got_rows = sent_rows()
        tail_grad, patch_grad = lines.scatter_plain(
            grad_w_lo, grad_w_hi, kv_w_lo, kv_w_hi, grad_patch_w
        )
        project_grad = down_turned.astype(f32).T + patch_grad
    late_grad = late_grad.astype(f32)
    block_grad = jnp.concatenate(
        [tail_grad, late_grad[:, FF : FF + D], late_grad[:, :FF]], axis=1
    )
    vector_total = vector_total + lax.ppermute(vector_total, "section", [(0, 1), (1, 0)])
    vector_grad = lax.dynamic_slice_in_dim(
        vector_total.reshape(-1), me * vector_master.shape[0], vector_master.shape[0]
    )

    own_pre = jnp.where(is_stem, grad_lo, got_hi).astype(f32)
    first_channel = section * half_channels

    def own_half(array):
        return lax.dynamic_slice_in_dim(array, first_channel, half_channels, axis=array.ndim - 1)

    own_normed = (own_half(features).astype(f32) - own_half(center)) * own_half(factor)
    own_gain = own_half(bn_gain)
    feature_grad = own_half(factor) * (
        own_pre * own_gain
        - own_gain * own_half(vector_total[1]) / every_patch
        - own_normed * (own_gain * own_half(vector_total[0]) / every_patch)
    )

    def row_sums(asked, rows):
        hit = (jnp.arange(table_rows, dtype=i32)[:, None] == asked[None, :]).astype(bf16)
        return mm(hit, rows.reshape(half_room, D))

    def table_more(turn, total):
        place, asked = round_of(turn)
        slot = jnp.arange(group * room, dtype=i32)
        rows = mm((slot[:, None] == place[None, :]).astype(bf16), grad_embed).astype(bf16)
        moved = lax.ppermute(rows[:half_room], "section", [(1, 0)])
        rows = jnp.where(is_stem, moved, rows[half_room:]).reshape(dp, room, D)
        return total + row_sums(send(asked).reshape(half_room), send(rows))

    root_tokens = math.sqrt(tokens * dp)

    def table_update(total):
        return sgd_update(total, table_momentum, table_master, table_average, 0.05)

    table_new = lax.cond(
        rounds > 1,
        lambda: table_update(lax.fori_loop(1, rounds, table_more, row_sums(asked, got_rows))),
        lambda: table_update(row_sums(asked, got_rows)),
    )
    block_new = sgd_update(
        block_grad, block_momentum, block_master, block_average, 0.5 * D ** (-0.5) / root_tokens
    )
    project_new = sgd_update(
        project_grad,
        project_momentum,
        project_master,
        project_average,
        0.5 * FF ** (-0.5) / root_tokens,
    )
    vector_new = sgd_update(
        vector_grad, vector_momentum, vector_master, vector_average, 0.1 / root_tokens
    )
    return (block_piece, feature_grad, *table_new, *block_new, *project_new, *vector_new)


def solution(mesh):
    rows = P(BOTH, None)
    flat = P(BOTH)
    placed = (
        (P("dp", None), P(), P("dp"), P("dp", None), P("dp", None))
        + (rows,) * 9
        + (flat,) * 3
    )
    return jax.shard_map(
        per_device,
        mesh=mesh,
        in_specs=placed,
        out_specs=(P("dp", "section"), P("dp", "section")) + (rows,) * 15 + (flat,) * 5,
        check_vma=False,
    )
```

```python
import functools
import math

import jax
import jax.numpy as jnp
from jax import lax
from jax.experimental import pallas as pl
from jax.experimental.pallas import tpu as pltpu
from jax.sharding import PartitionSpec as P

D = 768
HEADS = 12
HEAD_DIM = 64
QUAD = 4 * HEAD_DIM
QUADS = HEADS // 4
FF = 3072
CH = 1024
PATCH = 196
WINDOW = 208
IMG_DEV = 16
GROUPS_DEV = 32
LONGEST = 32
HALF = D // 2
ROWS = 256
BLOCK = 128
SPAN = BLOCK + LONGEST
SCALE = HEAD_DIM ** (-0.5)
EPS = 1e-05
NEG = -1e30
BOTH = ("section", "dp")
VMEM_BYTES = 58 * 1024 * 1024
bf16 = jnp.bfloat16
f32 = jnp.float32
i32 = jnp.int32


def mm(left, right):
    return jnp.dot(left, right, preferred_element_type=f32)


def mm_rt(left, right):
    return lax.dot_general(left, right, (((1,), (1,)), ((), ())), preferred_element_type=f32)


def mm_lt(left, right):
    return lax.dot_general(left, right, (((0,), (0,)), ((), ())), preferred_element_type=f32)


def normalise(values):
    shifted = values - jnp.mean(values, axis=-1, keepdims=True)
    factor = lax.rsqrt(jnp.mean(shifted * shifted, axis=-1, keepdims=True) + EPS)
    return shifted * factor, factor


def norm_back(incoming, unit, factor, gain):
    scaled = incoming * gain
    mean_grad = jnp.mean(scaled, axis=-1, keepdims=True)
    mean_cross = jnp.mean(scaled * unit, axis=-1, keepdims=True)
    return factor * (scaled - mean_grad - unit * mean_cross)


GELU_C = math.sqrt(2.0 / math.pi)


def gelu_parts(values):
    square = values * values
    bend = jnp.tanh(GELU_C * values * (1.0 + 0.044715 * square))
    half = 0.5 * (1.0 + bend)
    slope = half + 0.5 * values * (1.0 - bend * bend) * (GELU_C * (1.0 + 3 * 0.044715 * square))
    return values * half, slope


def gelu_only(values):
    bend = jnp.tanh(GELU_C * values * (1.0 + 0.044715 * (values * values)))
    return 0.5 * values * (1.0 + bend)


def head_masks(dtype, width=QUAD):
    lanes = lax.broadcasted_iota(i32, (1, width), 1) // HEAD_DIM
    return [jnp.where(lanes == h, 1.0, 0.0).astype(dtype) for h in range(width // HEAD_DIM)]


def spread_heads(rows, masks):
    return jnp.concatenate([rows * m for m in masks], axis=0)


def join_heads(stacked, masks):
    count = stacked.shape[0] // len(masks)
    total = stacked[:count] * masks[0]
    for h in range(1, len(masks)):
        total = total + stacked[h * count : (h + 1) * count] * masks[h]
    return total


def softmax(scores, allowed):
    scores = jnp.where(allowed, scores * SCALE, NEG)
    weights = jnp.exp(scores - jnp.max(scores, axis=-1, keepdims=True))
    return weights * (1.0 / jnp.sum(weights, axis=-1, keepdims=True))


def one_hot_cols(index_col, width):
    places = lax.broadcasted_iota(i32, (index_col.shape[0], width), 1)
    return jnp.where(places == index_col, 1.0, 0.0).astype(bf16)


def one_hot_rows(index_row, height, offset=0):
    places = lax.broadcasted_iota(i32, (height, index_row.shape[1]), 0) + offset
    return jnp.where(places == index_row, 1.0, 0.0).astype(bf16)


def join_halves(target, low_ref, high_ref):
    count = low_ref.shape[0]
    target[:count, :] = low_ref[...]
    target[count : 2 * count, :] = high_ref[...]


def key_span(first):
    return pl.multiple_of(jnp.maximum(first - LONGEST, 0), LONGEST)


def self_allowed(start_rows, first, key_first):
    rows = lax.broadcasted_iota(i32, (BLOCK, SPAN), 0) + first
    keys = lax.broadcasted_iota(i32, (BLOCK, SPAN), 1) + key_first
    allowed = (keys <= rows) & (keys >= start_rows)
    return jnp.concatenate([jnp.where(allowed, 1, 0)] * 4, axis=0) > 0


def each_block(count, body):
    def step(index, carry):
        body(pl.multiple_of(index * BLOCK, BLOCK))
        return carry

    lax.fori_loop(0, count, step, 0)


def each_pair(count, body):
    pairs = count // 2

    def step(index, carry):
        body(pl.multiple_of(index * ROWS, ROWS), ROWS)
        return carry

    lax.fori_loop(0, pairs, step, 0)

    @pl.when(count % 2 == 1)
    def _():
        body(pl.multiple_of(pairs * ROWS, ROWS), BLOCK)


def text_first(
    blocks, embed, start, pack, vecs,
    qkv_lo, qkv_hi, out_lo, out_hi, cq_lo, cq_hi,
    qkv_rows, mix_rows, resid_one, slots_a, slots_b,
    w_qkv, w_out, w_cq, queries,
):
    count = blocks[0]
    join_halves(w_qkv, qkv_lo, qkv_hi)
    join_halves(w_out, out_lo, out_hi)
    join_halves(w_cq, cq_lo, cq_hi)
    queries[...] = jnp.zeros_like(queries)
    masks = head_masks(bf16)
    masks_f = head_masks(f32)

    def project(first, size):
        rows = pl.ds(first, size)
        unit, _ = normalise(embed[rows, :].astype(f32))
        normed = (unit * vecs[0:1, :] + vecs[1:2, :]).astype(bf16)
        for third in range(3):
            columns = slice(third * D, (third + 1) * D)
            qkv_rows[rows, columns] = mm(normed, w_qkv[:, columns]).astype(bf16)

    def attend(first):
        rows = pl.ds(first, BLOCK)
        key_first = key_span(first)
        span = pl.ds(key_first, SPAN)
        allowed = self_allowed(start[rows, :], first, key_first)
        for quad in range(QUADS):
            lanes, keys, values = quad_lanes(quad)
            query = spread_heads(qkv_rows[rows, lanes], masks)
            shares = softmax(mm_rt(query, qkv_rows[span, keys]), allowed)
            mixed = mm(shares.astype(bf16), qkv_rows[span, values])
            mix_rows[rows, lanes] = join_heads(mixed, masks_f).astype(bf16)

    def finish(first, size):
        rows = pl.ds(first, size)
        resid = embed[rows, :].astype(f32) + mm(mix_rows[rows, :], w_out[...])
        resid_one[rows, :] = resid
        unit, _ = normalise(resid)
        normed = (unit * vecs[2:3, :] + vecs[3:4, :]).astype(bf16)
        queries[rows, :] = mm(normed, w_cq[...]).astype(bf16)

    each_pair(count, project)
    each_block(count, attend)
    each_pair(count, finish)
    packed = mm(one_hot_cols(pack[...], queries.shape[0]), queries[...]).astype(bf16)
    slots_a[...] = packed[:, :HALF]
    slots_b[...] = packed[:, HALF:]


def quad_lanes(quad):
    return [slice(part * D + quad * QUAD, part * D + (quad + 1) * QUAD) for part in range(3)]


def text_middle(
    blocks, mix_a, mix_b, take, pack, arrival, own, resid_one, cotangent, vecs, up_bias,
    cout_lo, cout_hi, up_lo, up_hi, down_part,
    out_lo, out_hi, own_lo, own_hi, grad_two, late, slots_a, slots_b,
    vec_grad, up_bias_grad,
    w_cout, w_up, mixed, normed, normed_t, factor_s, total, back, grad_down_t,
    up_sum, down_sum, up_buffer, down_buffer, w_down_t, block_out, sems,
):
    step = pl.program_id(0)
    last = pl.num_programs(0) - 1
    count = blocks[0]
    wide = w_up.shape[1]
    by_owner = down_buffer.shape[1] != D

    def copies(chunk):
        slot = chunk % 2
        place = (chunk + 1) % 4
        columns = slice(chunk * wide, (chunk + 1) * wide)
        pairs = [(up_buffer.at[slot], late.at[:, columns])]
        if by_owner:
            height = down_buffer.shape[1]
            rows = slice(place * height, (place + 1) * height)
            pairs.append((down_buffer.at[slot], late.at[rows, CH + FF :]))
        else:
            columns = slice(CH + FF + place * wide, CH + FF + (place + 1) * wide)
            pairs.append((down_buffer.at[slot], late.at[:, columns]))
        return [
            pltpu.make_async_copy(source, target, sems.at[slot, i])
            for i, (source, target) in enumerate(pairs)
        ]

    for chunk in (0, 1):

        @pl.when(step == chunk + 2)
        def _():
            for copy in copies(chunk):
                copy.wait()

    @pl.when(step == 0)
    def _():
        w_cout[:HALF, :] = cout_lo[:, :D]
        w_cout[HALF:, :] = cout_hi[:, :D]
        normed[...] = jnp.zeros_like(normed)
        block_out[...] = jnp.zeros_like(block_out)
        vec_grad[...] = jnp.zeros_like(vec_grad)

        def begin(first, size):
            rows = pl.ds(first, size)
            places = lax.broadcasted_iota(i32, (size, take.shape[1]), 0) + first
            hit = jnp.where(places == take[...], 1.0, 0.0).astype(bf16)
            mixed[rows, :HALF] = mm(hit, mix_a[...]).astype(bf16)
            mixed[rows, HALF:] = mm(hit, mix_b[...]).astype(bf16)
            resid_two = resid_one[rows, :] + mm(mixed[rows, :], w_cout[...])
            unit, factor = normalise(resid_two)
            grad_two[rows, :] = unit
            factor_s[rows, :] = factor
            low = (unit * vecs[0:1, :] + vecs[1:2, :]).astype(bf16)
            normed[rows, :] = low
            normed_t[:, rows] = low.T
            total[rows, :] = resid_two + vecs[2:3, :]
            back[rows, :] = jnp.zeros((size, D), f32)
            grad_down_t[:, rows] = cotangent[rows, :].T

        each_pair(count, begin)

    @pl.when(step < last)
    def _():
        join_halves(w_up, up_lo, up_hi)
        parts = wide // 128
        if by_owner:
            height = down_buffer.shape[1] // parts
            for i in range(0, parts, 2):
                pair = down_part[i * height : (i + 2) * height, :].astype(f32)
                for h in range(2):
                    one = pair[h * height : (h + 1) * height]
                    one = jnp.concatenate([one[:, j : j + 128] for j in range(0, CH + FF, 128)], axis=0)
                    w_down_t[:, (i + h) * 128 : (i + h + 1) * 128] = one.astype(bf16)
        else:
            w_down_t[...] = down_part[...]
        up_sum[...] = jnp.zeros_like(up_sum)
        down_sum[...] = jnp.zeros_like(down_sum)
        up_bias_grad[...] = jnp.zeros_like(up_bias_grad)

        def forward_back(first, size):
            rows = pl.ds(first, size)
            act, slope = gelu_parts(mm(normed[rows, :], w_up[...]) + up_bias[...])
            act = act.astype(bf16)
            total[rows, :] += mm_rt(act, w_down_t[...])
            grad_up = (mm(cotangent[rows, :], w_down_t[...]) * slope).astype(bf16)
            up_bias_grad[...] += jnp.sum(grad_up.astype(f32), axis=0, keepdims=True)
            up_sum[...] += mm(normed_t[:, rows], grad_up)
            down_sum[...] += mm(grad_down_t[:, rows], act)
            back[rows, :] += mm_rt(grad_up, w_up[...])

        each_pair(count, forward_back)
        slot = step % 2
        up_buffer[slot] = up_sum[...].astype(bf16)
        if by_owner:
            pieces = [
                jnp.concatenate(
                    [down_sum[j : j + height, first : first + 128] for j in range(0, D, height)],
                    axis=1,
                )
                for first in range(0, wide, 128)
            ]
            for i in range(0, parts, 2):
                pair = jnp.concatenate(pieces[i : i + 2], axis=0).astype(bf16)
                down_buffer[slot, i * height : (i + 2) * height, :] = pair
        else:
            down_buffer[slot] = down_sum[...].astype(bf16)

    for chunk in range(3):

        @pl.when(step == chunk)
        def _():
            for copy in copies(chunk):
                copy.start()

    @pl.when(step == last)
    def _():
        up_sum[:, :D] = jnp.zeros((D, D), f32)

        def end(first, size):
            rows = pl.ds(first, size)
            block_out[rows, :] = total[rows, :].astype(bf16)
            incoming, unit = back[rows, :], grad_two[rows, :]
            vec_grad[0:1, :] += jnp.sum(incoming * unit, axis=0, keepdims=True)
            vec_grad[1:2, :] += jnp.sum(incoming, axis=0, keepdims=True)
            grad = norm_back(incoming, unit, factor_s[rows, :], vecs[0:1, :])
            grad = cotangent[rows, :].astype(f32) + grad
            grad_two[rows, :] = grad
            grad = grad.astype(bf16)
            up_sum[:, :D] += mm_lt(mixed[rows, :], grad)
            normed[rows, :] = mm_rt(grad, w_cout[...]).astype(bf16)

        each_pair(count, end)
        slot = step % 2
        up_buffer[slot, :, :D] = up_sum[:, :D].astype(bf16)
        up_buffer[slot, :, D:] = jnp.zeros((D, wide - D), bf16)
        down_buffer[slot] = jnp.zeros(down_buffer.shape[1:], bf16)
        for copy in copies(3):
            copy.start()
        for index, rows, lo, hi in (
            (pack, normed, slots_a, slots_b),
            (arrival, block_out, out_lo, out_hi),
            (own, block_out, own_lo, own_hi),
        ):
            for at_row in range(0, index.shape[0], 512):
                some = slice(at_row, at_row + 512)
                packed = mm(one_hot_cols(index[some, :], rows.shape[0]), rows[...]).astype(bf16)
                lo[some, :] = packed[:, :HALF]
                hi[some, :] = packed[:, HALF:]
        for chunk in (2, 3):
            for copy in copies(chunk):
                copy.wait()


def text_last(
    blocks, grad_a, grad_b, take, place, grad_two, resid_one, embed, qkv_rows, mix_rows, start, vecs,
    qkv_lo, qkv_hi, out_lo, out_hi, cq_lo, cq_hi,
    grad_embed, rows_a, rows_b, grad_lo, grad_hi, vec_grad,
    grad_mix, grad_queries, total, sums, grad_one,
):
    count = blocks[0]

    def keep(first, value):
        low = value.astype(bf16)
        width = value.shape[1]
        grad_lo[:, first : first + width] = low[:HALF]
        grad_hi[:, first : first + width] = low[HALF:]

    def turned_back(rows, lo, hi):
        return jnp.concatenate([mm_rt(rows, lo[...]), mm_rt(rows, hi[...])], axis=1)

    masks = head_masks(bf16)
    masks_f = head_masks(f32)
    vec_grad[...] = jnp.zeros_like(vec_grad)
    total[...] = jnp.zeros_like(total)
    sums[...] = jnp.zeros_like(sums)
    grad_embed[...] = jnp.zeros_like(grad_embed)

    def begin(first, size):
        rows = pl.ds(first, size)
        places = lax.broadcasted_iota(i32, (size, take.shape[1]), 0) + first
        hit = jnp.where(places == take[...], 1.0, 0.0).astype(bf16)
        grad_q = jnp.concatenate([mm(hit, grad_a[...]), mm(hit, grad_b[...])], axis=1).astype(bf16)
        unit, factor = normalise(resid_one[rows, :])
        normed = (unit * vecs[2:3, :] + vecs[3:4, :]).astype(bf16)
        sums[:, :D] += mm_lt(normed, grad_q)
        incoming = turned_back(grad_q, cq_lo, cq_hi)
        vec_grad[2:3, :] += jnp.sum(incoming * unit, axis=0, keepdims=True)
        vec_grad[3:4, :] += jnp.sum(incoming, axis=0, keepdims=True)
        grad = grad_two[rows, :] + norm_back(incoming, unit, factor, vecs[2:3, :])
        grad_one[rows, :] = grad
        grad = grad.astype(bf16)
        sums[:, D : 2 * D] += mm_lt(mix_rows[rows, :], grad)
        grad_mix[rows, :] = turned_back(grad, out_lo, out_hi).astype(bf16)

    def attend(first):
        rows = pl.ds(first, BLOCK)
        key_first = key_span(first)
        span = pl.ds(key_first, SPAN)
        allowed = self_allowed(start[rows, :], first, key_first)
        for quad in range(QUADS):
            lanes, keys, values = quad_lanes(quad)
            query = spread_heads(qkv_rows[rows, lanes], masks)
            grad = spread_heads(grad_mix[rows, lanes], masks)
            key_rows = qkv_rows[span, keys]
            shares = softmax(mm_rt(query, key_rows), allowed)
            grad_shares = mm_rt(grad, qkv_rows[span, values])
            inner = jnp.sum(grad_shares * shares, axis=-1, keepdims=True)
            grad_scores = (shares * (grad_shares - inner)).astype(bf16)
            back = join_heads(mm(grad_scores, key_rows), masks_f) * SCALE
            grad_queries[rows, lanes] = back.astype(bf16)
            later = slice(D + quad * QUAD, D + (quad + 1) * QUAD)
            total[span, lanes] += mm_lt(grad_scores, query) * SCALE
            total[span, later] += mm_lt(shares.astype(bf16), grad)

    def end(first, size):
        rows = pl.ds(first, size)
        unit, factor = normalise(embed[rows, :].astype(f32))
        normed = (unit * vecs[0:1, :] + vecs[1:2, :]).astype(bf16)
        grad = jnp.concatenate([grad_queries[rows, :], total[rows, :].astype(bf16)], axis=1)
        for third in range(3):
            columns = slice(third * D, (third + 1) * D)
            sums[:, columns] += mm_lt(normed, grad[:, columns])
        incoming = turned_back(grad, qkv_lo, qkv_hi)
        vec_grad[0:1, :] += jnp.sum(incoming * unit, axis=0, keepdims=True)
        vec_grad[1:2, :] += jnp.sum(incoming, axis=0, keepdims=True)
        grad = grad_one[rows, :] + norm_back(incoming, unit, factor, vecs[0:1, :])
        grad_embed[rows, :] = grad.astype(bf16)

    each_pair(count, begin)
    keep(4 * D, sums[:, :D])
    keep(3 * D, sums[:, D : 2 * D])
    each_block(count, attend)
    sums[...] = jnp.zeros_like(sums)
    each_pair(count, end)
    keep(0, sums[...])
    half = rows_a.shape[0]
    rows_a[...] = mm(one_hot_rows(place[...], half), grad_embed[...]).astype(bf16)
    rows_b[...] = mm(one_hot_rows(place[...], half, half), grad_embed[...]).astype(bf16)


def unpack_rows(rows_a, rows_b, place, embed):
    count = rows_a.shape[0]
    total = mm(one_hot_cols(place[...], count), rows_a[...])
    total = total + mm(one_hot_cols(place[...] - count, count), rows_b[...])
    embed[...] = total.astype(bf16)


def pack_half(index, rows, packed):
    packed[...] = mm(one_hot_cols(index[...], rows.shape[0]), rows[...].astype(bf16)).astype(bf16)


def join_cotangent(arrival, own, slots_a, slots_b, rows, joined):
    height = joined.shape[0]
    low = mm(one_hot_rows(own[...], height), rows[...].astype(bf16))
    hit = one_hot_rows(arrival[...], height)
    joined[:, :HALF] = (low[:, :HALF] + mm(hit, slots_a[...])).astype(bf16)
    joined[:, HALF:] = (low[:, HALF:] + mm(hit, slots_b[...])).astype(bf16)


def join_output(slot_rows, slots, own, joined):
    total = mm(one_hot_rows(slot_rows[...], joined.shape[0]), slots[...])
    joined[...] = (total + own[...].astype(f32)).astype(bf16)


def join_kv(w_kv, k_lo, k_hi, v_lo, v_hi):
    for first, (lo, hi) in enumerate(((k_lo, k_hi), (v_lo, v_hi))):
        for part in range(2):
            columns = slice((2 * part + first) * HALF, (2 * part + first + 1) * HALF)
            w_kv[:HALF, columns] = lo[:, part * HALF : (part + 1) * HALF]
            w_kv[HALF:, columns] = hi[:, part * HALF : (part + 1) * HALF]


def stem_forward(
    features, bn, w_patch, patch_bias, k_lo, k_hi, v_lo, v_hi, patches, kv_lo, kv_hi, w_kv
):
    @pl.when(pl.program_id(0) == 0)
    def _():
        join_kv(w_kv, k_lo, k_hi, v_lo, v_hi)

    normed = (features[...].astype(f32) - bn[0:1, :]) * bn[1:2, :]
    hidden = gelu_only(normed * bn[2:3, :] + bn[3:4, :]).astype(bf16)
    rows = (mm(hidden, w_patch[...]) + patch_bias[...]).astype(bf16)
    patches[...] = rows
    kv_lo[...] = mm(rows, w_kv[:, :D]).astype(bf16)
    kv_hi[...] = mm(rows, w_kv[:, D:]).astype(bf16)


def image_window(image):
    first = image * PATCH
    aligned = pl.multiple_of(first // 16 * 16, 16)
    lanes = lax.broadcasted_iota(i32, (1, WINDOW), 1) + (aligned - first)
    return aligned, (lanes >= 0) & (lanes < PATCH)


def cross_forward(queries, kv, mixed):
    masks = head_masks(bf16, HALF)
    masks_f = head_masks(f32, HALF)

    def image(index, carry):
        aligned, allowed = image_window(index)
        window = pl.ds(aligned, WINDOW)
        place = pl.ds(pl.multiple_of(index * LONGEST, LONGEST), LONGEST)
        scores = mm_rt(spread_heads(queries[place, :], masks), kv[window, :HALF])
        shares = softmax(scores, allowed).astype(bf16)
        mixed[place, :] = join_heads(mm(shares, kv[window, HALF:]), masks_f).astype(bf16)
        return carry

    lax.fori_loop(0, IMG_DEV, image, 0, unroll=4)


def cross_backward(queries, grads, kv, grad_q, grad_kv):
    grad_kv[...] = jnp.zeros_like(grad_kv)
    masks = head_masks(bf16, HALF)
    masks_f = head_masks(f32, HALF)

    def image(index, carry):
        aligned, allowed = image_window(index)
        window = pl.ds(aligned, WINDOW)
        place = pl.ds(pl.multiple_of(index * LONGEST, LONGEST), LONGEST)
        query = spread_heads(queries[place, :], masks)
        grad = spread_heads(grads[place, :], masks)
        keys = kv[window, :HALF]
        shares = softmax(mm_rt(query, keys), allowed)
        grad_shares = mm_rt(grad, kv[window, HALF:])
        inner = jnp.sum(grad_shares * shares, axis=-1, keepdims=True)
        grad_scores = (shares * (grad_shares - inner)).astype(bf16)
        grad_q[place, :] = (join_heads(mm(grad_scores, keys), masks_f) * SCALE).astype(bf16)
        grad_kv[window, :HALF] += (mm_lt(grad_scores, query) * SCALE).astype(bf16)
        grad_kv[window, HALF:] += mm_lt(shares.astype(bf16), grad).astype(bf16)
        return carry

    lax.fori_loop(0, IMG_DEV, image, 0, unroll=4)


def stem_backward_kv(
    k_lo, k_hi, v_lo, v_hi, patches, grad_kv_lo, grad_kv_hi,
    grad_rows, grad_lo, grad_hi, bias_sum,
    w_kv, total,
):
    step = pl.program_id(0)

    @pl.when(step == 0)
    def _():
        join_kv(w_kv, k_lo, k_hi, v_lo, v_hi)
        total[...] = jnp.zeros_like(total)
        bias_sum[...] = jnp.zeros_like(bias_sum)

    rows = mm_rt(grad_kv_lo[...], w_kv[:, :D]) + mm_rt(grad_kv_hi[...], w_kv[:, D:])
    rows = rows.astype(bf16)
    grad_rows[...] = rows
    bias_sum[...] += jnp.sum(rows.astype(f32), axis=0, keepdims=True)
    turned = patches[...].T
    total[:, :D] += mm(turned, grad_kv_lo[...])
    total[:, D:] += mm(turned, grad_kv_hi[...])

    @pl.when(step == pl.num_programs(0) - 1)
    def _():
        for first in range(2):
            for part in range(2):
                source = slice((2 * part + first) * HALF, (2 * part + first + 1) * HALF)
                target = slice((2 * first + part) * HALF, (2 * first + part + 1) * HALF)
                grad_lo[:, target] = total[:HALF, source].astype(bf16)
                grad_hi[:, target] = total[HALF:, source].astype(bf16)


def stem_backward(
    features, bn, w_patch, grad_rows, grad_lo, grad_hi, grad_patch_w, sums, patch_acc
):
    step = pl.program_id(0)

    @pl.when(step == 0)
    def _():
        patch_acc[...] = jnp.zeros_like(patch_acc)
        sums[...] = jnp.zeros_like(sums)

    normed = (features[...].astype(f32) - bn[0:1, :]) * bn[1:2, :]
    hidden, slope = gelu_parts(normed * bn[2:3, :] + bn[3:4, :])
    patch_acc[...] += mm_lt(hidden.astype(bf16), grad_rows[...])
    grad_pre = mm_rt(grad_rows[...], w_patch[...]) * slope
    sums[0:1, :] += jnp.sum(grad_pre * normed, axis=0, keepdims=True)
    sums[1:2, :] += jnp.sum(grad_pre, axis=0, keepdims=True)
    grad_low = grad_pre.astype(bf16)
    grad_lo[...] = grad_low[:, : CH // 2]
    grad_hi[...] = grad_low[:, CH // 2 :]

    @pl.when(step == pl.num_programs(0) - 1)
    def _():
        grad_patch_w[...] = patch_acc[...].astype(bf16)


def place_pieces(where_, two, four, two_other, four_other, first, second, *scratch, split):
    dp_index, section = where_[0], where_[1]
    width, all_width = first.shape[-1], two.shape[-1]
    cuts = (slice(0, width), slice(width, all_width))
    sems = scratch[-1]

    def pieces(part, jobs):
        copies = []
        for core, sources in ((1 - part, (two_other, four_other)), (part, (two, four))):
            for z in range(4):
                for far, turn, bits in ((0, 0, 0), (0, 1, 1 + core), (1, 0, 2 - core), (1, 1, 3)):
                    target = dp_index ^ (4 * z) ^ bits
                    for cut, place in jobs:
                        copies.append(
                            pltpu.make_async_copy(
                                sources[far].at[turn, z, :, cut],
                                place.at[core, target],
                                sems.at[len(copies)],
                            )
                        )
        for copy in copies:
            copy.start()
        for copy in copies:
            copy.wait()

    for part in range(2):

        @pl.when(section == part)
        def _():
            if split:
                out = (second, first)[part]
                buffer = (scratch[1], scratch[0])[part]
                pieces(part, [(cuts[1 - part], buffer)])
                final = pltpu.make_async_copy(buffer, out, sems.at[0])
                final.start()
                final.wait()
            else:
                pieces(part, [(cuts[0], first), (cuts[1], second)])


def shape(dims, dtype):
    return jax.ShapeDtypeStruct(dims, dtype)


def whole(array):
    zeros = (0,) * len(array.shape)
    return pl.BlockSpec(array.shape, lambda *_: zeros, pipeline_mode=pl.Buffered(1))


def at(dims, *index):
    return pl.BlockSpec(dims, lambda *_: index)


def call(kernel, steps, in_specs, out_specs, outs, scratch, flops):
    return pl.pallas_call(
        kernel,
        grid=(steps,),
        in_specs=in_specs,
        out_specs=out_specs,
        out_shape=outs,
        scratch_shapes=scratch,
        compiler_params=pltpu.CompilerParams(vmem_limit_bytes=VMEM_BYTES),
        cost_estimate=pl.CostEstimate(flops=flops, bytes_accessed=0, transcendentals=0),
    )


def simple(kernel, inputs, outs, scratch, flops):
    return call(
        kernel,
        1,
        [whole(a) for a in inputs],
        [at(o.shape, *(0,) * len(o.shape)) for o in outs],
        outs,
        scratch,
        flops,
    )(*inputs)


def blank(outs):
    return pl.pallas_call(
        lambda *refs: None,
        out_shape=outs,
        out_specs=[pl.BlockSpec(memory_space=pl.ANY) for _ in outs],
    )()


barrier = lax.optimization_barrier


class Lines:
    def __init__(self, dp, dp_index, section):
        self.dp, self.dp_index, self.section = dp, dp_index, section
        self.is_stem = section == 0
        self.by_hand = dp == 16
        self.x, self.y, self.z = dp_index & 1, dp_index // 2 & 1, dp_index // 4

    def across(self, array, low, high):
        count = self.dp
        pairs = [(d, d ^ low) for d in range(count)]
        pairs += [(count + d, count + (d ^ high)) for d in range(count)]
        return lax.ppermute(array, BOTH, pairs)

    def swap(self, array):
        return lax.ppermute(array, "section", [(0, 1), (1, 0)])

    def gather_line(self, shard):
        return jnp.stack([shard] + [self.across(shard, 4 * k, 4 * k) for k in (1, 2, 3)])

    def gather_first(self, line):
        return jnp.stack([line, self.across(line, 1, 2)])

    def gather_second(self, two):
        return two, self.across(two, 2, 1)

    def gather_place(self, two, four, text_width):
        inputs = [two, four, self.swap(two), self.swap(four)]
        split = text_width is not None
        any_spec = pl.BlockSpec(memory_space=pl.ANY)
        rows, width = two.shape[2:]
        count = 2 * self.dp
        first = text_width if split else CH
        shapes = [(2, self.dp, rows, w) for w in (first, width - first)]
        buffers = [pltpu.VMEM(dims, bf16) for dims in shapes] if split else []
        out_spec = any_spec if split else pl.BlockSpec(memory_space=pltpu.VMEM)
        placed = pl.pallas_call(
            functools.partial(place_pieces, split=split),
            in_specs=[pl.BlockSpec(memory_space=pltpu.SMEM)] + [any_spec] * 4,
            out_specs=[out_spec] * 2,
            out_shape=[shape(dims, bf16) for dims in shapes],
            scratch_shapes=buffers + [pltpu.SemaphoreType.DMA((2 * count,))],
            compiler_params=pltpu.CompilerParams(vmem_limit_bytes=VMEM_BYTES),
        )(jnp.stack([self.dp_index, self.section]), *inputs)
        return [p.reshape(count * rows, p.shape[-1]) for p in placed]

    def fold_small(self, stats, vector, rows):
        first = lax.reduce_precision(stats, 8, 7)
        second = lax.reduce_precision(stats - first, 8, 7)
        third = stats - first - second
        terms = jnp.stack([first, second, third]).astype(bf16).reshape(rows, -1)
        count = rows * 128 - vector.shape[0]
        vector = jnp.concatenate([vector.astype(bf16), jnp.zeros((count,), bf16)])
        return jnp.concatenate([terms, vector.reshape(rows, 128)], axis=1)

    def unfold_small(self, shared, count, each):
        shared = shared.reshape(2, self.dp, -1, shared.shape[-1])
        stats = shared[0, :, :, :-128].astype(f32).reshape(self.dp, 3, 2, CH)
        stats = stats[:, 0] + stats[:, 1] + stats[:, 2]
        center = jnp.mean(stats[:, 0], axis=0)
        squares = jnp.sum(stats[:, 1] + each * jnp.square(stats[:, 0] - center), axis=0)
        lines = (count + 127) // 128
        vector = shared[:, :, :lines, -128:].reshape(2 * self.dp, lines * 128)[:, :count]
        return center, squares, vector.reshape(-1).astype(f32)

    def share_patch(self, project_low):
        count = self.dp // 2
        half = project_low.shape[0] // 2
        moved = lax.ppermute(project_low[half:], BOTH, [(d, d + count) for d in range(count)])
        mine = jnp.where(self.z < 2, project_low[:half], moved)
        moved = lax.ppermute(mine[half // 2 :], "section", [(0, 1)])
        return jnp.where(self.is_stem, mine[: half // 2], moved)

    def fold_patch(self, part, rows):
        rest = part.shape[0] - rows
        width = D * rest // rows
        tail = [part[rows:, first : first + width] for first in range(0, D, width)]
        return jnp.concatenate([part[:rows], jnp.concatenate(tail)], axis=1)

    def unfold_patch(self, parts):
        count, rows, width = parts.shape
        rest = rows * (width - D) // D
        tail = [parts[:, first : first + rest, D:] for first in range(0, rows, rest)]
        parts = jnp.concatenate([parts[:, :, :D], jnp.concatenate(tail, axis=2)], axis=1)
        parts = parts.reshape(2, 2, self.dp // 2, rows + rest, D)
        return parts.transpose(2, 1, 0, 3, 4).reshape(-1, D)

    def pick(self, places, axis, place):
        return lax.dynamic_index_in_dim(places, place, axis, keepdims=False)

    def first_half(self, terms, flip):
        along_y = [self.pick(stem, 1, self.y ^ flip) for stem, _ in terms]
        along_x = [self.pick(text, 2, self.x ^ flip) for _, text in terms]
        parts = [jnp.where(self.is_stem, *both) for both in zip(along_y, along_x)]
        return jnp.concatenate(parts, axis=-1)

    def second_half(self, terms, got, flip):
        place = jnp.where(self.is_stem, self.x, self.y) ^ flip
        kept = self.pick(self.first_half(terms, 0), 1, place).astype(f32)
        return (kept + self.pick(got, 1, place).astype(f32)).astype(bf16)

    def sum_first(self, terms):
        return self.across(self.first_half(terms, 1), 2, 1)

    def sum_second(self, terms, got):
        return self.across(self.second_half(terms, got, 1), 1, 2)

    def line_of(self, terms, got, got_two):
        kept = self.second_half(terms, got, 0).astype(f32)
        return (kept + got_two.astype(f32)).astype(bf16)

    def sum_line(self, line):
        parts = [self.pick(line, 0, self.z ^ k) for k in (1, 2, 3)]
        return [self.across(p, 4 * k, 4 * k) for k, p in zip((1, 2, 3), parts)]

    def line_total(self, line, parts):
        return self.pick(line, 0, self.z).astype(f32) + sum(part.astype(f32) for part in parts)

    def sum_low_first(self, line):
        return self.across(line, 8, 8)

    def sum_low_last(self, line, got):
        line = (line.astype(f32) + got.astype(f32)).astype(bf16)
        low = self.z & 1
        got = self.across(self.pick(line, 0, 1 - low), 4, 4)
        return self.pick(line, 0, low).astype(f32) + got.astype(f32)

    def scatter_plain(self, w_lo, w_hi, kv_lo, kv_hi, patch):
        def total(term):
            return lax.psum_scatter(term, BOTH, scatter_dimension=0, tiled=True).astype(f32)

        own_w = jnp.concatenate([w_lo, w_hi])
        own_kv = jnp.concatenate([kv_lo, kv_hi])
        own_patch = jnp.concatenate([patch, jnp.zeros((FF, D), bf16)])
        return (
            total(
                jnp.concatenate(
                    [
                        jnp.where(self.is_stem, jnp.zeros_like(own_w), own_w),
                        jnp.where(self.is_stem, own_kv, jnp.zeros_like(own_kv)),
                    ],
                    axis=1,
                )
            ),
            total(jnp.where(self.is_stem, own_patch, jnp.zeros_like(own_patch))),
        )


def sgd_update(gradient, momentum, master, average, step_rate):
    new_momentum = 0.9 * momentum + gradient
    new_master = master - step_rate * (gradient + 0.9 * new_momentum)
    new_average = 0.8 * average + 0.2 * new_master
    return (gradient, new_momentum, new_average, new_master, new_master.astype(bf16))


def per_device(
    features,
    image_group,
    token_ids,
    text_lengths,
    cotangent,
    table_master,
    table_momentum,
    table_average,
    block_master,
    block_momentum,
    block_average,
    project_master,
    project_momentum,
    project_average,
    vector_master,
    vector_momentum,
    vector_average,
):
    dp = lax.axis_size("dp")
    group = lax.axis_size(BOTH)
    dp_index = lax.axis_index("dp")
    section = lax.axis_index("section")
    is_stem = section == 0
    me = section * dp + dp_index
    tokens = token_ids.shape[0]
    image_rows = features.shape[0]
    every_patch = image_rows * dp
    table_rows = table_master.shape[0]
    images = image_group.shape[0]

    lines = Lines(dp, dp_index, section)
    block_low = block_master.astype(bf16)
    project_low = project_master.astype(bf16)
    early = block_low[:, : 7 * D]
    late_low = jnp.concatenate(
        [
            block_low[:, 8 * D :],
            block_low[:, 7 * D : 8 * D],
            jnp.zeros((block_low.shape[0], CH - D), bf16),
        ],
        axis=1,
    )
    project_rows = project_master.shape[0]
    if lines.by_hand:
        rows = late_low.shape[0]
        down_low = project_low.T.reshape(-1, rows, 128).transpose(1, 0, 2).reshape(rows, CH + FF)
        late_low = jnp.concatenate([down_low, late_low], axis=1)

    def send(block):
        return lax.all_to_all(block, "dp", split_axis=0, concat_axis=0, tiled=True)

    capacity = (2 * IMG_DEV + dp - 1) // dp
    slots = dp * capacity
    destination = image_group // GROUPS_DEV
    by_source = destination.reshape(dp, IMG_DEV)
    order = jnp.arange(IMG_DEV, dtype=i32)
    earlier = order[None, :] < order[:, None]
    rank_all = jnp.sum(
        ((by_source[:, :, None] == by_source[:, None, :]) & earlier[None]).astype(i32), axis=2
    ).reshape(images)
    my_dest = lax.dynamic_slice_in_dim(destination, dp_index * IMG_DEV, IMG_DEV)
    my_rank = lax.dynamic_slice_in_dim(rank_all, dp_index * IMG_DEV, IMG_DEV)
    stem_slot = my_dest * capacity + my_rank
    slot_of_image = jnp.where(
        destination == dp_index,
        jnp.arange(images, dtype=i32) // IMG_DEV * capacity + rank_all,
        -1,
    )
    lengths = text_lengths[0]
    group_ends = jnp.cumsum(lengths)
    group_starts = group_ends - lengths
    places = jnp.arange(tokens, dtype=i32)
    groups = jnp.arange(GROUPS_DEV, dtype=i32)
    named = jnp.any(image_group[None, :] == (dp_index * GROUPS_DEV + groups)[:, None], axis=1)
    within_group = (group_starts[None, :] <= places[:, None]) & (
        places[:, None] < group_ends[None, :]
    )
    token_start = jnp.sum(jnp.where(within_group, group_starts[None, :], 0), axis=1)
    token_named = jnp.any(within_group & named[None, :], axis=1)
    match = slot_of_image[None, :] == jnp.arange(slots, dtype=i32)[:, None]
    slot_group = jnp.max(jnp.where(match, (image_group % GROUPS_DEV)[None, :], -1), axis=1)
    group_hit = slot_group[:, None] == groups[None, :]
    slot_start = jnp.sum(jnp.where(group_hit, group_starts[None, :], 0), axis=1)
    slot_length = jnp.sum(jnp.where(group_hit, lengths[None, :], 0), axis=1)
    within = jnp.arange(LONGEST, dtype=i32)
    slot_rows = jnp.where(
        within[None, :] < slot_length[:, None], slot_start[:, None] + within[None, :], -1
    ).reshape(slots * LONGEST)
    slot_ids = jnp.max(
        jnp.where(slot_rows[:, None] == places[None, :], token_ids[None, :], -1), axis=1
    )

    slot_ids, features = barrier((slot_ids, features))
    rows_f = features.astype(f32)
    local_center = jnp.mean(rows_f, axis=0)
    local_square = jnp.sum(jnp.square(rows_f - local_center), axis=0)
    state = jnp.stack([local_center, local_square])
    vector_low = lax.reduce_precision(vector_master, 8, 7)
    if lines.by_hand:
        later = jnp.concatenate(
            [
                lines.fold_patch(lines.share_patch(project_low), early.shape[0]),
                lines.fold_small(state, vector_low, early.shape[0]),
            ],
            axis=1,
        )
        early = lines.gather_line(early)

    got_ids = send(slot_ids.reshape(dp, capacity * LONGEST)).reshape(slots, LONGEST)
    slot_hit = stem_slot[:, None] == jnp.arange(slots, dtype=i32)[None, :]
    image_ids = jnp.max(jnp.where(slot_hit[:, :, None], got_ids[None], -1), axis=1)
    ids = jnp.concatenate([image_ids.reshape(-1), jnp.where(token_named, -1, token_ids)])
    height = ids.shape[0]
    here = ids >= 0
    candidates = jnp.arange(height, dtype=i32)
    before = candidates[None, :] < candidates[:, None]
    row = jnp.sum((before & here[None, :]).astype(i32), axis=1)
    row = jnp.where(here, row, -1)
    row_count = jnp.sum(here.astype(i32))
    row_blocks = jnp.maximum((row_count + BLOCK - 1) // BLOCK, 2).reshape(1)
    depth = jnp.concatenate(
        [jnp.tile(within, IMG_DEV), places - token_start]
    )
    image_row, own_row = row[: IMG_DEV * LONGEST], row[IMG_DEV * LONGEST :]
    arrival_row = jnp.max(
        jnp.where(slot_hit[:, :, None], image_row.reshape(IMG_DEV, 1, LONGEST), -1), axis=0
    ).reshape(slots * LONGEST)
    chosen = row[None, :] == candidates[:, None]
    start = jnp.max(jnp.where(chosen, (row - depth)[None, :], -1), axis=1)
    start = jnp.where(candidates < row_count, start, candidates)[:, None]

    room = max(16, (2 * tokens + 2 * tokens // 4) // group)
    half_room = dp * room
    owner = ids // table_rows
    same = (ids[:, None] == ids[None, :]) & here[None, :]
    is_first = here & ~jnp.any(same & before, axis=1)
    rank = jnp.sum(
        ((owner[:, None] == owner[None, :]) & before & is_first[None, :]).astype(i32), axis=1
    )
    rounds_here = jnp.max(jnp.where(is_first, rank, 0)) // room + 1
    table_low = table_master.astype(bf16)

    def round_of(turn):
        turn_rank = rank - turn * room
        first_place = jnp.where(
            is_first & (turn_rank >= 0) & (turn_rank < room), owner * room + turn_rank, -1
        )
        place = jnp.max(jnp.where(same, first_place[None, :], -1), axis=1)
        place = jnp.max(jnp.where(chosen, place[None, :], -1), axis=1)
        slot = jnp.arange(half_room, dtype=i32) + section * half_room
        asked = jnp.max(
            jnp.where(first_place[None, :] == slot[:, None], (ids % table_rows)[None, :], -1),
            axis=1,
        )
        return place, asked.reshape(dp, room)

    def serve(asked):
        hit = (asked[:, None] == jnp.arange(table_rows, dtype=i32)[None, :]).astype(bf16)
        served = mm(hit, table_low).astype(bf16)
        return send(served.reshape(dp, room, D)).reshape(half_room, D)

    def unpacked(place, served, served_low):
        return simple(
            unpack_rows,
            [served_low, served, place[:, None]],
            [shape((height, D), bf16)],
            [],
            4 * 10**9,
        )[0]

    arrival_shape = shape((slots * LONGEST, HALF), bf16)
    cot_sent = simple(
        pack_half,
        [slot_rows[:, None], lax.dynamic_slice_in_dim(cotangent, section * HALF, HALF, axis=1)],
        [arrival_shape],
        [],
        3 * 10**9,
    )[0]
    if lines.by_hand:
        got_ids, early, later, cot_sent = barrier((got_ids, early, later, cot_sent))
        early = lines.gather_first(early)
        later = lines.gather_line(later)
    place, asked = round_of(0)
    asked = jnp.concatenate([asked, jnp.broadcast_to(rounds_here, (dp, 1))], axis=1)
    asked = send(asked)
    if lines.by_hand:
        asked, early, later, cot_sent = barrier((asked, early, later, cot_sent))
        early = lines.gather_second(early)
        later = lines.gather_first(later)
        cot_b = send(cot_sent.reshape(dp, capacity * LONGEST, HALF))
        cot_b = cot_b.reshape(slots * LONGEST, HALF)
    rounds = jnp.max(asked[:, room])
    asked = asked[:, :room].reshape(half_room)
    served = serve(asked)
    served_low = lax.ppermute(served, "section", [(0, 1)])
    if lines.by_hand:
        served, served_low, early, later, place, start, late_low, cot_b = barrier(
            (served, served_low, early, later, place, start, late_low, cot_b)
        )
        w_late = w_down = lax.all_gather(late_low, BOTH, axis=0, tiled=True)
        later = lines.gather_second(later)
        w_text, w_kv = lines.gather_place(*early, 5 * D)
        w_patch, shared = lines.gather_place(*later, None)
        w_patch = lines.unfold_patch(w_patch.reshape(2 * dp, -1, CH))
        center, squares, flat = lines.unfold_small(shared, vector_master.shape[0], image_rows)
    else:
        w_text = lax.all_gather(early[:, : 5 * D], BOTH, axis=0, tiled=True)
        w_kv = lax.all_gather(early[:, 5 * D :], BOTH, axis=0, tiled=True)
        cot_b = send(cot_sent.reshape(dp, capacity * LONGEST, HALF))
        cot_b = cot_b.reshape(slots * LONGEST, HALF)
        w_late = lax.all_gather(late_low, BOTH, axis=0, tiled=True)
        project_full = lax.all_gather(project_low, BOTH, axis=0, tiled=True)
        w_down = project_full.T
        w_patch = project_full[:CH]
        stats = lax.all_gather(state, "dp")
        center = jnp.mean(stats[:, 0], axis=0)
        squares = jnp.sum(stats[:, 1] + image_rows * jnp.square(stats[:, 0] - center), axis=0)
        flat = lax.all_gather(vector_low, BOTH, axis=0, tiled=True)
    factor = lax.rsqrt(squares / every_patch + EPS)
    bn_gain, bn_bias = flat[:CH], flat[CH : 2 * CH]
    offset = 2 * CH + D
    patch_bias = flat[2 * CH : offset].reshape(1, D)
    ln_vecs = flat[offset : offset + 6 * D].reshape(6, D)
    up_bias = flat[offset + 6 * D : offset + 6 * D + FF].reshape(1, FF)
    down_bias = flat[offset + 6 * D + FF :].reshape(1, D)
    vecs_outer = ln_vecs[:4]
    vecs_three = jnp.concatenate([ln_vecs[4:], down_bias])
    bn = jnp.stack([center, factor, bn_gain, bn_bias])

    def embed_more(turn, embed):
        place, asked = round_of(turn)
        served = serve(send(asked).reshape(half_room))
        return embed + unpacked(place, served, lax.ppermute(served, "section", [(0, 1)]))

    embed = lax.fori_loop(1, rounds, embed_more, unpacked(place, served, served_low))

    if lines.by_hand:
        w_text, w_kv, w_patch, embed = barrier((w_text, w_kv, w_patch, embed))

    def halves(width, column):
        return [at((HALF, width), 0, column), at((HALF, width), 1, column)]

    qkv_specs = halves(3 * D, 0) + halves(D, 3) + halves(D, 4)
    qkv_inputs = [w_text] * 6
    kv_specs = halves(D, 0) + halves(D, 1)
    kv_inputs = [w_kv] * 4
    patch_spec = at((CH, D), 0, 0)
    blocks = 7
    per_block = image_rows // blocks
    qkv_scratch = [
        pltpu.VMEM((D, 3 * D), bf16),
        pltpu.VMEM((D, D), bf16),
        pltpu.VMEM((D, D), bf16),
        pltpu.VMEM((height, D), bf16),
    ]

    def rows_spec(width):
        return pl.BlockSpec((per_block, width), lambda step: (step, 0))

    slot_shape = shape((IMG_DEV * LONGEST, HALF), bf16)
    blocks_spec = pl.BlockSpec(memory_space=pltpu.SMEM)
    pack, take = image_row[:, None], image_row[None, :]
    rows_shape = shape((image_rows, D), bf16)

    text_saved = [
        shape((height, 3 * D), bf16),
        shape((height, D), bf16),
        shape((height, D), f32),
        slot_shape,
        slot_shape,
    ]
    stem_saved = [rows_shape] * 3

    def first_text():
        inputs = [embed, start, pack, vecs_outer]
        done = call(
            text_first,
            1,
            [blocks_spec] + [whole(a) for a in inputs] + qkv_specs,
            [whole(o) for o in text_saved],
            text_saved,
            qkv_scratch,
            15 * 10**9,
        )(row_blocks, *inputs, *qkv_inputs)
        return (*done, *blank(stem_saved))

    def first_stem():
        done = call(
            stem_forward,
            blocks,
            [rows_spec(CH), whole(bn), patch_spec, whole(patch_bias)] + kv_specs,
            [rows_spec(D)] * 3,
            stem_saved,
            [pltpu.VMEM((D, 2 * D), bf16)],
            23 * 10**9,
        )(features, bn, w_patch, patch_bias, *kv_inputs)
        return (*blank(text_saved), *done)

    qkv_rows, mix_rows, resid_one, q_a, q_b, patches, kv_lo, kv_hi = lax.cond(
        is_stem, first_stem, first_text
    )

    kv_moved = lax.ppermute(kv_hi, "section", [(0, 1)])

    def to_cores(block_a, block_b):
        return jnp.where(is_stem, lax.ppermute(block_a, "section", [(1, 0)]), block_b)

    q_here = to_cores(q_a, q_b)
    def cross(kv):
        return call(
            cross_forward,
            1,
            [whole(q_here), whole(kv)],
            [whole(q_here)],
            [slot_shape],
            [],
            8 * 10**9,
        )(q_here, kv)[0]

    mix_b = lax.cond(is_stem, lambda: cross(kv_lo), lambda: cross(kv_moved))

    mix_a = lax.ppermute(mix_b, "section", [(0, 1)])
    cot_a = lax.ppermute(cot_b, "section", [(0, 1)])
    grad_out = simple(
        join_cotangent,
        [arrival_row[None, :], own_row[None, :], cot_a, cot_b, cotangent],
        [shape((height, D), bf16)],
        [],
        4 * 10**9,
    )[0]

    chunks = 3
    wide = FF // chunks
    own_shape = shape((tokens, HALF), bf16)
    middle_shapes = [
        arrival_shape,
        arrival_shape,
        own_shape,
        own_shape,
        shape((height, D), f32),
        shape((D, 2 * (CH + FF)), bf16),
        slot_shape,
        slot_shape,
        shape((2, D), f32),
        shape((1, FF), f32),
    ]

    def middle_text():
        inputs = [
            mix_a, mix_b, take, pack, arrival_row[:, None], own_row[:, None],
            resid_one, grad_out, vecs_three,
        ]

        def chunk(step):
            return jnp.minimum(step, chunks - 1)

        if lines.by_hand:
            first_up = (CH + FF) // wide
            down_rows = D // (chunks + 1)
            down_spec = pl.BlockSpec((down_rows, CH + FF), lambda step: (1 + chunk(step), 0))
        else:
            first_up = 0
            down_rows = D
            down_spec = pl.BlockSpec((D, wide), lambda step: (0, 1 + chunk(step)))
        down_width = wide * D // down_rows
        outs = [whole(o) for o in middle_shapes]
        outs[5] = pl.BlockSpec(memory_space=pl.ANY)
        outs[9] = pl.BlockSpec((1, wide), lambda step: (0, chunk(step)))
        return call(
            text_middle,
            chunks + 1,
            [blocks_spec]
            + [whole(a) for a in inputs]
            + [pl.BlockSpec((1, wide), lambda step: (0, chunk(step)))]
            + halves(wide, first_up + chunks)
            + [
                pl.BlockSpec((HALF, wide), lambda step: (0, first_up + chunk(step))),
                pl.BlockSpec((HALF, wide), lambda step: (1, first_up + chunk(step))),
                down_spec,
            ],
            outs,
            middle_shapes,
            [
                pltpu.VMEM((D, D), bf16),
                pltpu.VMEM((D, wide), bf16),
                pltpu.VMEM((height, D), bf16),
                pltpu.VMEM((height, D), bf16),
                pltpu.VMEM((D, height), bf16),
                pltpu.VMEM((height, 1), f32),
                pltpu.VMEM((height, D), f32),
                pltpu.VMEM((height, D), f32),
                pltpu.VMEM((D, height), bf16),
                pltpu.VMEM((D, wide), f32),
                pltpu.VMEM((D, wide), f32),
                pltpu.VMEM((2, D, wide), bf16),
                pltpu.VMEM((2, down_rows, down_width), bf16),
                pltpu.VMEM((D, wide), bf16),
                pltpu.VMEM((height, D), bf16),
                pltpu.SemaphoreType.DMA((2, 2)),
            ],
            29 * 10**9,
        )(row_blocks, *inputs, up_bias, *[w_late] * 4, w_down)

    def middle_stem():
        made = list(blank(middle_shapes))
        made[5] = jnp.zeros(middle_shapes[5].shape, bf16)
        return tuple(made)

    (
        out_lo, out_hi, own_lo, own_hi, grad_two, late_term, g_a, g_b, grads_three, grad_up_bias,
    ) = lax.cond(is_stem, middle_stem, middle_text)
    if lines.by_hand:
        late_grad = lax.psum_scatter(late_term, BOTH, scatter_dimension=0, tiled=True)
    else:
        late_grad = lax.psum_scatter(
            late_term[:, : CH + FF], BOTH, scatter_dimension=0, tiled=True
        )
        down_turned = lax.psum_scatter(
            late_term[:, CH + FF :], BOTH, scatter_dimension=1, tiled=True
        )
    g_here = to_cores(g_a, g_b)
    out_here = to_cores(out_lo, out_hi)
    g_here, out_here = barrier((g_here, out_here))
    got_out = send(out_here.reshape(dp, capacity * LONGEST, HALF)).reshape(slots * LONGEST, HALF)

    def cross_back(kv):
        return tuple(
            call(
                cross_backward,
                1,
                [whole(q_here), whole(g_here), whole(kv)],
                [whole(q_here), whole(kv)],
                [slot_shape, rows_shape],
                [],
                0,
            )(q_here, g_here, kv)
        )

    grad_here, grad_kv = lax.cond(is_stem, lambda: cross_back(kv_lo), lambda: cross_back(kv_moved))
    grad_here, grad_kv, got_out = barrier((grad_here, grad_kv, got_out))
    grad_kv_moved = lax.ppermute(grad_kv, "section", [(1, 0)])

    stem_kv_shapes = [
        rows_shape,
        shape((HALF, 2 * D), bf16),
        shape((HALF, 2 * D), bf16),
        shape((1, D), f32),
    ]

    def stem_kv():
        return tuple(
            call(
                stem_backward_kv,
                blocks,
                kv_specs + [rows_spec(D)] * 3,
                [rows_spec(D)] + [at(o.shape, 0, 0) for o in stem_kv_shapes[1:]],
                stem_kv_shapes,
                [pltpu.VMEM((D, 2 * D), bf16), pltpu.VMEM((D, 2 * D), f32)],
                23 * 10**9,
            )(*kv_inputs, patches, grad_kv, grad_kv_moved)
        )

    grad_b = grad_here
    grad_rows, kv_w_lo, kv_w_hi, patch_bias_sum = lax.cond(
        is_stem, stem_kv, lambda: tuple(blank(stem_kv_shapes))
    )
    grad_a = lax.ppermute(grad_b, "section", [(0, 1)])
    grad_a, grad_rows = barrier((grad_a, grad_rows))

    row_shape = shape((half_room, D), bf16)
    text_last_shapes = [
        shape((height, D), bf16),
        row_shape,
        row_shape,
        shape((HALF, 5 * D), bf16),
        shape((HALF, 5 * D), bf16),
        shape((4, D), f32),
    ]
    half_channels = CH // 2
    stem_last_shapes = [
        shape((image_rows, half_channels), bf16),
        shape((image_rows, half_channels), bf16),
        shape((CH, D), bf16),
        shape((2, CH), f32),
    ]

    def last_text():
        inputs = [
            grad_a, grad_b, take, place[None, :], grad_two, resid_one, embed,
            qkv_rows, mix_rows, start, vecs_outer,
        ]
        done = call(
            text_last,
            1,
            [blocks_spec] + [whole(a) for a in inputs] + qkv_specs,
            [whole(o) for o in text_last_shapes],
            text_last_shapes,
            [
                pltpu.VMEM((height, D), bf16),
                pltpu.VMEM((height, D), bf16),
                pltpu.VMEM((height, 2 * D), f32),
                pltpu.VMEM((D, 3 * D), f32),
                pltpu.VMEM((height, D), f32),
            ],
            0,
        )(row_blocks, *inputs, *qkv_inputs)
        return (*done, *blank(stem_last_shapes))

    def last_stem():
        done = call(
            stem_backward,
            blocks,
            [rows_spec(CH), whole(bn), patch_spec, rows_spec(D)],
            [rows_spec(half_channels)] * 2 + [at(o.shape, 0, 0) for o in stem_last_shapes[2:]],
            stem_last_shapes,
            [pltpu.VMEM((CH, D), f32)],
            0,
        )(features, bn, w_patch, grad_rows)
        return (*blank(text_last_shapes), *done)

    (
        grad_embed, rows_low, rows_high, grad_w_lo, grad_w_hi, grads_outer,
        grad_lo, grad_hi, grad_patch_w, bn_sums,
    ) = lax.cond(is_stem, last_stem, last_text)

    gone = jnp.zeros((), f32)
    vector_term = jnp.concatenate(
        [
            jnp.where(is_stem, bn_sums.reshape(-1), gone),
            jnp.where(is_stem, patch_bias_sum.reshape(-1), gone),
            jnp.where(
                is_stem,
                gone,
                jnp.concatenate(
                    [
                        grads_outer.reshape(-1),
                        grads_three.reshape(-1),
                        grad_up_bias.reshape(-1),
                        jnp.sum(cotangent, axis=0),
                    ]
                ),
            ),
        ]
    ).reshape(-1, CH)

    def summed(vector, steps):
        for step in steps:
            vector = vector + lax.ppermute(vector, "dp", [(i, i ^ step) for i in range(dp)])
        return vector

    grad_w_lo, grad_w_hi, kv_w_lo, kv_w_hi = barrier(
        (grad_w_lo, grad_w_hi, kv_w_lo, kv_w_hi)
    )
    own_here = to_cores(own_lo, own_hi)

    def output(got_out):
        return simple(
            join_output,
            [slot_rows[None, :], got_out, own_here],
            [own_shape],
            [],
            3 * 10**9,
        )[0]

    if lines.by_hand:
        owners = CH // project_rows
        parts = grad_patch_w.reshape(owners, 2, project_rows // 2, D)
        terms = [
            (lax.ppermute(grad_w_lo, "section", [(1, 0)]), grad_w_hi),
            (kv_w_lo, lax.ppermute(kv_w_hi, "section", [(0, 1)])),
        ]
        terms = [
            tuple(w.reshape(4, 2, 2, HALF // dp, w.shape[1]) for w in term) for term in terms
        ]
        patch = (parts[:, 0], lax.ppermute(parts[:, 1], "section", [(0, 1)]))
        patch = [tuple(w.reshape(2, 2, 2, project_rows // 2, D) for w in patch)]
        terms, patch = barrier((terms, patch))
        first = lines.first_half(terms, 1)
        first, rows_low, vector_term = barrier((first, rows_low, vector_term))
        got = lines.across(first, 2, 1)
        patch_got = lines.sum_first(patch)
        vector_term = summed(vector_term, (4, 8))
        sent_rows = to_cores(rows_low, rows_high).reshape(dp, room, D)
        got_rows = send(sent_rows)
        got, patch_got, got_rows, vector_term = barrier((got, patch_got, got_rows, vector_term))
        got_two = lines.sum_second(terms, got)
        patch_got_two = lines.sum_second(patch, patch_got)
        got_two, patch_got_two, got_rows, vector_term, grad_hi, got_out, late_grad = barrier(
            (got_two, patch_got_two, got_rows, vector_term, grad_hi, got_out, late_grad)
        )
        line = lines.line_of(terms, got, got_two)
        line_parts = lines.sum_line(line)
        patch_line = lines.line_of(patch, patch_got, patch_got_two)
        patch_got = lines.sum_low_first(patch_line)
        vector_total = summed(vector_term, (1, 2))
        block_piece = output(got_out)
        got_hi = lax.ppermute(grad_hi, "section", [(0, 1)])
        tail_grad = lines.line_total(line, line_parts)
        patch_low = lines.sum_low_last(patch_line, patch_got)
        patch_high = lax.ppermute(patch_low, "section", [(1, 0)])
        down_grad = late_grad[:, CH + FF :].astype(f32).reshape(late_grad.shape[0], -1, 128)
        down_grad = down_grad.transpose(1, 0, 2).reshape(D, 128).T
        project_grad = down_grad + jnp.where(
            is_stem & (dp_index < owners), jnp.concatenate([patch_low, patch_high]), 0.0
        )
    else:
        vector_total = summed(vector_term, [1 << bit for bit in range(dp.bit_length() - 1)])
        got_rows = send(to_cores(rows_low, rows_high).reshape(dp, room, D))
        block_piece = output(got_out)
        got_hi = lax.ppermute(grad_hi, "section", [(0, 1)])
        tail_grad, patch_grad = lines.scatter_plain(
            grad_w_lo, grad_w_hi, kv_w_lo, kv_w_hi, grad_patch_w
        )
        project_grad = down_turned.astype(f32).T + patch_grad
    late_grad = late_grad.astype(f32)
    block_grad = jnp.concatenate(
        [tail_grad, late_grad[:, FF : FF + D], late_grad[:, :FF]], axis=1
    )
    vector_total = vector_total + lax.ppermute(vector_total, "section", [(0, 1), (1, 0)])
    vector_grad = lax.dynamic_slice_in_dim(
        vector_total.reshape(-1), me * vector_master.shape[0], vector_master.shape[0]
    )

    own_pre = jnp.where(is_stem, grad_lo, got_hi).astype(f32)
    first_channel = section * half_channels

    def own_half(array):
        return lax.dynamic_slice_in_dim(array, first_channel, half_channels, axis=array.ndim - 1)

    own_normed = (own_half(features).astype(f32) - own_half(center)) * own_half(factor)
    own_gain = own_half(bn_gain)
    feature_grad = own_half(factor) * (
        own_pre * own_gain
        - own_gain * own_half(vector_total[1]) / every_patch
        - own_normed * (own_gain * own_half(vector_total[0]) / every_patch)
    )

    def row_sums(asked, rows):
        hit = (jnp.arange(table_rows, dtype=i32)[:, None] == asked[None, :]).astype(bf16)
        return mm(hit, rows.reshape(half_room, D))

    def table_more(turn, total):
        place, asked = round_of(turn)
        slot = jnp.arange(group * room, dtype=i32)
        rows = mm((slot[:, None] == place[None, :]).astype(bf16), grad_embed).astype(bf16)
        moved = lax.ppermute(rows[:half_room], "section", [(1, 0)])
        rows = jnp.where(is_stem, moved, rows[half_room:]).reshape(dp, room, D)
        return total + row_sums(send(asked).reshape(half_room), send(rows))

    root_tokens = math.sqrt(tokens * dp)

    def table_update(total):
        return sgd_update(total, table_momentum, table_master, table_average, 0.05)

    table_new = lax.cond(
        rounds > 1,
        lambda: table_update(lax.fori_loop(1, rounds, table_more, row_sums(asked, got_rows))),
        lambda: table_update(row_sums(asked, got_rows)),
    )
    block_new = sgd_update(
        block_grad, block_momentum, block_master, block_average, 0.5 * D ** (-0.5) / root_tokens
    )
    project_new = sgd_update(
        project_grad,
        project_momentum,
        project_master,
        project_average,
        0.5 * FF ** (-0.5) / root_tokens,
    )
    vector_new = sgd_update(
        vector_grad, vector_momentum, vector_master, vector_average, 0.1 / root_tokens
    )
    return (block_piece, feature_grad, *table_new, *block_new, *project_new, *vector_new)


def solution(mesh):
    rows = P(BOTH, None)
    flat = P(BOTH)
    placed = (
        (P("dp", None), P(), P("dp"), P("dp", None), P("dp", None))
        + (rows,) * 9
        + (flat,) * 3
    )
    return jax.shard_map(
        per_device,
        mesh=mesh,
        in_specs=placed,
        out_specs=(P("dp", "section"), P("dp", "section")) + (rows,) * 15 + (flat,) * 5,
        check_vma=False,
    )
```

```python
import functools
import math

import jax
import jax.numpy as jnp
from jax import lax
from jax.experimental import pallas as pl
from jax.experimental.pallas import tpu as pltpu
from jax.sharding import PartitionSpec as P

D = 768
HEADS = 12
HEAD_DIM = 64
QUAD = 4 * HEAD_DIM
QUADS = HEADS // 4
FF = 3072
CH = 1024
PATCH = 196
WINDOW = 208
IMG_DEV = 16
GROUPS_DEV = 32
LONGEST = 32
HALF = D // 2
ROWS = 256
BLOCK = 128
SPAN = BLOCK + LONGEST
SCALE = HEAD_DIM ** (-0.5)
EPS = 1e-05
NEG = -1e30
BOTH = ("section", "dp")
VMEM_BYTES = 58 * 1024 * 1024
bf16 = jnp.bfloat16
f32 = jnp.float32
i32 = jnp.int32


def mm(left, right):
    return jnp.dot(left, right, preferred_element_type=f32)


def mm_rt(left, right):
    return lax.dot_general(left, right, (((1,), (1,)), ((), ())), preferred_element_type=f32)


def mm_lt(left, right):
    return lax.dot_general(left, right, (((0,), (0,)), ((), ())), preferred_element_type=f32)


def normalise(values):
    shifted = values - jnp.mean(values, axis=-1, keepdims=True)
    factor = lax.rsqrt(jnp.mean(shifted * shifted, axis=-1, keepdims=True) + EPS)
    return shifted * factor, factor


def norm_back(incoming, unit, factor, gain):
    scaled = incoming * gain
    mean_grad = jnp.mean(scaled, axis=-1, keepdims=True)
    mean_cross = jnp.mean(scaled * unit, axis=-1, keepdims=True)
    return factor * (scaled - mean_grad - unit * mean_cross)


GELU_C = math.sqrt(2.0 / math.pi)


def gelu_parts(values):
    square = values * values
    bend = jnp.tanh(GELU_C * values * (1.0 + 0.044715 * square))
    half = 0.5 * (1.0 + bend)
    slope = half + 0.5 * values * (1.0 - bend * bend) * (GELU_C * (1.0 + 3 * 0.044715 * square))
    return values * half, slope


def gelu_only(values):
    bend = jnp.tanh(GELU_C * values * (1.0 + 0.044715 * (values * values)))
    return 0.5 * values * (1.0 + bend)


def head_masks(dtype, width=QUAD):
    lanes = lax.broadcasted_iota(i32, (1, width), 1) // HEAD_DIM
    return [jnp.where(lanes == h, 1.0, 0.0).astype(dtype) for h in range(width // HEAD_DIM)]


def spread_heads(rows, masks):
    return jnp.concatenate([rows * m for m in masks], axis=0)


def join_heads(stacked, masks):
    count = stacked.shape[0] // len(masks)
    total = stacked[:count] * masks[0]
    for h in range(1, len(masks)):
        total = total + stacked[h * count : (h + 1) * count] * masks[h]
    return total


def softmax(scores, allowed):
    scores = jnp.where(allowed, scores * SCALE, NEG)
    weights = jnp.exp(scores - jnp.max(scores, axis=-1, keepdims=True))
    return weights * (1.0 / jnp.sum(weights, axis=-1, keepdims=True))


def one_hot_cols(index_col, width):
    places = lax.broadcasted_iota(i32, (index_col.shape[0], width), 1)
    return jnp.where(places == index_col, 1.0, 0.0).astype(bf16)


def one_hot_rows(index_row, height, offset=0):
    places = lax.broadcasted_iota(i32, (height, index_row.shape[1]), 0) + offset
    return jnp.where(places == index_row, 1.0, 0.0).astype(bf16)


def join_halves(target, low_ref, high_ref):
    count = low_ref.shape[0]
    target[:count, :] = low_ref[...]
    target[count : 2 * count, :] = high_ref[...]


def key_span(first):
    return pl.multiple_of(jnp.maximum(first - LONGEST, 0), LONGEST)


def self_allowed(start_rows, first, key_first):
    rows = lax.broadcasted_iota(i32, (BLOCK, SPAN), 0) + first
    keys = lax.broadcasted_iota(i32, (BLOCK, SPAN), 1) + key_first
    allowed = (keys <= rows) & (keys >= start_rows)
    return jnp.concatenate([jnp.where(allowed, 1, 0)] * 4, axis=0) > 0


def chunks_of(count, size, body):
    def step(index, carry):
        body(pl.multiple_of(index * size, size))
        return carry

    lax.fori_loop(0, count, step, 0)


def text_first(
    blocks, embed, start, pack, vecs,
    qkv_lo, qkv_hi, out_lo, out_hi, cq_lo, cq_hi,
    qkv_rows, mix_rows, resid_one, slots_a, slots_b,
    w_qkv, w_out, w_cq, queries,
):
    count = blocks[0]
    join_halves(w_qkv, qkv_lo, qkv_hi)
    join_halves(w_out, out_lo, out_hi)
    join_halves(w_cq, cq_lo, cq_hi)
    queries[...] = jnp.zeros_like(queries)
    masks = head_masks(bf16)
    masks_f = head_masks(f32)

    def project(first):
        rows = pl.ds(first, ROWS)
        unit, _ = normalise(embed[rows, :].astype(f32))
        normed = (unit * vecs[0:1, :] + vecs[1:2, :]).astype(bf16)
        for third in range(3):
            columns = slice(third * D, (third + 1) * D)
            qkv_rows[rows, columns] = mm(normed, w_qkv[:, columns]).astype(bf16)

    def attend(first):
        rows = pl.ds(first, BLOCK)
        key_first = key_span(first)
        span = pl.ds(key_first, SPAN)
        allowed = self_allowed(start[rows, :], first, key_first)
        for quad in range(QUADS):
            lanes, keys, values = quad_lanes(quad)
            query = spread_heads(qkv_rows[rows, lanes], masks)
            shares = softmax(mm_rt(query, qkv_rows[span, keys]), allowed)
            mixed = mm(shares.astype(bf16), qkv_rows[span, values])
            mix_rows[rows, lanes] = join_heads(mixed, masks_f).astype(bf16)

    def finish(first):
        rows = pl.ds(first, ROWS)
        resid = embed[rows, :].astype(f32) + mm(mix_rows[rows, :], w_out[...])
        resid_one[rows, :] = resid
        unit, _ = normalise(resid)
        normed = (unit * vecs[2:3, :] + vecs[3:4, :]).astype(bf16)
        queries[rows, :] = mm(normed, w_cq[...]).astype(bf16)

    chunks_of(count, ROWS, project)
    chunks_of(count * (ROWS // BLOCK), BLOCK, attend)
    chunks_of(count, ROWS, finish)
    packed = mm(one_hot_cols(pack[...], queries.shape[0]), queries[...]).astype(bf16)
    slots_a[...] = packed[:, :HALF]
    slots_b[...] = packed[:, HALF:]


def quad_lanes(quad):
    return [slice(part * D + quad * QUAD, part * D + (quad + 1) * QUAD) for part in range(3)]


def text_middle(
    blocks, mix_a, mix_b, take, pack, arrival, own, resid_one, cotangent, vecs, up_bias,
    cout_lo, cout_hi, up_lo, up_hi, down_part,
    out_lo, out_hi, own_lo, own_hi, grad_two, late, slots_a, slots_b,
    vec_grad, up_bias_grad,
    w_cout, w_up, mixed, normed, normed_t, factor_s, total, back, grad_down_t,
    up_sum, down_sum, up_buffer, down_buffer, w_down_t, block_out, sems,
):
    step = pl.program_id(0)
    last = pl.num_programs(0) - 1
    count = blocks[0]
    wide = w_up.shape[1]
    by_owner = down_buffer.shape[1] != D

    def copies(chunk):
        slot = chunk % 2
        place = (chunk + 1) % 4
        columns = slice(chunk * wide, (chunk + 1) * wide)
        pairs = [(up_buffer.at[slot], late.at[:, columns])]
        if by_owner:
            height = down_buffer.shape[1]
            rows = slice(place * height, (place + 1) * height)
            pairs.append((down_buffer.at[slot], late.at[rows, CH + FF :]))
        else:
            columns = slice(CH + FF + place * wide, CH + FF + (place + 1) * wide)
            pairs.append((down_buffer.at[slot], late.at[:, columns]))
        return [
            pltpu.make_async_copy(source, target, sems.at[slot, i])
            for i, (source, target) in enumerate(pairs)
        ]

    for chunk in (0, 1):

        @pl.when(step == chunk + 2)
        def _():
            for copy in copies(chunk):
                copy.wait()

    @pl.when(step == 0)
    def _():
        w_cout[:HALF, :] = cout_lo[:, :D]
        w_cout[HALF:, :] = cout_hi[:, :D]
        normed[...] = jnp.zeros_like(normed)
        block_out[...] = jnp.zeros_like(block_out)
        vec_grad[...] = jnp.zeros_like(vec_grad)

        def begin(first):
            rows = pl.ds(first, ROWS)
            places = lax.broadcasted_iota(i32, (ROWS, take.shape[1]), 0) + first
            hit = jnp.where(places == take[...], 1.0, 0.0).astype(bf16)
            mixed[rows, :HALF] = mm(hit, mix_a[...]).astype(bf16)
            mixed[rows, HALF:] = mm(hit, mix_b[...]).astype(bf16)
            resid_two = resid_one[rows, :] + mm(mixed[rows, :], w_cout[...])
            unit, factor = normalise(resid_two)
            grad_two[rows, :] = unit
            factor_s[rows, :] = factor
            low = (unit * vecs[0:1, :] + vecs[1:2, :]).astype(bf16)
            normed[rows, :] = low
            normed_t[:, rows] = low.T
            total[rows, :] = resid_two + vecs[2:3, :]
            back[rows, :] = jnp.zeros((ROWS, D), f32)
            grad_down_t[:, rows] = cotangent[rows, :].T

        chunks_of(count, ROWS, begin)

    @pl.when(step < last)
    def _():
        join_halves(w_up, up_lo, up_hi)
        parts = wide // 128
        if by_owner:
            height = down_buffer.shape[1] // parts
            for i in range(0, parts, 2):
                pair = down_part[i * height : (i + 2) * height, :].astype(f32)
                for h in range(2):
                    one = pair[h * height : (h + 1) * height]
                    one = jnp.concatenate([one[:, j : j + 128] for j in range(0, CH + FF, 128)], axis=0)
                    w_down_t[:, (i + h) * 128 : (i + h + 1) * 128] = one.astype(bf16)
        else:
            w_down_t[...] = down_part[...]
        up_sum[...] = jnp.zeros_like(up_sum)
        down_sum[...] = jnp.zeros_like(down_sum)
        up_bias_grad[...] = jnp.zeros_like(up_bias_grad)

        def forward_back(first):
            rows = pl.ds(first, ROWS)
            act, slope = gelu_parts(mm(normed[rows, :], w_up[...]) + up_bias[...])
            act = act.astype(bf16)
            total[rows, :] += mm_rt(act, w_down_t[...])
            grad_up = (mm(cotangent[rows, :], w_down_t[...]) * slope).astype(bf16)
            up_bias_grad[...] += jnp.sum(grad_up.astype(f32), axis=0, keepdims=True)
            up_sum[...] += mm(normed_t[:, rows], grad_up)
            down_sum[...] += mm(grad_down_t[:, rows], act)
            back[rows, :] += mm_rt(grad_up, w_up[...])

        chunks_of(count, ROWS, forward_back)
        slot = step % 2
        up_buffer[slot] = up_sum[...].astype(bf16)
        if by_owner:
            pieces = [
                jnp.concatenate(
                    [down_sum[j : j + height, first : first + 128] for j in range(0, D, height)],
                    axis=1,
                )
                for first in range(0, wide, 128)
            ]
            for i in range(0, parts, 2):
                pair = jnp.concatenate(pieces[i : i + 2], axis=0).astype(bf16)
                down_buffer[slot, i * height : (i + 2) * height, :] = pair
        else:
            down_buffer[slot] = down_sum[...].astype(bf16)

    for chunk in range(3):

        @pl.when(step == chunk)
        def _():
            for copy in copies(chunk):
                copy.start()

    @pl.when(step == last)
    def _():
        up_sum[:, :D] = jnp.zeros((D, D), f32)

        def end(first):
            rows = pl.ds(first, ROWS)
            block_out[rows, :] = total[rows, :].astype(bf16)
            incoming, unit = back[rows, :], grad_two[rows, :]
            vec_grad[0:1, :] += jnp.sum(incoming * unit, axis=0, keepdims=True)
            vec_grad[1:2, :] += jnp.sum(incoming, axis=0, keepdims=True)
            grad = norm_back(incoming, unit, factor_s[rows, :], vecs[0:1, :])
            grad = cotangent[rows, :].astype(f32) + grad
            grad_two[rows, :] = grad
            grad = grad.astype(bf16)
            up_sum[:, :D] += mm_lt(mixed[rows, :], grad)
            normed[rows, :] = mm_rt(grad, w_cout[...]).astype(bf16)

        chunks_of(count, ROWS, end)
        slot = step % 2
        up_buffer[slot, :, :D] = up_sum[:, :D].astype(bf16)
        up_buffer[slot, :, D:] = jnp.zeros((D, wide - D), bf16)
        down_buffer[slot] = jnp.zeros(down_buffer.shape[1:], bf16)
        for copy in copies(3):
            copy.start()
        for index, rows, lo, hi in (
            (pack, normed, slots_a, slots_b),
            (arrival, block_out, out_lo, out_hi),
            (own, block_out, own_lo, own_hi),
        ):
            for at_row in range(0, index.shape[0], 512):
                some = slice(at_row, at_row + 512)
                packed = mm(one_hot_cols(index[some, :], rows.shape[0]), rows[...]).astype(bf16)
                lo[some, :] = packed[:, :HALF]
                hi[some, :] = packed[:, HALF:]
        for chunk in (2, 3):
            for copy in copies(chunk):
                copy.wait()


def text_last(
    blocks, grad_a, grad_b, take, place, grad_two, resid_one, embed, qkv_rows, mix_rows, start, vecs,
    qkv_lo, qkv_hi, out_lo, out_hi, cq_lo, cq_hi,
    grad_embed, rows_a, rows_b, grad_lo, grad_hi, vec_grad,
    grad_mix, grad_queries, total, sums, grad_one,
):
    count = blocks[0]

    def keep(first, value):
        low = value.astype(bf16)
        width = value.shape[1]
        grad_lo[:, first : first + width] = low[:HALF]
        grad_hi[:, first : first + width] = low[HALF:]

    def turned_back(rows, lo, hi):
        return jnp.concatenate([mm_rt(rows, lo[...]), mm_rt(rows, hi[...])], axis=1)

    masks = head_masks(bf16)
    masks_f = head_masks(f32)
    vec_grad[...] = jnp.zeros_like(vec_grad)
    total[...] = jnp.zeros_like(total)
    sums[...] = jnp.zeros_like(sums)
    grad_embed[...] = jnp.zeros_like(grad_embed)

    def begin(first):
        rows = pl.ds(first, ROWS)
        places = lax.broadcasted_iota(i32, (ROWS, take.shape[1]), 0) + first
        hit = jnp.where(places == take[...], 1.0, 0.0).astype(bf16)
        grad_q = jnp.concatenate([mm(hit, grad_a[...]), mm(hit, grad_b[...])], axis=1).astype(bf16)
        unit, factor = normalise(resid_one[rows, :])
        normed = (unit * vecs[2:3, :] + vecs[3:4, :]).astype(bf16)
        sums[:, :D] += mm_lt(normed, grad_q)
        incoming = turned_back(grad_q, cq_lo, cq_hi)
        vec_grad[2:3, :] += jnp.sum(incoming * unit, axis=0, keepdims=True)
        vec_grad[3:4, :] += jnp.sum(incoming, axis=0, keepdims=True)
        grad = grad_two[rows, :] + norm_back(incoming, unit, factor, vecs[2:3, :])
        grad_one[rows, :] = grad
        grad = grad.astype(bf16)
        sums[:, D : 2 * D] += mm_lt(mix_rows[rows, :], grad)
        grad_mix[rows, :] = turned_back(grad, out_lo, out_hi).astype(bf16)

    def attend(first):
        rows = pl.ds(first, BLOCK)
        key_first = key_span(first)
        span = pl.ds(key_first, SPAN)
        allowed = self_allowed(start[rows, :], first, key_first)
        for quad in range(QUADS):
            lanes, keys, values = quad_lanes(quad)
            query = spread_heads(qkv_rows[rows, lanes], masks)
            grad = spread_heads(grad_mix[rows, lanes], masks)
            key_rows = qkv_rows[span, keys]
            shares = softmax(mm_rt(query, key_rows), allowed)
            grad_shares = mm_rt(grad, qkv_rows[span, values])
            inner = jnp.sum(grad_shares * shares, axis=-1, keepdims=True)
            grad_scores = (shares * (grad_shares - inner)).astype(bf16)
            back = join_heads(mm(grad_scores, key_rows), masks_f) * SCALE
            grad_queries[rows, lanes] = back.astype(bf16)
            later = slice(D + quad * QUAD, D + (quad + 1) * QUAD)
            total[span, lanes] += mm_lt(grad_scores, query) * SCALE
            total[span, later] += mm_lt(shares.astype(bf16), grad)

    def end(first):
        rows = pl.ds(first, ROWS)
        unit, factor = normalise(embed[rows, :].astype(f32))
        normed = (unit * vecs[0:1, :] + vecs[1:2, :]).astype(bf16)
        grad = jnp.concatenate([grad_queries[rows, :], total[rows, :].astype(bf16)], axis=1)
        for third in range(3):
            columns = slice(third * D, (third + 1) * D)
            sums[:, columns] += mm_lt(normed, grad[:, columns])
        incoming = turned_back(grad, qkv_lo, qkv_hi)
        vec_grad[0:1, :] += jnp.sum(incoming * unit, axis=0, keepdims=True)
        vec_grad[1:2, :] += jnp.sum(incoming, axis=0, keepdims=True)
        grad = grad_one[rows, :] + norm_back(incoming, unit, factor, vecs[0:1, :])
        grad_embed[rows, :] = grad.astype(bf16)

    chunks_of(count, ROWS, begin)
    keep(4 * D, sums[:, :D])
    keep(3 * D, sums[:, D : 2 * D])
    chunks_of(count * (ROWS // BLOCK), BLOCK, attend)
    sums[...] = jnp.zeros_like(sums)
    chunks_of(count, ROWS, end)
    keep(0, sums[...])
    half = rows_a.shape[0]
    rows_a[...] = mm(one_hot_rows(place[...], half), grad_embed[...]).astype(bf16)
    rows_b[...] = mm(one_hot_rows(place[...], half, half), grad_embed[...]).astype(bf16)


def unpack_rows(rows_a, rows_b, place, embed):
    count = rows_a.shape[0]
    total = mm(one_hot_cols(place[...], count), rows_a[...])
    total = total + mm(one_hot_cols(place[...] - count, count), rows_b[...])
    embed[...] = total.astype(bf16)


def pack_half(index, rows, packed):
    packed[...] = mm(one_hot_cols(index[...], rows.shape[0]), rows[...].astype(bf16)).astype(bf16)


def join_cotangent(arrival, own, slots_a, slots_b, rows, joined):
    height = joined.shape[0]
    low = mm(one_hot_rows(own[...], height), rows[...].astype(bf16))
    hit = one_hot_rows(arrival[...], height)
    joined[:, :HALF] = (low[:, :HALF] + mm(hit, slots_a[...])).astype(bf16)
    joined[:, HALF:] = (low[:, HALF:] + mm(hit, slots_b[...])).astype(bf16)


def join_output(slot_rows, slots, own, joined):
    total = mm(one_hot_rows(slot_rows[...], joined.shape[0]), slots[...])
    joined[...] = (total + own[...].astype(f32)).astype(bf16)


def join_kv(w_kv, k_lo, k_hi, v_lo, v_hi):
    for first, (lo, hi) in enumerate(((k_lo, k_hi), (v_lo, v_hi))):
        for part in range(2):
            columns = slice((2 * part + first) * HALF, (2 * part + first + 1) * HALF)
            w_kv[:HALF, columns] = lo[:, part * HALF : (part + 1) * HALF]
            w_kv[HALF:, columns] = hi[:, part * HALF : (part + 1) * HALF]


def stem_forward(
    features, bn, w_patch, patch_bias, k_lo, k_hi, v_lo, v_hi, patches, kv_lo, kv_hi, w_kv
):
    @pl.when(pl.program_id(0) == 0)
    def _():
        join_kv(w_kv, k_lo, k_hi, v_lo, v_hi)

    normed = (features[...].astype(f32) - bn[0:1, :]) * bn[1:2, :]
    hidden = gelu_only(normed * bn[2:3, :] + bn[3:4, :]).astype(bf16)
    rows = (mm(hidden, w_patch[...]) + patch_bias[...]).astype(bf16)
    patches[...] = rows
    kv_lo[...] = mm(rows, w_kv[:, :D]).astype(bf16)
    kv_hi[...] = mm(rows, w_kv[:, D:]).astype(bf16)


def image_window(image):
    first = image * PATCH
    aligned = pl.multiple_of(first // 16 * 16, 16)
    lanes = lax.broadcasted_iota(i32, (1, WINDOW), 1) + (aligned - first)
    return aligned, (lanes >= 0) & (lanes < PATCH)


def cross_forward(queries, kv, mixed):
    masks = head_masks(bf16, HALF)
    masks_f = head_masks(f32, HALF)

    def image(index, carry):
        aligned, allowed = image_window(index)
        window = pl.ds(aligned, WINDOW)
        place = pl.ds(pl.multiple_of(index * LONGEST, LONGEST), LONGEST)
        scores = mm_rt(spread_heads(queries[place, :], masks), kv[window, :HALF])
        shares = softmax(scores, allowed).astype(bf16)
        mixed[place, :] = join_heads(mm(shares, kv[window, HALF:]), masks_f).astype(bf16)
        return carry

    lax.fori_loop(0, IMG_DEV, image, 0, unroll=4)


def cross_backward(queries, grads, kv, grad_q, grad_kv):
    grad_kv[...] = jnp.zeros_like(grad_kv)
    masks = head_masks(bf16, HALF)
    masks_f = head_masks(f32, HALF)

    def image(index, carry):
        aligned, allowed = image_window(index)
        window = pl.ds(aligned, WINDOW)
        place = pl.ds(pl.multiple_of(index * LONGEST, LONGEST), LONGEST)
        query = spread_heads(queries[place, :], masks)
        grad = spread_heads(grads[place, :], masks)
        keys = kv[window, :HALF]
        shares = softmax(mm_rt(query, keys), allowed)
        grad_shares = mm_rt(grad, kv[window, HALF:])
        inner = jnp.sum(grad_shares * shares, axis=-1, keepdims=True)
        grad_scores = (shares * (grad_shares - inner)).astype(bf16)
        grad_q[place, :] = (join_heads(mm(grad_scores, keys), masks_f) * SCALE).astype(bf16)
        grad_kv[window, :HALF] += (mm_lt(grad_scores, query) * SCALE).astype(bf16)
        grad_kv[window, HALF:] += mm_lt(shares.astype(bf16), grad).astype(bf16)
        return carry

    lax.fori_loop(0, IMG_DEV, image, 0, unroll=4)


def stem_backward_kv(
    k_lo, k_hi, v_lo, v_hi, patches, grad_kv_lo, grad_kv_hi,
    grad_rows, grad_lo, grad_hi, bias_sum,
    w_kv, total,
):
    step = pl.program_id(0)

    @pl.when(step == 0)
    def _():
        join_kv(w_kv, k_lo, k_hi, v_lo, v_hi)
        total[...] = jnp.zeros_like(total)
        bias_sum[...] = jnp.zeros_like(bias_sum)

    rows = mm_rt(grad_kv_lo[...], w_kv[:, :D]) + mm_rt(grad_kv_hi[...], w_kv[:, D:])
    rows = rows.astype(bf16)
    grad_rows[...] = rows
    bias_sum[...] += jnp.sum(rows.astype(f32), axis=0, keepdims=True)
    turned = patches[...].T
    total[:, :D] += mm(turned, grad_kv_lo[...])
    total[:, D:] += mm(turned, grad_kv_hi[...])

    @pl.when(step == pl.num_programs(0) - 1)
    def _():
        for first in range(2):
            for part in range(2):
                source = slice((2 * part + first) * HALF, (2 * part + first + 1) * HALF)
                target = slice((2 * first + part) * HALF, (2 * first + part + 1) * HALF)
                grad_lo[:, target] = total[:HALF, source].astype(bf16)
                grad_hi[:, target] = total[HALF:, source].astype(bf16)


def stem_backward(
    features, bn, w_patch, grad_rows, grad_lo, grad_hi, grad_patch_w, sums, patch_acc
):
    step = pl.program_id(0)

    @pl.when(step == 0)
    def _():
        patch_acc[...] = jnp.zeros_like(patch_acc)
        sums[...] = jnp.zeros_like(sums)

    normed = (features[...].astype(f32) - bn[0:1, :]) * bn[1:2, :]
    hidden, slope = gelu_parts(normed * bn[2:3, :] + bn[3:4, :])
    patch_acc[...] += mm_lt(hidden.astype(bf16), grad_rows[...])
    grad_pre = mm_rt(grad_rows[...], w_patch[...]) * slope
    sums[0:1, :] += jnp.sum(grad_pre * normed, axis=0, keepdims=True)
    sums[1:2, :] += jnp.sum(grad_pre, axis=0, keepdims=True)
    grad_low = grad_pre.astype(bf16)
    grad_lo[...] = grad_low[:, : CH // 2]
    grad_hi[...] = grad_low[:, CH // 2 :]

    @pl.when(step == pl.num_programs(0) - 1)
    def _():
        grad_patch_w[...] = patch_acc[...].astype(bf16)


def place_pieces(where_, two, four, two_other, four_other, first, second, *scratch, split):
    dp_index, section = where_[0], where_[1]
    width, all_width = first.shape[-1], two.shape[-1]
    cuts = (slice(0, width), slice(width, all_width))
    sems = scratch[-1]

    def pieces(part, jobs):
        copies = []
        for core, sources in ((1 - part, (two_other, four_other)), (part, (two, four))):
            for z in range(4):
                for far, turn, bits in ((0, 0, 0), (0, 1, 1 + core), (1, 0, 2 - core), (1, 1, 3)):
                    target = dp_index ^ (4 * z) ^ bits
                    for cut, place in jobs:
                        copies.append(
                            pltpu.make_async_copy(
                                sources[far].at[turn, z, :, cut],
                                place.at[core, target],
                                sems.at[len(copies)],
                            )
                        )
        for copy in copies:
            copy.start()
        for copy in copies:
            copy.wait()

    for part in range(2):

        @pl.when(section == part)
        def _():
            if split:
                out = (second, first)[part]
                buffer = (scratch[1], scratch[0])[part]
                pieces(part, [(cuts[1 - part], buffer)])
                final = pltpu.make_async_copy(buffer, out, sems.at[0])
                final.start()
                final.wait()
            else:
                pieces(part, [(cuts[0], first), (cuts[1], second)])


def shape(dims, dtype):
    return jax.ShapeDtypeStruct(dims, dtype)


def whole(array):
    zeros = (0,) * len(array.shape)
    return pl.BlockSpec(array.shape, lambda *_: zeros, pipeline_mode=pl.Buffered(1))


def at(dims, *index):
    return pl.BlockSpec(dims, lambda *_: index)


def call(kernel, steps, in_specs, out_specs, outs, scratch, flops):
    return pl.pallas_call(
        kernel,
        grid=(steps,),
        in_specs=in_specs,
        out_specs=out_specs,
        out_shape=outs,
        scratch_shapes=scratch,
        compiler_params=pltpu.CompilerParams(vmem_limit_bytes=VMEM_BYTES),
        cost_estimate=pl.CostEstimate(flops=flops, bytes_accessed=0, transcendentals=0),
    )


def simple(kernel, inputs, outs, scratch, flops):
    return call(
        kernel,
        1,
        [whole(a) for a in inputs],
        [at(o.shape, *(0,) * len(o.shape)) for o in outs],
        outs,
        scratch,
        flops,
    )(*inputs)


def blank(outs):
    return pl.pallas_call(
        lambda *refs: None,
        out_shape=outs,
        out_specs=[pl.BlockSpec(memory_space=pl.ANY) for _ in outs],
    )()


barrier = lax.optimization_barrier


class Lines:
    def __init__(self, dp, dp_index, section):
        self.dp, self.dp_index, self.section = dp, dp_index, section
        self.is_stem = section == 0
        self.by_hand = dp == 16
        self.x, self.y, self.z = dp_index & 1, dp_index // 2 & 1, dp_index // 4

    def across(self, array, low, high):
        count = self.dp
        pairs = [(d, d ^ low) for d in range(count)]
        pairs += [(count + d, count + (d ^ high)) for d in range(count)]
        return lax.ppermute(array, BOTH, pairs)

    def swap(self, array):
        return lax.ppermute(array, "section", [(0, 1), (1, 0)])

    def gather_line(self, shard):
        return jnp.stack([shard] + [self.across(shard, 4 * k, 4 * k) for k in (1, 2, 3)])

    def gather_first(self, line):
        return jnp.stack([line, self.across(line, 1, 2)])

    def gather_second(self, two):
        return two, self.across(two, 2, 1)

    def gather_place(self, two, four, text_width):
        inputs = [two, four, self.swap(two), self.swap(four)]
        split = text_width is not None
        any_spec = pl.BlockSpec(memory_space=pl.ANY)
        rows, width = two.shape[2:]
        count = 2 * self.dp
        first = text_width if split else CH
        shapes = [(2, self.dp, rows, w) for w in (first, width - first)]
        buffers = [pltpu.VMEM(dims, bf16) for dims in shapes] if split else []
        out_spec = any_spec if split else pl.BlockSpec(memory_space=pltpu.VMEM)
        placed = pl.pallas_call(
            functools.partial(place_pieces, split=split),
            in_specs=[pl.BlockSpec(memory_space=pltpu.SMEM)] + [any_spec] * 4,
            out_specs=[out_spec] * 2,
            out_shape=[shape(dims, bf16) for dims in shapes],
            scratch_shapes=buffers + [pltpu.SemaphoreType.DMA((2 * count,))],
            compiler_params=pltpu.CompilerParams(vmem_limit_bytes=VMEM_BYTES),
        )(jnp.stack([self.dp_index, self.section]), *inputs)
        return [p.reshape(count * rows, p.shape[-1]) for p in placed]

    def fold_small(self, stats, vector, rows):
        first = lax.reduce_precision(stats, 8, 7)
        second = lax.reduce_precision(stats - first, 8, 7)
        third = stats - first - second
        terms = jnp.stack([first, second, third]).astype(bf16).reshape(rows, -1)
        count = rows * 128 - vector.shape[0]
        vector = jnp.concatenate([vector.astype(bf16), jnp.zeros((count,), bf16)])
        return jnp.concatenate([terms, vector.reshape(rows, 128)], axis=1)

    def unfold_small(self, shared, count, each):
        shared = shared.reshape(2, self.dp, -1, shared.shape[-1])
        stats = shared[0, :, :, :-128].astype(f32).reshape(self.dp, 3, 2, CH)
        stats = stats[:, 0] + stats[:, 1] + stats[:, 2]
        center = jnp.mean(stats[:, 0], axis=0)
        squares = jnp.sum(stats[:, 1] + each * jnp.square(stats[:, 0] - center), axis=0)
        lines = (count + 127) // 128
        vector = shared[:, :, :lines, -128:].reshape(2 * self.dp, lines * 128)[:, :count]
        return center, squares, vector.reshape(-1).astype(f32)

    def share_patch(self, project_low):
        count = self.dp // 2
        half = project_low.shape[0] // 2
        moved = lax.ppermute(project_low[half:], BOTH, [(d, d + count) for d in range(count)])
        mine = jnp.where(self.z < 2, project_low[:half], moved)
        moved = lax.ppermute(mine[half // 2 :], "section", [(0, 1)])
        return jnp.where(self.is_stem, mine[: half // 2], moved)

    def fold_patch(self, part, rows):
        rest = part.shape[0] - rows
        width = D * rest // rows
        tail = [part[rows:, first : first + width] for first in range(0, D, width)]
        return jnp.concatenate([part[:rows], jnp.concatenate(tail)], axis=1)

    def unfold_patch(self, parts):
        count, rows, width = parts.shape
        rest = rows * (width - D) // D
        tail = [parts[:, first : first + rest, D:] for first in range(0, rows, rest)]
        parts = jnp.concatenate([parts[:, :, :D], jnp.concatenate(tail, axis=2)], axis=1)
        parts = parts.reshape(2, 2, self.dp // 2, rows + rest, D)
        return parts.transpose(2, 1, 0, 3, 4).reshape(-1, D)

    def pick(self, places, axis, place):
        return lax.dynamic_index_in_dim(places, place, axis, keepdims=False)

    def first_half(self, terms, flip):
        along_y = [self.pick(stem, 1, self.y ^ flip) for stem, _ in terms]
        along_x = [self.pick(text, 2, self.x ^ flip) for _, text in terms]
        parts = [jnp.where(self.is_stem, *both) for both in zip(along_y, along_x)]
        return jnp.concatenate(parts, axis=-1)

    def second_half(self, terms, got, flip):
        place = jnp.where(self.is_stem, self.x, self.y) ^ flip
        kept = self.pick(self.first_half(terms, 0), 1, place).astype(f32)
        return (kept + self.pick(got, 1, place).astype(f32)).astype(bf16)

    def sum_first(self, terms):
        return self.across(self.first_half(terms, 1), 2, 1)

    def sum_second(self, terms, got):
        return self.across(self.second_half(terms, got, 1), 1, 2)

    def line_of(self, terms, got, got_two):
        kept = self.second_half(terms, got, 0).astype(f32)
        return (kept + got_two.astype(f32)).astype(bf16)

    def sum_line(self, line):
        groups = [[c + 4 * z for z in range(4)] for c in range(4)]
        return lax.all_to_all(
            line, "dp", split_axis=0, concat_axis=0, axis_index_groups=groups, tiled=True
        )

    def line_total(self, parts):
        return jnp.sum(parts.astype(f32), axis=0)

    def sum_low_first(self, line):
        return self.across(line, 8, 8)

    def sum_low_last(self, line, got):
        line = (line.astype(f32) + got.astype(f32)).astype(bf16)
        low = self.z & 1
        got = self.across(self.pick(line, 0, 1 - low), 4, 4)
        return self.pick(line, 0, low).astype(f32) + got.astype(f32)

    def scatter_plain(self, w_lo, w_hi, kv_lo, kv_hi, patch):
        def total(term):
            return lax.psum_scatter(term, BOTH, scatter_dimension=0, tiled=True).astype(f32)

        own_w = jnp.concatenate([w_lo, w_hi])
        own_kv = jnp.concatenate([kv_lo, kv_hi])
        own_patch = jnp.concatenate([patch, jnp.zeros((FF, D), bf16)])
        return (
            total(
                jnp.concatenate(
                    [
                        jnp.where(self.is_stem, jnp.zeros_like(own_w), own_w),
                        jnp.where(self.is_stem, own_kv, jnp.zeros_like(own_kv)),
                    ],
                    axis=1,
                )
            ),
            total(jnp.where(self.is_stem, own_patch, jnp.zeros_like(own_patch))),
        )


def sgd_update(gradient, momentum, master, average, step_rate):
    new_momentum = 0.9 * momentum + gradient
    new_master = master - step_rate * (gradient + 0.9 * new_momentum)
    new_average = 0.8 * average + 0.2 * new_master
    return (gradient, new_momentum, new_average, new_master, new_master.astype(bf16))


def per_device(
    features,
    image_group,
    token_ids,
    text_lengths,
    cotangent,
    table_master,
    table_momentum,
    table_average,
    block_master,
    block_momentum,
    block_average,
    project_master,
    project_momentum,
    project_average,
    vector_master,
    vector_momentum,
    vector_average,
):
    dp = lax.axis_size("dp")
    group = lax.axis_size(BOTH)
    dp_index = lax.axis_index("dp")
    section = lax.axis_index("section")
    is_stem = section == 0
    me = section * dp + dp_index
    tokens = token_ids.shape[0]
    image_rows = features.shape[0]
    every_patch = image_rows * dp
    table_rows = table_master.shape[0]
    images = image_group.shape[0]

    lines = Lines(dp, dp_index, section)
    block_low = block_master.astype(bf16)
    project_low = project_master.astype(bf16)
    early = block_low[:, : 7 * D]
    late_low = jnp.concatenate(
        [
            block_low[:, 8 * D :],
            block_low[:, 7 * D : 8 * D],
            jnp.zeros((block_low.shape[0], CH - D), bf16),
        ],
        axis=1,
    )
    project_rows = project_master.shape[0]
    if lines.by_hand:
        rows = late_low.shape[0]
        down_low = project_low.T.reshape(-1, rows, 128).transpose(1, 0, 2).reshape(rows, CH + FF)
        late_low = jnp.concatenate([down_low, late_low], axis=1)

    def send(block):
        return lax.all_to_all(block, "dp", split_axis=0, concat_axis=0, tiled=True)

    capacity = (2 * IMG_DEV + dp - 1) // dp
    slots = dp * capacity
    destination = image_group // GROUPS_DEV
    by_source = destination.reshape(dp, IMG_DEV)
    order = jnp.arange(IMG_DEV, dtype=i32)
    earlier = order[None, :] < order[:, None]
    rank_all = jnp.sum(
        ((by_source[:, :, None] == by_source[:, None, :]) & earlier[None]).astype(i32), axis=2
    ).reshape(images)
    my_dest = lax.dynamic_slice_in_dim(destination, dp_index * IMG_DEV, IMG_DEV)
    my_rank = lax.dynamic_slice_in_dim(rank_all, dp_index * IMG_DEV, IMG_DEV)
    stem_slot = my_dest * capacity + my_rank
    slot_of_image = jnp.where(
        destination == dp_index,
        jnp.arange(images, dtype=i32) // IMG_DEV * capacity + rank_all,
        -1,
    )
    lengths = text_lengths[0]
    group_ends = jnp.cumsum(lengths)
    group_starts = group_ends - lengths
    places = jnp.arange(tokens, dtype=i32)
    groups = jnp.arange(GROUPS_DEV, dtype=i32)
    named = jnp.any(image_group[None, :] == (dp_index * GROUPS_DEV + groups)[:, None], axis=1)
    within_group = (group_starts[None, :] <= places[:, None]) & (
        places[:, None] < group_ends[None, :]
    )
    token_start = jnp.sum(jnp.where(within_group, group_starts[None, :], 0), axis=1)
    token_named = jnp.any(within_group & named[None, :], axis=1)
    match = slot_of_image[None, :] == jnp.arange(slots, dtype=i32)[:, None]
    slot_group = jnp.max(jnp.where(match, (image_group % GROUPS_DEV)[None, :], -1), axis=1)
    group_hit = slot_group[:, None] == groups[None, :]
    slot_start = jnp.sum(jnp.where(group_hit, group_starts[None, :], 0), axis=1)
    slot_length = jnp.sum(jnp.where(group_hit, lengths[None, :], 0), axis=1)
    within = jnp.arange(LONGEST, dtype=i32)
    slot_rows = jnp.where(
        within[None, :] < slot_length[:, None], slot_start[:, None] + within[None, :], -1
    ).reshape(slots * LONGEST)
    slot_ids = jnp.max(
        jnp.where(slot_rows[:, None] == places[None, :], token_ids[None, :], -1), axis=1
    )

    slot_ids, features = barrier((slot_ids, features))
    rows_f = features.astype(f32)
    local_center = jnp.mean(rows_f, axis=0)
    local_square = jnp.sum(jnp.square(rows_f - local_center), axis=0)
    state = jnp.stack([local_center, local_square])
    vector_low = lax.reduce_precision(vector_master, 8, 7)
    if lines.by_hand:
        later = jnp.concatenate(
            [
                lines.fold_patch(lines.share_patch(project_low), early.shape[0]),
                lines.fold_small(state, vector_low, early.shape[0]),
            ],
            axis=1,
        )
        early = lines.gather_line(early)

    got_ids = send(slot_ids.reshape(dp, capacity * LONGEST)).reshape(slots, LONGEST)
    slot_hit = stem_slot[:, None] == jnp.arange(slots, dtype=i32)[None, :]
    image_ids = jnp.max(jnp.where(slot_hit[:, :, None], got_ids[None], -1), axis=1)
    ids = jnp.concatenate([image_ids.reshape(-1), jnp.where(token_named, -1, token_ids)])
    height = ids.shape[0]
    here = ids >= 0
    candidates = jnp.arange(height, dtype=i32)
    before = candidates[None, :] < candidates[:, None]
    row = jnp.sum((before & here[None, :]).astype(i32), axis=1)
    row = jnp.where(here, row, -1)
    row_count = jnp.sum(here.astype(i32))
    row_blocks = ((row_count + ROWS - 1) // ROWS).reshape(1)
    depth = jnp.concatenate(
        [jnp.tile(within, IMG_DEV), places - token_start]
    )
    image_row, own_row = row[: IMG_DEV * LONGEST], row[IMG_DEV * LONGEST :]
    arrival_row = jnp.max(
        jnp.where(slot_hit[:, :, None], image_row.reshape(IMG_DEV, 1, LONGEST), -1), axis=0
    ).reshape(slots * LONGEST)
    chosen = row[None, :] == candidates[:, None]
    start = jnp.max(jnp.where(chosen, (row - depth)[None, :], -1), axis=1)
    start = jnp.where(candidates < row_count, start, candidates)[:, None]

    room = max(16, (2 * tokens + 2 * tokens // 4) // group)
    half_room = dp * room
    owner = ids // table_rows
    same = (ids[:, None] == ids[None, :]) & here[None, :]
    is_first = here & ~jnp.any(same & before, axis=1)
    rank = jnp.sum(
        ((owner[:, None] == owner[None, :]) & before & is_first[None, :]).astype(i32), axis=1
    )
    rounds_here = jnp.max(jnp.where(is_first, rank, 0)) // room + 1
    table_low = table_master.astype(bf16)

    def round_of(turn):
        turn_rank = rank - turn * room
        first_place = jnp.where(
            is_first & (turn_rank >= 0) & (turn_rank < room), owner * room + turn_rank, -1
        )
        place = jnp.max(jnp.where(same, first_place[None, :], -1), axis=1)
        place = jnp.max(jnp.where(chosen, place[None, :], -1), axis=1)
        slot = jnp.arange(half_room, dtype=i32) + section * half_room
        asked = jnp.max(
            jnp.where(first_place[None, :] == slot[:, None], (ids % table_rows)[None, :], -1),
            axis=1,
        )
        return place, asked.reshape(dp, room)

    def serve(asked):
        hit = (asked[:, None] == jnp.arange(table_rows, dtype=i32)[None, :]).astype(bf16)
        served = mm(hit, table_low).astype(bf16)
        return send(served.reshape(dp, room, D)).reshape(half_room, D)

    def unpacked(place, served, served_low):
        return simple(
            unpack_rows,
            [served_low, served, place[:, None]],
            [shape((height, D), bf16)],
            [],
            4 * 10**9,
        )[0]

    cot_sum = jnp.sum(cotangent, axis=0)
    arrival_shape = shape((slots * LONGEST, HALF), bf16)
    cot_sent = simple(
        pack_half,
        [slot_rows[:, None], lax.dynamic_slice_in_dim(cotangent, section * HALF, HALF, axis=1)],
        [arrival_shape],
        [],
        3 * 10**9,
    )[0]
    if lines.by_hand:
        got_ids, early, later, cot_sent, cot_sum = barrier(
            (got_ids, early, later, cot_sent, cot_sum)
        )
        early = lines.gather_first(early)
        later = lines.gather_line(later)
    place, asked = round_of(0)
    asked = jnp.concatenate([asked, jnp.broadcast_to(rounds_here, (dp, 1))], axis=1)
    asked = send(asked)
    if lines.by_hand:
        asked, early, later, cot_sent = barrier((asked, early, later, cot_sent))
        early = lines.gather_second(early)
        later = lines.gather_first(later)
        cot_b = send(cot_sent.reshape(dp, capacity * LONGEST, HALF))
        cot_b = cot_b.reshape(slots * LONGEST, HALF)
    rounds = jnp.max(asked[:, room])
    asked = asked[:, :room].reshape(half_room)
    served = serve(asked)
    served_low = lax.ppermute(served, "section", [(0, 1)])
    if lines.by_hand:
        served, served_low, early, later, place, start, late_low, cot_b = barrier(
            (served, served_low, early, later, place, start, late_low, cot_b)
        )
        w_late = w_down = lax.all_gather(late_low, BOTH, axis=0, tiled=True)
        later = lines.gather_second(later)
        w_text, w_kv = lines.gather_place(*early, 5 * D)
        w_patch, shared = lines.gather_place(*later, None)
        w_patch = lines.unfold_patch(w_patch.reshape(2 * dp, -1, CH))
        center, squares, flat = lines.unfold_small(shared, vector_master.shape[0], image_rows)
    else:
        w_text = lax.all_gather(early[:, : 5 * D], BOTH, axis=0, tiled=True)
        w_kv = lax.all_gather(early[:, 5 * D :], BOTH, axis=0, tiled=True)
        cot_b = send(cot_sent.reshape(dp, capacity * LONGEST, HALF))
        cot_b = cot_b.reshape(slots * LONGEST, HALF)
        w_late = lax.all_gather(late_low, BOTH, axis=0, tiled=True)
        project_full = lax.all_gather(project_low, BOTH, axis=0, tiled=True)
        w_down = project_full.T
        w_patch = project_full[:CH]
        stats = lax.all_gather(state, "dp")
        center = jnp.mean(stats[:, 0], axis=0)
        squares = jnp.sum(stats[:, 1] + image_rows * jnp.square(stats[:, 0] - center), axis=0)
        flat = lax.all_gather(vector_low, BOTH, axis=0, tiled=True)
    factor = lax.rsqrt(squares / every_patch + EPS)
    bn_gain, bn_bias = flat[:CH], flat[CH : 2 * CH]
    offset = 2 * CH + D
    patch_bias = flat[2 * CH : offset].reshape(1, D)
    ln_vecs = flat[offset : offset + 6 * D].reshape(6, D)
    up_bias = flat[offset + 6 * D : offset + 6 * D + FF].reshape(1, FF)
    down_bias = flat[offset + 6 * D + FF :].reshape(1, D)
    vecs_outer = ln_vecs[:4]
    vecs_three = jnp.concatenate([ln_vecs[4:], down_bias])
    bn = jnp.stack([center, factor, bn_gain, bn_bias])

    def embed_more(turn, embed):
        place, asked = round_of(turn)
        served = serve(send(asked).reshape(half_room))
        return embed + unpacked(place, served, lax.ppermute(served, "section", [(0, 1)]))

    embed = lax.fori_loop(1, rounds, embed_more, unpacked(place, served, served_low))

    if lines.by_hand:
        w_text, w_kv, w_patch, embed = barrier((w_text, w_kv, w_patch, embed))

    def halves(width, column):
        return [at((HALF, width), 0, column), at((HALF, width), 1, column)]

    qkv_specs = halves(3 * D, 0) + halves(D, 3) + halves(D, 4)
    qkv_inputs = [w_text] * 6
    kv_specs = halves(D, 0) + halves(D, 1)
    kv_inputs = [w_kv] * 4
    patch_spec = at((CH, D), 0, 0)
    blocks = 7
    per_block = image_rows // blocks
    qkv_scratch = [
        pltpu.VMEM((D, 3 * D), bf16),
        pltpu.VMEM((D, D), bf16),
        pltpu.VMEM((D, D), bf16),
        pltpu.VMEM((height, D), bf16),
    ]

    def rows_spec(width):
        return pl.BlockSpec((per_block, width), lambda step: (step, 0))

    slot_shape = shape((IMG_DEV * LONGEST, HALF), bf16)
    blocks_spec = pl.BlockSpec(memory_space=pltpu.SMEM)
    pack, take = image_row[:, None], image_row[None, :]
    rows_shape = shape((image_rows, D), bf16)

    text_saved = [
        shape((height, 3 * D), bf16),
        shape((height, D), bf16),
        shape((height, D), f32),
        slot_shape,
        slot_shape,
    ]
    stem_saved = [rows_shape] * 3

    def first_text():
        inputs = [embed, start, pack, vecs_outer]
        done = call(
            text_first,
            1,
            [blocks_spec] + [whole(a) for a in inputs] + qkv_specs,
            [whole(o) for o in text_saved],
            text_saved,
            qkv_scratch,
            15 * 10**9,
        )(row_blocks, *inputs, *qkv_inputs)
        return (*done, *blank(stem_saved))

    def first_stem():
        done = call(
            stem_forward,
            blocks,
            [rows_spec(CH), whole(bn), patch_spec, whole(patch_bias)] + kv_specs,
            [rows_spec(D)] * 3,
            stem_saved,
            [pltpu.VMEM((D, 2 * D), bf16)],
            23 * 10**9,
        )(features, bn, w_patch, patch_bias, *kv_inputs)
        return (*blank(text_saved), *done)

    qkv_rows, mix_rows, resid_one, q_a, q_b, patches, kv_lo, kv_hi = lax.cond(
        is_stem, first_stem, first_text
    )

    kv_moved = lax.ppermute(kv_hi, "section", [(0, 1)])

    def to_cores(block_a, block_b):
        return jnp.where(is_stem, lax.ppermute(block_a, "section", [(1, 0)]), block_b)

    q_here = to_cores(q_a, q_b)
    def cross(kv):
        return call(
            cross_forward,
            1,
            [whole(q_here), whole(kv)],
            [whole(q_here)],
            [slot_shape],
            [],
            8 * 10**9,
        )(q_here, kv)[0]

    mix_b = lax.cond(is_stem, lambda: cross(kv_lo), lambda: cross(kv_moved))

    mix_a = lax.ppermute(mix_b, "section", [(0, 1)])
    cot_a = lax.ppermute(cot_b, "section", [(0, 1)])
    grad_out = simple(
        join_cotangent,
        [arrival_row[None, :], own_row[None, :], cot_a, cot_b, cotangent],
        [shape((height, D), bf16)],
        [],
        4 * 10**9,
    )[0]

    chunks = 3
    wide = FF // chunks
    own_shape = shape((tokens, HALF), bf16)
    middle_shapes = [
        arrival_shape,
        arrival_shape,
        own_shape,
        own_shape,
        shape((height, D), f32),
        shape((D, 2 * (CH + FF)), bf16),
        slot_shape,
        slot_shape,
        shape((2, D), f32),
        shape((1, FF), f32),
    ]

    def middle_text():
        inputs = [
            mix_a, mix_b, take, pack, arrival_row[:, None], own_row[:, None],
            resid_one, grad_out, vecs_three,
        ]

        def chunk(step):
            return jnp.minimum(step, chunks - 1)

        if lines.by_hand:
            first_up = (CH + FF) // wide
            down_rows = D // (chunks + 1)
            down_spec = pl.BlockSpec((down_rows, CH + FF), lambda step: (1 + chunk(step), 0))
        else:
            first_up = 0
            down_rows = D
            down_spec = pl.BlockSpec((D, wide), lambda step: (0, 1 + chunk(step)))
        down_width = wide * D // down_rows
        outs = [whole(o) for o in middle_shapes]
        outs[5] = pl.BlockSpec(memory_space=pl.ANY)
        outs[9] = pl.BlockSpec((1, wide), lambda step: (0, chunk(step)))
        return call(
            text_middle,
            chunks + 1,
            [blocks_spec]
            + [whole(a) for a in inputs]
            + [pl.BlockSpec((1, wide), lambda step: (0, chunk(step)))]
            + halves(wide, first_up + chunks)
            + [
                pl.BlockSpec((HALF, wide), lambda step: (0, first_up + chunk(step))),
                pl.BlockSpec((HALF, wide), lambda step: (1, first_up + chunk(step))),
                down_spec,
            ],
            outs,
            middle_shapes,
            [
                pltpu.VMEM((D, D), bf16),
                pltpu.VMEM((D, wide), bf16),
                pltpu.VMEM((height, D), bf16),
                pltpu.VMEM((height, D), bf16),
                pltpu.VMEM((D, height), bf16),
                pltpu.VMEM((height, 1), f32),
                pltpu.VMEM((height, D), f32),
                pltpu.VMEM((height, D), f32),
                pltpu.VMEM((D, height), bf16),
                pltpu.VMEM((D, wide), f32),
                pltpu.VMEM((D, wide), f32),
                pltpu.VMEM((2, D, wide), bf16),
                pltpu.VMEM((2, down_rows, down_width), bf16),
                pltpu.VMEM((D, wide), bf16),
                pltpu.VMEM((height, D), bf16),
                pltpu.SemaphoreType.DMA((2, 2)),
            ],
            29 * 10**9,
        )(row_blocks, *inputs, up_bias, *[w_late] * 4, w_down)

    def middle_stem():
        made = list(blank(middle_shapes))
        made[5] = jnp.zeros(middle_shapes[5].shape, bf16)
        return tuple(made)

    (
        out_lo, out_hi, own_lo, own_hi, grad_two, late_term, g_a, g_b, grads_three, grad_up_bias,
    ) = lax.cond(is_stem, middle_stem, middle_text)
    if lines.by_hand:
        late_grad = lax.psum_scatter(late_term, BOTH, scatter_dimension=0, tiled=True)
    else:
        late_grad = lax.psum_scatter(
            late_term[:, : CH + FF], BOTH, scatter_dimension=0, tiled=True
        )
        down_turned = lax.psum_scatter(
            late_term[:, CH + FF :], BOTH, scatter_dimension=1, tiled=True
        )
    g_here = to_cores(g_a, g_b)
    out_here = to_cores(out_lo, out_hi)
    g_here, out_here = barrier((g_here, out_here))
    got_out = send(out_here.reshape(dp, capacity * LONGEST, HALF)).reshape(slots * LONGEST, HALF)

    def cross_back(kv):
        return tuple(
            call(
                cross_backward,
                1,
                [whole(q_here), whole(g_here), whole(kv)],
                [whole(q_here), whole(kv)],
                [slot_shape, rows_shape],
                [],
                0,
            )(q_here, g_here, kv)
        )

    grad_here, grad_kv = lax.cond(is_stem, lambda: cross_back(kv_lo), lambda: cross_back(kv_moved))
    grad_here, grad_kv, got_out = barrier((grad_here, grad_kv, got_out))
    grad_kv_moved = lax.ppermute(grad_kv, "section", [(1, 0)])

    stem_kv_shapes = [
        rows_shape,
        shape((HALF, 2 * D), bf16),
        shape((HALF, 2 * D), bf16),
        shape((1, D), f32),
    ]

    def stem_kv():
        return tuple(
            call(
                stem_backward_kv,
                blocks,
                kv_specs + [rows_spec(D)] * 3,
                [rows_spec(D)] + [at(o.shape, 0, 0) for o in stem_kv_shapes[1:]],
                stem_kv_shapes,
                [pltpu.VMEM((D, 2 * D), bf16), pltpu.VMEM((D, 2 * D), f32)],
                23 * 10**9,
            )(*kv_inputs, patches, grad_kv, grad_kv_moved)
        )

    grad_b = grad_here
    grad_rows, kv_w_lo, kv_w_hi, patch_bias_sum = lax.cond(
        is_stem, stem_kv, lambda: tuple(blank(stem_kv_shapes))
    )
    grad_a = lax.ppermute(grad_b, "section", [(0, 1)])
    grad_a, grad_rows = barrier((grad_a, grad_rows))

    row_shape = shape((half_room, D), bf16)
    text_last_shapes = [
        shape((height, D), bf16),
        row_shape,
        row_shape,
        shape((HALF, 5 * D), bf16),
        shape((HALF, 5 * D), bf16),
        shape((4, D), f32),
    ]
    half_channels = CH // 2
    stem_last_shapes = [
        shape((image_rows, half_channels), bf16),
        shape((image_rows, half_channels), bf16),
        shape((CH, D), bf16),
        shape((2, CH), f32),
    ]

    def last_text():
        inputs = [
            grad_a, grad_b, take, place[None, :], grad_two, resid_one, embed,
            qkv_rows, mix_rows, start, vecs_outer,
        ]
        done = call(
            text_last,
            1,
            [blocks_spec] + [whole(a) for a in inputs] + qkv_specs,
            [whole(o) for o in text_last_shapes],
            text_last_shapes,
            [
                pltpu.VMEM((height, D), bf16),
                pltpu.VMEM((height, D), bf16),
                pltpu.VMEM((height, 2 * D), f32),
                pltpu.VMEM((D, 3 * D), f32),
                pltpu.VMEM((height, D), f32),
            ],
            0,
        )(row_blocks, *inputs, *qkv_inputs)
        return (*done, *blank(stem_last_shapes))

    def last_stem():
        done = call(
            stem_backward,
            blocks,
            [rows_spec(CH), whole(bn), patch_spec, rows_spec(D)],
            [rows_spec(half_channels)] * 2 + [at(o.shape, 0, 0) for o in stem_last_shapes[2:]],
            stem_last_shapes,
            [pltpu.VMEM((CH, D), f32)],
            0,
        )(features, bn, w_patch, grad_rows)
        return (*blank(text_last_shapes), *done)

    (
        grad_embed, rows_low, rows_high, grad_w_lo, grad_w_hi, grads_outer,
        grad_lo, grad_hi, grad_patch_w, bn_sums,
    ) = lax.cond(is_stem, last_stem, last_text)

    def row_sums(asked, rows):
        hit = (jnp.arange(table_rows, dtype=i32)[:, None] == asked[None, :]).astype(bf16)
        return mm(hit, rows.reshape(half_room, D))

    def table_more(turn, total):
        place, asked = round_of(turn)
        slot = jnp.arange(group * room, dtype=i32)
        rows = mm((slot[:, None] == place[None, :]).astype(bf16), grad_embed).astype(bf16)
        moved = lax.ppermute(rows[:half_room], "section", [(1, 0)])
        rows = jnp.where(is_stem, moved, rows[half_room:]).reshape(dp, room, D)
        return total + row_sums(send(asked).reshape(half_room), send(rows))

    def table_update(total):
        return sgd_update(total, table_momentum, table_master, table_average, 0.05)

    def table_updated(got_rows):
        return lax.cond(
            rounds > 1,
            lambda: table_update(lax.fori_loop(1, rounds, table_more, row_sums(asked, got_rows))),
            lambda: table_update(row_sums(asked, got_rows)),
        )

    gone = jnp.zeros((), f32)
    vector_term = jnp.concatenate(
        [
            jnp.where(is_stem, bn_sums.reshape(-1), gone),
            jnp.where(is_stem, patch_bias_sum.reshape(-1), gone),
            jnp.where(
                is_stem,
                gone,
                jnp.concatenate(
                    [
                        grads_outer.reshape(-1),
                        grads_three.reshape(-1),
                        grad_up_bias.reshape(-1),
                        cot_sum,
                    ]
                ),
            ),
        ]
    ).reshape(-1, CH)

    def summed(vector, steps):
        for step in steps:
            vector = vector + lax.ppermute(vector, "dp", [(i, i ^ step) for i in range(dp)])
        return vector

    grad_w_lo, grad_w_hi, kv_w_lo, kv_w_hi = barrier(
        (grad_w_lo, grad_w_hi, kv_w_lo, kv_w_hi)
    )
    own_here = to_cores(own_lo, own_hi)

    def output(got_out):
        return simple(
            join_output,
            [slot_rows[None, :], got_out, own_here],
            [own_shape],
            [],
            3 * 10**9,
        )[0]

    if lines.by_hand:
        owners = CH // project_rows
        parts = grad_patch_w.reshape(owners, 2, project_rows // 2, D)
        terms = [
            (lax.ppermute(grad_w_lo, "section", [(1, 0)]), grad_w_hi),
            (kv_w_lo, lax.ppermute(kv_w_hi, "section", [(0, 1)])),
        ]
        terms = [
            tuple(w.reshape(4, 2, 2, HALF // dp, w.shape[1]) for w in term) for term in terms
        ]
        patch = (parts[:, 0], lax.ppermute(parts[:, 1], "section", [(0, 1)]))
        patch = [tuple(w.reshape(2, 2, 2, project_rows // 2, D) for w in patch)]
        terms, patch = barrier((terms, patch))
        first = lines.first_half(terms, 1)
        first, rows_low, vector_term = barrier((first, rows_low, vector_term))
        got = lines.across(first, 2, 1)
        patch_got = lines.sum_first(patch)
        vector_term = summed(vector_term, (4, 8))
        sent_rows = to_cores(rows_low, rows_high).reshape(dp, room, D)
        got_rows = send(sent_rows)
        got, patch_got, got_rows, vector_term = barrier((got, patch_got, got_rows, vector_term))
        got_two = lines.sum_second(terms, got)
        patch_got_two = lines.sum_second(patch, patch_got)
        table_new = table_updated(got_rows)
        got_two, patch_got_two, _, vector_term, grad_hi, got_out = barrier(
            (got_two, patch_got_two, table_new[0][:8, :128], vector_term, grad_hi, got_out)
        )
        line = lines.line_of(terms, got, got_two)
        patch_line = lines.line_of(patch, patch_got, patch_got_two)
        patch_got = lines.sum_low_first(patch_line)
        line, patch_got = barrier((line, patch_got))
        line_parts = lines.sum_line(line)
        vector_total = summed(vector_term, (1, 2))
        block_piece = output(got_out)
        got_hi = lax.ppermute(grad_hi, "section", [(0, 1)])
        line_parts, late_grad = barrier((line_parts, late_grad))
        tail_grad = lines.line_total(line_parts)
        patch_low = lines.sum_low_last(patch_line, patch_got)
        patch_high = lax.ppermute(patch_low, "section", [(1, 0)])
        down_grad = late_grad[:, CH + FF :].astype(f32).reshape(late_grad.shape[0], -1, 128)
        down_grad = down_grad.transpose(1, 0, 2).reshape(D, 128).T
        project_grad = down_grad + jnp.where(
            is_stem & (dp_index < owners), jnp.concatenate([patch_low, patch_high]), 0.0
        )
    else:
        vector_total = summed(vector_term, [1 << bit for bit in range(dp.bit_length() - 1)])
        got_rows = send(to_cores(rows_low, rows_high).reshape(dp, room, D))
        block_piece = output(got_out)
        got_hi = lax.ppermute(grad_hi, "section", [(0, 1)])
        table_new = table_updated(got_rows)
        tail_grad, patch_grad = lines.scatter_plain(
            grad_w_lo, grad_w_hi, kv_w_lo, kv_w_hi, grad_patch_w
        )
        project_grad = down_turned.astype(f32).T + patch_grad
    late_grad = late_grad.astype(f32)
    block_grad = jnp.concatenate(
        [tail_grad, late_grad[:, FF : FF + D], late_grad[:, :FF]], axis=1
    )
    vector_total = vector_total + lax.ppermute(vector_total, "section", [(0, 1), (1, 0)])
    vector_grad = lax.dynamic_slice_in_dim(
        vector_total.reshape(-1), me * vector_master.shape[0], vector_master.shape[0]
    )

    own_pre = jnp.where(is_stem, grad_lo, got_hi).astype(f32)
    first_channel = section * half_channels

    def own_half(array):
        return lax.dynamic_slice_in_dim(array, first_channel, half_channels, axis=array.ndim - 1)

    own_normed = (own_half(features).astype(f32) - own_half(center)) * own_half(factor)
    own_gain = own_half(bn_gain)
    feature_grad = own_half(factor) * (
        own_pre * own_gain
        - own_gain * own_half(vector_total[1]) / every_patch
        - own_normed * (own_gain * own_half(vector_total[0]) / every_patch)
    )

    root_tokens = math.sqrt(tokens * dp)
    block_new = sgd_update(
        block_grad, block_momentum, block_master, block_average, 0.5 * D ** (-0.5) / root_tokens
    )
    project_new = sgd_update(
        project_grad,
        project_momentum,
        project_master,
        project_average,
        0.5 * FF ** (-0.5) / root_tokens,
    )
    vector_new = sgd_update(
        vector_grad, vector_momentum, vector_master, vector_average, 0.1 / root_tokens
    )
    return (block_piece, feature_grad, *table_new, *block_new, *project_new, *vector_new)


def solution(mesh):
    rows = P(BOTH, None)
    flat = P(BOTH)
    placed = (
        (P("dp", None), P(), P("dp"), P("dp", None), P("dp", None))
        + (rows,) * 9
        + (flat,) * 3
    )
    return jax.shard_map(
        per_device,
        mesh=mesh,
        in_specs=placed,
        out_specs=(P("dp", "section"), P("dp", "section")) + (rows,) * 15 + (flat,) * 5,
        check_vma=False,
    )
```

```python
import functools
import math

import jax
import jax.numpy as jnp
from jax import lax
from jax.experimental import pallas as pl
from jax.experimental.pallas import tpu as pltpu
from jax.sharding import PartitionSpec as P

D = 768
HEADS = 12
HEAD_DIM = 64
QUAD = 4 * HEAD_DIM
QUADS = HEADS // 4
FF = 3072
CH = 1024
PATCH = 196
WINDOW = 208
IMG_DEV = 16
GROUPS_DEV = 32
LONGEST = 32
HALF = D // 2
ROWS = 256
BLOCK = 128
SPAN = BLOCK + LONGEST
SCALE = HEAD_DIM ** (-0.5)
EPS = 1e-05
NEG = -1e30
BOTH = ("section", "dp")
VMEM_BYTES = 58 * 1024 * 1024
bf16 = jnp.bfloat16
f32 = jnp.float32
i32 = jnp.int32


def mm(left, right):
    return jnp.dot(left, right, preferred_element_type=f32)


def mm_rt(left, right):
    return lax.dot_general(left, right, (((1,), (1,)), ((), ())), preferred_element_type=f32)


def mm_lt(left, right):
    return lax.dot_general(left, right, (((0,), (0,)), ((), ())), preferred_element_type=f32)


def normalise(values):
    shifted = values - jnp.mean(values, axis=-1, keepdims=True)
    factor = lax.rsqrt(jnp.mean(shifted * shifted, axis=-1, keepdims=True) + EPS)
    return shifted * factor, factor


def norm_back(incoming, unit, factor, gain):
    scaled = incoming * gain
    mean_grad = jnp.mean(scaled, axis=-1, keepdims=True)
    mean_cross = jnp.mean(scaled * unit, axis=-1, keepdims=True)
    return factor * (scaled - mean_grad - unit * mean_cross)


GELU_C = math.sqrt(2.0 / math.pi)


def gelu_parts(values):
    square = values * values
    bend = jnp.tanh(GELU_C * values * (1.0 + 0.044715 * square))
    half = 0.5 * (1.0 + bend)
    slope = half + 0.5 * values * (1.0 - bend * bend) * (GELU_C * (1.0 + 3 * 0.044715 * square))
    return values * half, slope


def gelu_only(values):
    bend = jnp.tanh(GELU_C * values * (1.0 + 0.044715 * (values * values)))
    return 0.5 * values * (1.0 + bend)


def head_masks(dtype, width=QUAD):
    lanes = lax.broadcasted_iota(i32, (1, width), 1) // HEAD_DIM
    return [jnp.where(lanes == h, 1.0, 0.0).astype(dtype) for h in range(width // HEAD_DIM)]


def spread_heads(rows, masks):
    return jnp.concatenate([rows * m for m in masks], axis=0)


def join_heads(stacked, masks):
    count = stacked.shape[0] // len(masks)
    total = stacked[:count] * masks[0]
    for h in range(1, len(masks)):
        total = total + stacked[h * count : (h + 1) * count] * masks[h]
    return total


def softmax(scores, allowed):
    scores = jnp.where(allowed, scores * SCALE, NEG)
    weights = jnp.exp(scores - jnp.max(scores, axis=-1, keepdims=True))
    return weights * (1.0 / jnp.sum(weights, axis=-1, keepdims=True))


def one_hot_cols(index_col, width):
    places = lax.broadcasted_iota(i32, (index_col.shape[0], width), 1)
    return jnp.where(places == index_col, 1.0, 0.0).astype(bf16)


def one_hot_rows(index_row, height, offset=0):
    places = lax.broadcasted_iota(i32, (height, index_row.shape[1]), 0) + offset
    return jnp.where(places == index_row, 1.0, 0.0).astype(bf16)


def join_halves(target, low_ref, high_ref):
    count = low_ref.shape[0]
    target[:count, :] = low_ref[...]
    target[count : 2 * count, :] = high_ref[...]


def key_span(first):
    return pl.multiple_of(jnp.maximum(first - LONGEST, 0), LONGEST)


def self_allowed(start_rows, first, key_first):
    rows = lax.broadcasted_iota(i32, (BLOCK, SPAN), 0) + first
    keys = lax.broadcasted_iota(i32, (BLOCK, SPAN), 1) + key_first
    allowed = (keys <= rows) & (keys >= start_rows)
    return jnp.concatenate([jnp.where(allowed, 1, 0)] * 4, axis=0) > 0


def chunks_of(count, size, body):
    def step(index, carry):
        body(pl.multiple_of(index * size, size))
        return carry

    lax.fori_loop(0, count, step, 0)


def text_first(
    blocks, embed, start, pack, vecs,
    qkv_lo, qkv_hi, out_lo, out_hi, cq_lo, cq_hi,
    qkv_rows, mix_rows, resid_one, slots_a, slots_b,
    w_qkv, w_out, w_cq, queries,
):
    count = blocks[0]
    join_halves(w_qkv, qkv_lo, qkv_hi)
    join_halves(w_out, out_lo, out_hi)
    join_halves(w_cq, cq_lo, cq_hi)
    queries[...] = jnp.zeros_like(queries)
    masks = head_masks(bf16)
    masks_f = head_masks(f32)

    def project(first):
        rows = pl.ds(first, ROWS)
        unit, _ = normalise(embed[rows, :].astype(f32))
        normed = (unit * vecs[0:1, :] + vecs[1:2, :]).astype(bf16)
        for third in range(3):
            columns = slice(third * D, (third + 1) * D)
            qkv_rows[rows, columns] = mm(normed, w_qkv[:, columns]).astype(bf16)

    def attend(first):
        rows = pl.ds(first, BLOCK)
        key_first = key_span(first)
        span = pl.ds(key_first, SPAN)
        allowed = self_allowed(start[rows, :], first, key_first)
        for quad in range(QUADS):
            lanes, keys, values = quad_lanes(quad)
            query = spread_heads(qkv_rows[rows, lanes], masks)
            shares = softmax(mm_rt(query, qkv_rows[span, keys]), allowed)
            mixed = mm(shares.astype(bf16), qkv_rows[span, values])
            mix_rows[rows, lanes] = join_heads(mixed, masks_f).astype(bf16)

    def finish(first):
        rows = pl.ds(first, ROWS)
        resid = embed[rows, :].astype(f32) + mm(mix_rows[rows, :], w_out[...])
        resid_one[rows, :] = resid
        unit, _ = normalise(resid)
        normed = (unit * vecs[2:3, :] + vecs[3:4, :]).astype(bf16)
        queries[rows, :] = mm(normed, w_cq[...]).astype(bf16)

    chunks_of(count, ROWS, project)
    chunks_of(count * (ROWS // BLOCK), BLOCK, attend)
    chunks_of(count, ROWS, finish)
    packed = mm(one_hot_cols(pack[...], queries.shape[0]), queries[...]).astype(bf16)
    slots_a[...] = packed[:, :HALF]
    slots_b[...] = packed[:, HALF:]


def quad_lanes(quad):
    return [slice(part * D + quad * QUAD, part * D + (quad + 1) * QUAD) for part in range(3)]


def text_middle(
    blocks, mix_a, mix_b, take, pack, arrival, own, resid_one, cotangent, vecs, up_bias,
    cout_lo, cout_hi, up_lo, up_hi, down_part,
    out_lo, out_hi, own_lo, own_hi, grad_two, late, slots_a, slots_b,
    vec_grad, up_bias_grad,
    w_cout, w_up, mixed, normed, normed_t, factor_s, total, back, grad_down_t,
    up_sum, down_sum, up_buffer, down_buffer, w_down_t, block_out, sems,
):
    step = pl.program_id(0)
    last = pl.num_programs(0) - 1
    count = blocks[0]
    wide = w_up.shape[1]
    by_owner = down_buffer.shape[1] != D

    def copies(chunk):
        slot = chunk % 2
        place = (chunk + 1) % 4
        columns = slice(chunk * wide, (chunk + 1) * wide)
        pairs = [(up_buffer.at[slot], late.at[:, columns])]
        if by_owner:
            height = down_buffer.shape[1]
            rows = slice(place * height, (place + 1) * height)
            pairs.append((down_buffer.at[slot], late.at[rows, CH + FF :]))
        else:
            columns = slice(CH + FF + place * wide, CH + FF + (place + 1) * wide)
            pairs.append((down_buffer.at[slot], late.at[:, columns]))
        return [
            pltpu.make_async_copy(source, target, sems.at[slot, i])
            for i, (source, target) in enumerate(pairs)
        ]

    for chunk in (0, 1):

        @pl.when(step == chunk + 2)
        def _():
            for copy in copies(chunk):
                copy.wait()

    @pl.when(step == 0)
    def _():
        w_cout[:HALF, :] = cout_lo[:, :D]
        w_cout[HALF:, :] = cout_hi[:, :D]
        normed[...] = jnp.zeros_like(normed)
        block_out[...] = jnp.zeros_like(block_out)
        vec_grad[...] = jnp.zeros_like(vec_grad)

        def begin(first):
            rows = pl.ds(first, ROWS)
            places = lax.broadcasted_iota(i32, (ROWS, take.shape[1]), 0) + first
            hit = jnp.where(places == take[...], 1.0, 0.0).astype(bf16)
            mixed[rows, :HALF] = mm(hit, mix_a[...]).astype(bf16)
            mixed[rows, HALF:] = mm(hit, mix_b[...]).astype(bf16)
            resid_two = resid_one[rows, :] + mm(mixed[rows, :], w_cout[...])
            unit, factor = normalise(resid_two)
            grad_two[rows, :] = unit
            factor_s[rows, :] = factor
            low = (unit * vecs[0:1, :] + vecs[1:2, :]).astype(bf16)
            normed[rows, :] = low
            normed_t[:, rows] = low.T
            total[rows, :] = resid_two + vecs[2:3, :]
            back[rows, :] = jnp.zeros((ROWS, D), f32)
            grad_down_t[:, rows] = cotangent[rows, :].T

        chunks_of(count, ROWS, begin)

    @pl.when(step < last)
    def _():
        join_halves(w_up, up_lo, up_hi)
        parts = wide // 128
        if by_owner:
            height = down_buffer.shape[1] // parts
            for i in range(0, parts, 2):
                pair = down_part[i * height : (i + 2) * height, :].astype(f32)
                for h in range(2):
                    one = pair[h * height : (h + 1) * height]
                    one = jnp.concatenate([one[:, j : j + 128] for j in range(0, CH + FF, 128)], axis=0)
                    w_down_t[:, (i + h) * 128 : (i + h + 1) * 128] = one.astype(bf16)
        else:
            w_down_t[...] = down_part[...]
        up_sum[...] = jnp.zeros_like(up_sum)
        down_sum[...] = jnp.zeros_like(down_sum)
        up_bias_grad[...] = jnp.zeros_like(up_bias_grad)

        def forward_back(first):
            rows = pl.ds(first, ROWS)
            act, slope = gelu_parts(mm(normed[rows, :], w_up[...]) + up_bias[...])
            act = act.astype(bf16)
            total[rows, :] += mm_rt(act, w_down_t[...])
            grad_up = (mm(cotangent[rows, :], w_down_t[...]) * slope).astype(bf16)
            up_bias_grad[...] += jnp.sum(grad_up.astype(f32), axis=0, keepdims=True)
            up_sum[...] += mm(normed_t[:, rows], grad_up)
            down_sum[...] += mm(grad_down_t[:, rows], act)
            back[rows, :] += mm_rt(grad_up, w_up[...])

        chunks_of(count, ROWS, forward_back)
        slot = step % 2
        up_buffer[slot] = up_sum[...].astype(bf16)
        if by_owner:
            pieces = [
                jnp.concatenate(
                    [down_sum[j : j + height, first : first + 128] for j in range(0, D, height)],
                    axis=1,
                )
                for first in range(0, wide, 128)
            ]
            for i in range(0, parts, 2):
                pair = jnp.concatenate(pieces[i : i + 2], axis=0).astype(bf16)
                down_buffer[slot, i * height : (i + 2) * height, :] = pair
        else:
            down_buffer[slot] = down_sum[...].astype(bf16)

    for chunk in range(3):

        @pl.when(step == chunk)
        def _():
            for copy in copies(chunk):
                copy.start()

    @pl.when(step == last)
    def _():
        up_sum[:, :D] = jnp.zeros((D, D), f32)

        def end(first):
            rows = pl.ds(first, ROWS)
            block_out[rows, :] = total[rows, :].astype(bf16)
            incoming, unit = back[rows, :], grad_two[rows, :]
            vec_grad[0:1, :] += jnp.sum(incoming * unit, axis=0, keepdims=True)
            vec_grad[1:2, :] += jnp.sum(incoming, axis=0, keepdims=True)
            grad = norm_back(incoming, unit, factor_s[rows, :], vecs[0:1, :])
            grad = cotangent[rows, :].astype(f32) + grad
            grad_two[rows, :] = grad
            grad = grad.astype(bf16)
            up_sum[:, :D] += mm_lt(mixed[rows, :], grad)
            normed[rows, :] = mm_rt(grad, w_cout[...]).astype(bf16)

        chunks_of(count, ROWS, end)
        slot = step % 2
        up_buffer[slot, :, :D] = up_sum[:, :D].astype(bf16)
        up_buffer[slot, :, D:] = jnp.zeros((D, wide - D), bf16)
        down_buffer[slot] = jnp.zeros(down_buffer.shape[1:], bf16)
        for copy in copies(3):
            copy.start()
        for index, rows, lo, hi in (
            (pack, normed, slots_a, slots_b),
            (arrival, block_out, out_lo, out_hi),
            (own, block_out, own_lo, own_hi),
        ):
            for at_row in range(0, index.shape[0], 512):
                some = slice(at_row, at_row + 512)
                packed = mm(one_hot_cols(index[some, :], rows.shape[0]), rows[...]).astype(bf16)
                lo[some, :] = packed[:, :HALF]
                hi[some, :] = packed[:, HALF:]
        for chunk in (2, 3):
            for copy in copies(chunk):
                copy.wait()


def text_last(
    blocks, grad_a, grad_b, take, place, grad_two, resid_one, embed, qkv_rows, mix_rows, start, vecs,
    qkv_lo, qkv_hi, out_lo, out_hi, cq_lo, cq_hi,
    grad_embed, rows_a, rows_b, grad_lo, grad_hi, vec_grad,
    grad_mix, grad_queries, total, sums, grad_one,
):
    count = blocks[0]

    def keep(first, value):
        low = value.astype(bf16)
        width = value.shape[1]
        grad_lo[:, first : first + width] = low[:HALF]
        grad_hi[:, first : first + width] = low[HALF:]

    def turned_back(rows, lo, hi):
        return jnp.concatenate([mm_rt(rows, lo[...]), mm_rt(rows, hi[...])], axis=1)

    masks = head_masks(bf16)
    masks_f = head_masks(f32)
    vec_grad[...] = jnp.zeros_like(vec_grad)
    total[...] = jnp.zeros_like(total)
    sums[...] = jnp.zeros_like(sums)
    grad_embed[...] = jnp.zeros_like(grad_embed)

    def begin(first):
        rows = pl.ds(first, ROWS)
        places = lax.broadcasted_iota(i32, (ROWS, take.shape[1]), 0) + first
        hit = jnp.where(places == take[...], 1.0, 0.0).astype(bf16)
        grad_q = jnp.concatenate([mm(hit, grad_a[...]), mm(hit, grad_b[...])], axis=1).astype(bf16)
        unit, factor = normalise(resid_one[rows, :])
        normed = (unit * vecs[2:3, :] + vecs[3:4, :]).astype(bf16)
        sums[:, :D] += mm_lt(normed, grad_q)
        incoming = turned_back(grad_q, cq_lo, cq_hi)
        vec_grad[2:3, :] += jnp.sum(incoming * unit, axis=0, keepdims=True)
        vec_grad[3:4, :] += jnp.sum(incoming, axis=0, keepdims=True)
        grad = grad_two[rows, :] + norm_back(incoming, unit, factor, vecs[2:3, :])
        grad_one[rows, :] = grad
        grad = grad.astype(bf16)
        sums[:, D : 2 * D] += mm_lt(mix_rows[rows, :], grad)
        grad_mix[rows, :] = turned_back(grad, out_lo, out_hi).astype(bf16)

    def attend(first):
        rows = pl.ds(first, BLOCK)
        key_first = key_span(first)
        span = pl.ds(key_first, SPAN)
        allowed = self_allowed(start[rows, :], first, key_first)
        for quad in range(QUADS):
            lanes, keys, values = quad_lanes(quad)
            query = spread_heads(qkv_rows[rows, lanes], masks)
            grad = spread_heads(grad_mix[rows, lanes], masks)
            key_rows = qkv_rows[span, keys]
            shares = softmax(mm_rt(query, key_rows), allowed)
            grad_shares = mm_rt(grad, qkv_rows[span, values])
            inner = jnp.sum(grad_shares * shares, axis=-1, keepdims=True)
            grad_scores = (shares * (grad_shares - inner)).astype(bf16)
            back = join_heads(mm(grad_scores, key_rows), masks_f) * SCALE
            grad_queries[rows, lanes] = back.astype(bf16)
            later = slice(D + quad * QUAD, D + (quad + 1) * QUAD)
            total[span, lanes] += mm_lt(grad_scores, query) * SCALE
            total[span, later] += mm_lt(shares.astype(bf16), grad)

    def end(first):
        rows = pl.ds(first, ROWS)
        unit, factor = normalise(embed[rows, :].astype(f32))
        normed = (unit * vecs[0:1, :] + vecs[1:2, :]).astype(bf16)
        grad = jnp.concatenate([grad_queries[rows, :], total[rows, :].astype(bf16)], axis=1)
        for third in range(3):
            columns = slice(third * D, (third + 1) * D)
            sums[:, columns] += mm_lt(normed, grad[:, columns])
        incoming = turned_back(grad, qkv_lo, qkv_hi)
        vec_grad[0:1, :] += jnp.sum(incoming * unit, axis=0, keepdims=True)
        vec_grad[1:2, :] += jnp.sum(incoming, axis=0, keepdims=True)
        grad = grad_one[rows, :] + norm_back(incoming, unit, factor, vecs[0:1, :])
        grad_embed[rows, :] = grad.astype(bf16)

    chunks_of(count, ROWS, begin)
    keep(4 * D, sums[:, :D])
    keep(3 * D, sums[:, D : 2 * D])
    chunks_of(count * (ROWS // BLOCK), BLOCK, attend)
    sums[...] = jnp.zeros_like(sums)
    chunks_of(count, ROWS, end)
    keep(0, sums[...])
    half = rows_a.shape[0]
    rows_a[...] = mm(one_hot_rows(place[...], half), grad_embed[...]).astype(bf16)
    rows_b[...] = mm(one_hot_rows(place[...], half, half), grad_embed[...]).astype(bf16)


def unpack_rows(rows_a, rows_b, place, embed):
    count = rows_a.shape[0]
    total = mm(one_hot_cols(place[...], count), rows_a[...])
    total = total + mm(one_hot_cols(place[...] - count, count), rows_b[...])
    embed[...] = total.astype(bf16)


def pack_half(index, rows, packed):
    packed[...] = mm(one_hot_cols(index[...], rows.shape[0]), rows[...].astype(bf16)).astype(bf16)


def join_cotangent(arrival, own, slots_a, slots_b, rows, joined):
    height = joined.shape[0]
    low = mm(one_hot_rows(own[...], height), rows[...].astype(bf16))
    hit = one_hot_rows(arrival[...], height)
    joined[:, :HALF] = (low[:, :HALF] + mm(hit, slots_a[...])).astype(bf16)
    joined[:, HALF:] = (low[:, HALF:] + mm(hit, slots_b[...])).astype(bf16)


def join_output(slot_rows, slots, own, joined):
    total = mm(one_hot_rows(slot_rows[...], joined.shape[0]), slots[...])
    joined[...] = (total + own[...].astype(f32)).astype(bf16)


def join_kv(w_kv, k_lo, k_hi, v_lo, v_hi):
    for first, (lo, hi) in enumerate(((k_lo, k_hi), (v_lo, v_hi))):
        for part in range(2):
            columns = slice((2 * part + first) * HALF, (2 * part + first + 1) * HALF)
            w_kv[:HALF, columns] = lo[:, part * HALF : (part + 1) * HALF]
            w_kv[HALF:, columns] = hi[:, part * HALF : (part + 1) * HALF]


def stem_forward(
    features, bn, w_patch, patch_bias, k_lo, k_hi, v_lo, v_hi, patches, kv_lo, kv_hi, w_kv
):
    @pl.when(pl.program_id(0) == 0)
    def _():
        join_kv(w_kv, k_lo, k_hi, v_lo, v_hi)

    normed = (features[...].astype(f32) - bn[0:1, :]) * bn[1:2, :]
    hidden = gelu_only(normed * bn[2:3, :] + bn[3:4, :]).astype(bf16)
    rows = (mm(hidden, w_patch[...]) + patch_bias[...]).astype(bf16)
    patches[...] = rows
    kv_lo[...] = mm(rows, w_kv[:, :D]).astype(bf16)
    kv_hi[...] = mm(rows, w_kv[:, D:]).astype(bf16)


def image_window(image):
    first = image * PATCH
    aligned = pl.multiple_of(first // 16 * 16, 16)
    lanes = lax.broadcasted_iota(i32, (1, WINDOW), 1) + (aligned - first)
    return aligned, (lanes >= 0) & (lanes < PATCH)


def cross_forward(queries, kv, mixed):
    masks = head_masks(bf16, HALF)
    masks_f = head_masks(f32, HALF)

    def image(index, carry):
        aligned, allowed = image_window(index)
        window = pl.ds(aligned, WINDOW)
        place = pl.ds(pl.multiple_of(index * LONGEST, LONGEST), LONGEST)
        scores = mm_rt(spread_heads(queries[place, :], masks), kv[window, :HALF])
        shares = softmax(scores, allowed).astype(bf16)
        mixed[place, :] = join_heads(mm(shares, kv[window, HALF:]), masks_f).astype(bf16)
        return carry

    lax.fori_loop(0, IMG_DEV, image, 0, unroll=4)


def cross_backward(queries, grads, kv, grad_q, grad_kv):
    grad_kv[...] = jnp.zeros_like(grad_kv)
    masks = head_masks(bf16, HALF)
    masks_f = head_masks(f32, HALF)

    def image(index, carry):
        aligned, allowed = image_window(index)
        window = pl.ds(aligned, WINDOW)
        place = pl.ds(pl.multiple_of(index * LONGEST, LONGEST), LONGEST)
        query = spread_heads(queries[place, :], masks)
        grad = spread_heads(grads[place, :], masks)
        keys = kv[window, :HALF]
        shares = softmax(mm_rt(query, keys), allowed)
        grad_shares = mm_rt(grad, kv[window, HALF:])
        inner = jnp.sum(grad_shares * shares, axis=-1, keepdims=True)
        grad_scores = (shares * (grad_shares - inner)).astype(bf16)
        grad_q[place, :] = (join_heads(mm(grad_scores, keys), masks_f) * SCALE).astype(bf16)
        grad_kv[window, :HALF] += (mm_lt(grad_scores, query) * SCALE).astype(bf16)
        grad_kv[window, HALF:] += mm_lt(shares.astype(bf16), grad).astype(bf16)
        return carry

    lax.fori_loop(0, IMG_DEV, image, 0, unroll=4)


def stem_backward_kv(
    k_lo, k_hi, v_lo, v_hi, patches, grad_kv_lo, grad_kv_hi,
    grad_rows, grad_lo, grad_hi, bias_sum,
    w_kv, total,
):
    step = pl.program_id(0)

    @pl.when(step == 0)
    def _():
        join_kv(w_kv, k_lo, k_hi, v_lo, v_hi)
        total[...] = jnp.zeros_like(total)
        bias_sum[...] = jnp.zeros_like(bias_sum)

    rows = mm_rt(grad_kv_lo[...], w_kv[:, :D]) + mm_rt(grad_kv_hi[...], w_kv[:, D:])
    rows = rows.astype(bf16)
    grad_rows[...] = rows
    bias_sum[...] += jnp.sum(rows.astype(f32), axis=0, keepdims=True)
    turned = patches[...].T
    total[:, :D] += mm(turned, grad_kv_lo[...])
    total[:, D:] += mm(turned, grad_kv_hi[...])

    @pl.when(step == pl.num_programs(0) - 1)
    def _():
        for first in range(2):
            for part in range(2):
                source = slice((2 * part + first) * HALF, (2 * part + first + 1) * HALF)
                target = slice((2 * first + part) * HALF, (2 * first + part + 1) * HALF)
                grad_lo[:, target] = total[:HALF, source].astype(bf16)
                grad_hi[:, target] = total[HALF:, source].astype(bf16)


def stem_backward(
    features, bn, w_patch, grad_rows, grad_lo, grad_hi, grad_patch_w, sums, patch_acc
):
    step = pl.program_id(0)

    @pl.when(step == 0)
    def _():
        patch_acc[...] = jnp.zeros_like(patch_acc)
        sums[...] = jnp.zeros_like(sums)

    normed = (features[...].astype(f32) - bn[0:1, :]) * bn[1:2, :]
    hidden, slope = gelu_parts(normed * bn[2:3, :] + bn[3:4, :])
    patch_acc[...] += mm_lt(hidden.astype(bf16), grad_rows[...])
    grad_pre = mm_rt(grad_rows[...], w_patch[...]) * slope
    sums[0:1, :] += jnp.sum(grad_pre * normed, axis=0, keepdims=True)
    sums[1:2, :] += jnp.sum(grad_pre, axis=0, keepdims=True)
    grad_low = grad_pre.astype(bf16)
    grad_lo[...] = grad_low[:, : CH // 2]
    grad_hi[...] = grad_low[:, CH // 2 :]

    @pl.when(step == pl.num_programs(0) - 1)
    def _():
        grad_patch_w[...] = patch_acc[...].astype(bf16)


def place_pieces(where_, two, four, two_other, four_other, first, second, *scratch, split):
    dp_index, section = where_[0], where_[1]
    width, all_width = first.shape[-1], two.shape[-1]
    cuts = (slice(0, width), slice(width, all_width))
    sems = scratch[-1]

    def pieces(part, jobs):
        copies = []
        for core, sources in ((1 - part, (two_other, four_other)), (part, (two, four))):
            for z in range(4):
                for far, turn, bits in ((0, 0, 0), (0, 1, 1 + core), (1, 0, 2 - core), (1, 1, 3)):
                    target = dp_index ^ (4 * z) ^ bits
                    for cut, place in jobs:
                        copies.append(
                            pltpu.make_async_copy(
                                sources[far].at[turn, z, :, cut],
                                place.at[core, target],
                                sems.at[len(copies)],
                            )
                        )
        for copy in copies:
            copy.start()
        for copy in copies:
            copy.wait()

    for part in range(2):

        @pl.when(section == part)
        def _():
            if split:
                out = (second, first)[part]
                buffer = (scratch[1], scratch[0])[part]
                pieces(part, [(cuts[1 - part], buffer)])
                final = pltpu.make_async_copy(buffer, out, sems.at[0])
                final.start()
                final.wait()
            else:
                pieces(part, [(cuts[0], first), (cuts[1], second)])


def shape(dims, dtype):
    return jax.ShapeDtypeStruct(dims, dtype)


def whole(array):
    zeros = (0,) * len(array.shape)
    return pl.BlockSpec(array.shape, lambda *_: zeros, pipeline_mode=pl.Buffered(1))


def at(dims, *index):
    return pl.BlockSpec(dims, lambda *_: index)


def call(kernel, steps, in_specs, out_specs, outs, scratch, flops):
    return pl.pallas_call(
        kernel,
        grid=(steps,),
        in_specs=in_specs,
        out_specs=out_specs,
        out_shape=outs,
        scratch_shapes=scratch,
        compiler_params=pltpu.CompilerParams(vmem_limit_bytes=VMEM_BYTES),
        cost_estimate=pl.CostEstimate(flops=flops, bytes_accessed=0, transcendentals=0),
    )


def simple(kernel, inputs, outs, scratch, flops):
    return call(
        kernel,
        1,
        [whole(a) for a in inputs],
        [at(o.shape, *(0,) * len(o.shape)) for o in outs],
        outs,
        scratch,
        flops,
    )(*inputs)


def blank(outs):
    return pl.pallas_call(
        lambda *refs: None,
        out_shape=outs,
        out_specs=[pl.BlockSpec(memory_space=pl.ANY) for _ in outs],
    )()


barrier = lax.optimization_barrier


class Lines:
    def __init__(self, dp, dp_index, section):
        self.dp, self.dp_index, self.section = dp, dp_index, section
        self.is_stem = section == 0
        self.by_hand = dp == 16
        self.x, self.y, self.z = dp_index & 1, dp_index // 2 & 1, dp_index // 4

    def across(self, array, low, high):
        count = self.dp
        pairs = [(d, d ^ low) for d in range(count)]
        pairs += [(count + d, count + (d ^ high)) for d in range(count)]
        return lax.ppermute(array, BOTH, pairs)

    def swap(self, array):
        return lax.ppermute(array, "section", [(0, 1), (1, 0)])

    def gather_line(self, shard):
        return jnp.stack([shard] + [self.across(shard, 4 * k, 4 * k) for k in (1, 2, 3)])

    def gather_first(self, line):
        return jnp.stack([line, self.across(line, 1, 2)])

    def gather_second(self, two):
        return two, self.across(two, 2, 1)

    def gather_place(self, two, four, text_width):
        inputs = [two, four, self.swap(two), self.swap(four)]
        split = text_width is not None
        any_spec = pl.BlockSpec(memory_space=pl.ANY)
        rows, width = two.shape[2:]
        count = 2 * self.dp
        first = text_width if split else CH
        shapes = [(2, self.dp, rows, w) for w in (first, width - first)]
        buffers = [pltpu.VMEM(dims, bf16) for dims in shapes] if split else []
        out_spec = any_spec if split else pl.BlockSpec(memory_space=pltpu.VMEM)
        placed = pl.pallas_call(
            functools.partial(place_pieces, split=split),
            in_specs=[pl.BlockSpec(memory_space=pltpu.SMEM)] + [any_spec] * 4,
            out_specs=[out_spec] * 2,
            out_shape=[shape(dims, bf16) for dims in shapes],
            scratch_shapes=buffers + [pltpu.SemaphoreType.DMA((2 * count,))],
            compiler_params=pltpu.CompilerParams(vmem_limit_bytes=VMEM_BYTES),
        )(jnp.stack([self.dp_index, self.section]), *inputs)
        return [p.reshape(count * rows, p.shape[-1]) for p in placed]

    def fold_small(self, stats, vector, rows):
        first = lax.reduce_precision(stats, 8, 7)
        second = lax.reduce_precision(stats - first, 8, 7)
        third = stats - first - second
        terms = jnp.stack([first, second, third]).astype(bf16).reshape(rows, -1)
        count = rows * 128 - vector.shape[0]
        vector = jnp.concatenate([vector.astype(bf16), jnp.zeros((count,), bf16)])
        return jnp.concatenate([terms, vector.reshape(rows, 128)], axis=1)

    def unfold_small(self, shared, count, each):
        shared = shared.reshape(2, self.dp, -1, shared.shape[-1])
        stats = shared[0, :, :, :-128].astype(f32).reshape(self.dp, 3, 2, CH)
        stats = stats[:, 0] + stats[:, 1] + stats[:, 2]
        center = jnp.mean(stats[:, 0], axis=0)
        squares = jnp.sum(stats[:, 1] + each * jnp.square(stats[:, 0] - center), axis=0)
        lines = (count + 127) // 128
        vector = shared[:, :, :lines, -128:].reshape(2 * self.dp, lines * 128)[:, :count]
        return center, squares, vector.reshape(-1).astype(f32)

    def share_patch(self, project_low):
        count = self.dp // 2
        half = project_low.shape[0] // 2
        moved = lax.ppermute(project_low[half:], BOTH, [(d, d + count) for d in range(count)])
        mine = jnp.where(self.z < 2, project_low[:half], moved)
        moved = lax.ppermute(mine[half // 2 :], "section", [(0, 1)])
        return jnp.where(self.is_stem, mine[: half // 2], moved)

    def fold_patch(self, part, rows):
        rest = part.shape[0] - rows
        width = D * rest // rows
        tail = [part[rows:, first : first + width] for first in range(0, D, width)]
        return jnp.concatenate([part[:rows], jnp.concatenate(tail)], axis=1)

    def unfold_patch(self, parts):
        count, rows, width = parts.shape
        rest = rows * (width - D) // D
        tail = [parts[:, first : first + rest, D:] for first in range(0, rows, rest)]
        parts = jnp.concatenate([parts[:, :, :D], jnp.concatenate(tail, axis=2)], axis=1)
        parts = parts.reshape(2, 2, self.dp // 2, rows + rest, D)
        return parts.transpose(2, 1, 0, 3, 4).reshape(-1, D)

    def pick(self, places, axis, place):
        return lax.dynamic_index_in_dim(places, place, axis, keepdims=False)

    def first_half(self, terms, flip):
        along_y = [self.pick(stem, 1, self.y ^ flip) for stem, _ in terms]
        along_x = [self.pick(text, 2, self.x ^ flip) for _, text in terms]
        parts = [jnp.where(self.is_stem, *both) for both in zip(along_y, along_x)]
        return jnp.concatenate(parts, axis=-1)

    def second_half(self, terms, got, flip):
        place = jnp.where(self.is_stem, self.x, self.y) ^ flip
        kept = self.pick(self.first_half(terms, 0), 1, place).astype(f32)
        return (kept + self.pick(got, 1, place).astype(f32)).astype(bf16)

    def sum_first(self, terms):
        return self.across(self.first_half(terms, 1), 2, 1)

    def sum_second(self, terms, got):
        return self.across(self.second_half(terms, got, 1), 1, 2)

    def line_of(self, terms, got, got_two):
        kept = self.second_half(terms, got, 0).astype(f32)
        return (kept + got_two.astype(f32)).astype(bf16)

    def sum_line(self, line):
        groups = [[c + 4 * z for z in range(4)] for c in range(4)]
        return lax.all_to_all(
            line, "dp", split_axis=0, concat_axis=0, axis_index_groups=groups, tiled=True
        )

    def line_total(self, parts):
        return jnp.sum(parts.astype(f32), axis=0)

    def sum_low_first(self, line):
        return self.across(line, 8, 8)

    def sum_low_last(self, line, got):
        line = (line.astype(f32) + got.astype(f32)).astype(bf16)
        low = self.z & 1
        got = self.across(self.pick(line, 0, 1 - low), 4, 4)
        return self.pick(line, 0, low).astype(f32) + got.astype(f32)

    def scatter_plain(self, w_lo, w_hi, kv_lo, kv_hi, patch):
        def total(term):
            return lax.psum_scatter(term, BOTH, scatter_dimension=0, tiled=True).astype(f32)

        own_w = jnp.concatenate([w_lo, w_hi])
        own_kv = jnp.concatenate([kv_lo, kv_hi])
        own_patch = jnp.concatenate([patch, jnp.zeros((FF, D), bf16)])
        return (
            total(
                jnp.concatenate(
                    [
                        jnp.where(self.is_stem, jnp.zeros_like(own_w), own_w),
                        jnp.where(self.is_stem, own_kv, jnp.zeros_like(own_kv)),
                    ],
                    axis=1,
                )
            ),
            total(jnp.where(self.is_stem, own_patch, jnp.zeros_like(own_patch))),
        )


def sgd_update(gradient, momentum, master, average, step_rate):
    new_momentum = 0.9 * momentum + gradient
    new_master = master - step_rate * (gradient + 0.9 * new_momentum)
    new_average = 0.8 * average + 0.2 * new_master
    return (gradient, new_momentum, new_average, new_master, new_master.astype(bf16))


def per_device(
    features,
    image_group,
    token_ids,
    text_lengths,
    cotangent,
    table_master,
    table_momentum,
    table_average,
    block_master,
    block_momentum,
    block_average,
    project_master,
    project_momentum,
    project_average,
    vector_master,
    vector_momentum,
    vector_average,
):
    dp = lax.axis_size("dp")
    group = lax.axis_size(BOTH)
    dp_index = lax.axis_index("dp")
    section = lax.axis_index("section")
    is_stem = section == 0
    me = section * dp + dp_index
    tokens = token_ids.shape[0]
    image_rows = features.shape[0]
    every_patch = image_rows * dp
    table_rows = table_master.shape[0]
    images = image_group.shape[0]

    lines = Lines(dp, dp_index, section)
    block_low = block_master.astype(bf16)
    project_low = project_master.astype(bf16)
    early = block_low[:, : 7 * D]
    late_low = jnp.concatenate(
        [
            block_low[:, 8 * D :],
            block_low[:, 7 * D : 8 * D],
            jnp.zeros((block_low.shape[0], CH - D), bf16),
        ],
        axis=1,
    )
    project_rows = project_master.shape[0]
    if lines.by_hand:
        rows = late_low.shape[0]
        down_low = project_low.T.reshape(-1, rows, 128).transpose(1, 0, 2).reshape(rows, CH + FF)
        late_low = jnp.concatenate([down_low, late_low], axis=1)

    def send(block):
        return lax.all_to_all(block, "dp", split_axis=0, concat_axis=0, tiled=True)

    capacity = (2 * IMG_DEV + dp - 1) // dp
    slots = dp * capacity
    destination = image_group // GROUPS_DEV
    by_source = destination.reshape(dp, IMG_DEV)
    order = jnp.arange(IMG_DEV, dtype=i32)
    earlier = order[None, :] < order[:, None]
    rank_all = jnp.sum(
        ((by_source[:, :, None] == by_source[:, None, :]) & earlier[None]).astype(i32), axis=2
    ).reshape(images)
    my_dest = lax.dynamic_slice_in_dim(destination, dp_index * IMG_DEV, IMG_DEV)
    my_rank = lax.dynamic_slice_in_dim(rank_all, dp_index * IMG_DEV, IMG_DEV)
    stem_slot = my_dest * capacity + my_rank
    slot_of_image = jnp.where(
        destination == dp_index,
        jnp.arange(images, dtype=i32) // IMG_DEV * capacity + rank_all,
        -1,
    )
    lengths = text_lengths[0]
    group_ends = jnp.cumsum(lengths)
    group_starts = group_ends - lengths
    places = jnp.arange(tokens, dtype=i32)
    groups = jnp.arange(GROUPS_DEV, dtype=i32)
    named = jnp.any(image_group[None, :] == (dp_index * GROUPS_DEV + groups)[:, None], axis=1)
    within_group = (group_starts[None, :] <= places[:, None]) & (
        places[:, None] < group_ends[None, :]
    )
    token_start = jnp.sum(jnp.where(within_group, group_starts[None, :], 0), axis=1)
    token_named = jnp.any(within_group & named[None, :], axis=1)
    match = slot_of_image[None, :] == jnp.arange(slots, dtype=i32)[:, None]
    slot_group = jnp.max(jnp.where(match, (image_group % GROUPS_DEV)[None, :], -1), axis=1)
    group_hit = slot_group[:, None] == groups[None, :]
    slot_start = jnp.sum(jnp.where(group_hit, group_starts[None, :], 0), axis=1)
    slot_length = jnp.sum(jnp.where(group_hit, lengths[None, :], 0), axis=1)
    within = jnp.arange(LONGEST, dtype=i32)
    slot_rows = jnp.where(
        within[None, :] < slot_length[:, None], slot_start[:, None] + within[None, :], -1
    ).reshape(slots * LONGEST)
    slot_ids = jnp.max(
        jnp.where(slot_rows[:, None] == places[None, :], token_ids[None, :], -1), axis=1
    )

    slot_ids, features = barrier((slot_ids, features))
    rows_f = features.astype(f32)
    local_center = jnp.mean(rows_f, axis=0)
    local_square = jnp.sum(jnp.square(rows_f - local_center), axis=0)
    state = jnp.stack([local_center, local_square])
    vector_low = lax.reduce_precision(vector_master, 8, 7)
    if lines.by_hand:
        later = jnp.concatenate(
            [
                lines.fold_patch(lines.share_patch(project_low), early.shape[0]),
                lines.fold_small(state, vector_low, early.shape[0]),
            ],
            axis=1,
        )
        early = lines.gather_line(early)

    got_ids = send(slot_ids.reshape(dp, capacity * LONGEST)).reshape(slots, LONGEST)
    slot_hit = stem_slot[:, None] == jnp.arange(slots, dtype=i32)[None, :]
    image_ids = jnp.max(jnp.where(slot_hit[:, :, None], got_ids[None], -1), axis=1)
    ids = jnp.concatenate([image_ids.reshape(-1), jnp.where(token_named, -1, token_ids)])
    height = ids.shape[0]
    here = ids >= 0
    candidates = jnp.arange(height, dtype=i32)
    before = candidates[None, :] < candidates[:, None]
    row = jnp.sum((before & here[None, :]).astype(i32), axis=1)
    row = jnp.where(here, row, -1)
    row_count = jnp.sum(here.astype(i32))
    row_blocks = ((row_count + ROWS - 1) // ROWS).reshape(1)
    depth = jnp.concatenate(
        [jnp.tile(within, IMG_DEV), places - token_start]
    )
    image_row, own_row = row[: IMG_DEV * LONGEST], row[IMG_DEV * LONGEST :]
    arrival_row = jnp.max(
        jnp.where(slot_hit[:, :, None], image_row.reshape(IMG_DEV, 1, LONGEST), -1), axis=0
    ).reshape(slots * LONGEST)
    chosen = row[None, :] == candidates[:, None]
    start = jnp.max(jnp.where(chosen, (row - depth)[None, :], -1), axis=1)
    start = jnp.where(candidates < row_count, start, candidates)[:, None]

    room = max(16, 2 * tokens // group)
    half_room = dp * room
    owner = ids // table_rows
    same = (ids[:, None] == ids[None, :]) & here[None, :]
    is_first = here & ~jnp.any(same & before, axis=1)
    rank = jnp.sum(
        ((owner[:, None] == owner[None, :]) & before & is_first[None, :]).astype(i32), axis=1
    )
    rounds_here = jnp.max(jnp.where(is_first, rank, 0)) // room + 1
    table_low = table_master.astype(bf16)

    def round_of(turn):
        turn_rank = rank - turn * room
        first_place = jnp.where(
            is_first & (turn_rank >= 0) & (turn_rank < room), owner * room + turn_rank, -1
        )
        place = jnp.max(jnp.where(same, first_place[None, :], -1), axis=1)
        place = jnp.max(jnp.where(chosen, place[None, :], -1), axis=1)
        slot = jnp.arange(half_room, dtype=i32) + section * half_room
        asked = jnp.max(
            jnp.where(first_place[None, :] == slot[:, None], (ids % table_rows)[None, :], -1),
            axis=1,
        )
        return place, asked.reshape(dp, room)

    def serve(asked):
        hit = (asked[:, None] == jnp.arange(table_rows, dtype=i32)[None, :]).astype(bf16)
        served = mm(hit, table_low).astype(bf16)
        return send(served.reshape(dp, room, D)).reshape(half_room, D)

    def unpacked(place, served, served_low):
        return simple(
            unpack_rows,
            [served_low, served, place[:, None]],
            [shape((height, D), bf16)],
            [],
            4 * 10**9,
        )[0]

    cot_sum = jnp.sum(cotangent, axis=0)
    arrival_shape = shape((slots * LONGEST, HALF), bf16)
    cot_sent = simple(
        pack_half,
        [slot_rows[:, None], lax.dynamic_slice_in_dim(cotangent, section * HALF, HALF, axis=1)],
        [arrival_shape],
        [],
        3 * 10**9,
    )[0]
    if lines.by_hand:
        got_ids, early, later, cot_sent, cot_sum = barrier(
            (got_ids, early, later, cot_sent, cot_sum)
        )
        early = lines.gather_first(early)
        later = lines.gather_line(later)
    place, asked = round_of(0)
    asked = jnp.concatenate([asked, jnp.broadcast_to(rounds_here, (dp, 1))], axis=1)
    asked = send(asked)
    if lines.by_hand:
        asked, early, later, cot_sent = barrier((asked, early, later, cot_sent))
        early = lines.gather_second(early)
        later = lines.gather_first(later)
        cot_b = send(cot_sent.reshape(dp, capacity * LONGEST, HALF))
        cot_b = cot_b.reshape(slots * LONGEST, HALF)
    rounds = jnp.max(asked[:, room])
    asked = asked[:, :room].reshape(half_room)
    served = serve(asked)
    served_low = lax.ppermute(served, "section", [(0, 1)])
    if lines.by_hand:
        served, served_low, early, later, place, start, late_low, cot_b = barrier(
            (served, served_low, early, later, place, start, late_low, cot_b)
        )
        w_late = w_down = lax.all_gather(late_low, BOTH, axis=0, tiled=True)
        later = lines.gather_second(later)
        w_text, w_kv = lines.gather_place(*early, 5 * D)
        w_patch, shared = lines.gather_place(*later, None)
        w_patch = lines.unfold_patch(w_patch.reshape(2 * dp, -1, CH))
        center, squares, flat = lines.unfold_small(shared, vector_master.shape[0], image_rows)
    else:
        w_text = lax.all_gather(early[:, : 5 * D], BOTH, axis=0, tiled=True)
        w_kv = lax.all_gather(early[:, 5 * D :], BOTH, axis=0, tiled=True)
        cot_b = send(cot_sent.reshape(dp, capacity * LONGEST, HALF))
        cot_b = cot_b.reshape(slots * LONGEST, HALF)
        w_late = lax.all_gather(late_low, BOTH, axis=0, tiled=True)
        project_full = lax.all_gather(project_low, BOTH, axis=0, tiled=True)
        w_down = project_full.T
        w_patch = project_full[:CH]
        stats = lax.all_gather(state, "dp")
        center = jnp.mean(stats[:, 0], axis=0)
        squares = jnp.sum(stats[:, 1] + image_rows * jnp.square(stats[:, 0] - center), axis=0)
        flat = lax.all_gather(vector_low, BOTH, axis=0, tiled=True)
    factor = lax.rsqrt(squares / every_patch + EPS)
    bn_gain, bn_bias = flat[:CH], flat[CH : 2 * CH]
    offset = 2 * CH + D
    patch_bias = flat[2 * CH : offset].reshape(1, D)
    ln_vecs = flat[offset : offset + 6 * D].reshape(6, D)
    up_bias = flat[offset + 6 * D : offset + 6 * D + FF].reshape(1, FF)
    down_bias = flat[offset + 6 * D + FF :].reshape(1, D)
    vecs_outer = ln_vecs[:4]
    vecs_three = jnp.concatenate([ln_vecs[4:], down_bias])
    bn = jnp.stack([center, factor, bn_gain, bn_bias])

    def embed_more(turn, embed):
        place, asked = round_of(turn)
        served = serve(send(asked).reshape(half_room))
        return embed + unpacked(place, served, lax.ppermute(served, "section", [(0, 1)]))

    embed = lax.fori_loop(1, rounds, embed_more, unpacked(place, served, served_low))

    if lines.by_hand:
        w_text, w_kv, w_patch, embed = barrier((w_text, w_kv, w_patch, embed))

    def halves(width, column):
        return [at((HALF, width), 0, column), at((HALF, width), 1, column)]

    qkv_specs = halves(3 * D, 0) + halves(D, 3) + halves(D, 4)
    qkv_inputs = [w_text] * 6
    kv_specs = halves(D, 0) + halves(D, 1)
    kv_inputs = [w_kv] * 4
    patch_spec = at((CH, D), 0, 0)
    blocks = 7
    per_block = image_rows // blocks
    qkv_scratch = [
        pltpu.VMEM((D, 3 * D), bf16),
        pltpu.VMEM((D, D), bf16),
        pltpu.VMEM((D, D), bf16),
        pltpu.VMEM((height, D), bf16),
    ]

    def rows_spec(width):
        return pl.BlockSpec((per_block, width), lambda step: (step, 0))

    slot_shape = shape((IMG_DEV * LONGEST, HALF), bf16)
    blocks_spec = pl.BlockSpec(memory_space=pltpu.SMEM)
    pack, take = image_row[:, None], image_row[None, :]
    rows_shape = shape((image_rows, D), bf16)

    text_saved = [
        shape((height, 3 * D), bf16),
        shape((height, D), bf16),
        shape((height, D), f32),
        slot_shape,
        slot_shape,
    ]
    stem_saved = [rows_shape] * 3

    def first_text():
        inputs = [embed, start, pack, vecs_outer]
        done = call(
            text_first,
            1,
            [blocks_spec] + [whole(a) for a in inputs] + qkv_specs,
            [whole(o) for o in text_saved],
            text_saved,
            qkv_scratch,
            15 * 10**9,
        )(row_blocks, *inputs, *qkv_inputs)
        return (*done, *blank(stem_saved))

    def first_stem():
        done = call(
            stem_forward,
            blocks,
            [rows_spec(CH), whole(bn), patch_spec, whole(patch_bias)] + kv_specs,
            [rows_spec(D)] * 3,
            stem_saved,
            [pltpu.VMEM((D, 2 * D), bf16)],
            23 * 10**9,
        )(features, bn, w_patch, patch_bias, *kv_inputs)
        return (*blank(text_saved), *done)

    qkv_rows, mix_rows, resid_one, q_a, q_b, patches, kv_lo, kv_hi = lax.cond(
        is_stem, first_stem, first_text
    )

    kv_moved = lax.ppermute(kv_hi, "section", [(0, 1)])

    def to_cores(block_a, block_b):
        return jnp.where(is_stem, lax.ppermute(block_a, "section", [(1, 0)]), block_b)

    q_here = to_cores(q_a, q_b)
    def cross(kv):
        return call(
            cross_forward,
            1,
            [whole(q_here), whole(kv)],
            [whole(q_here)],
            [slot_shape],
            [],
            8 * 10**9,
        )(q_here, kv)[0]

    mix_b = lax.cond(is_stem, lambda: cross(kv_lo), lambda: cross(kv_moved))

    mix_a = lax.ppermute(mix_b, "section", [(0, 1)])
    cot_a = lax.ppermute(cot_b, "section", [(0, 1)])
    grad_out = simple(
        join_cotangent,
        [arrival_row[None, :], own_row[None, :], cot_a, cot_b, cotangent],
        [shape((height, D), bf16)],
        [],
        4 * 10**9,
    )[0]

    chunks = 3
    wide = FF // chunks
    own_shape = shape((tokens, HALF), bf16)
    middle_shapes = [
        arrival_shape,
        arrival_shape,
        own_shape,
        own_shape,
        shape((height, D), f32),
        shape((D, 2 * (CH + FF)), bf16),
        slot_shape,
        slot_shape,
        shape((2, D), f32),
        shape((1, FF), f32),
    ]

    def middle_text():
        inputs = [
            mix_a, mix_b, take, pack, arrival_row[:, None], own_row[:, None],
            resid_one, grad_out, vecs_three,
        ]

        def chunk(step):
            return jnp.minimum(step, chunks - 1)

        if lines.by_hand:
            first_up = (CH + FF) // wide
            down_rows = D // (chunks + 1)
            down_spec = pl.BlockSpec((down_rows, CH + FF), lambda step: (1 + chunk(step), 0))
        else:
            first_up = 0
            down_rows = D
            down_spec = pl.BlockSpec((D, wide), lambda step: (0, 1 + chunk(step)))
        down_width = wide * D // down_rows
        outs = [whole(o) for o in middle_shapes]
        outs[5] = pl.BlockSpec(memory_space=pl.ANY)
        outs[9] = pl.BlockSpec((1, wide), lambda step: (0, chunk(step)))
        return call(
            text_middle,
            chunks + 1,
            [blocks_spec]
            + [whole(a) for a in inputs]
            + [pl.BlockSpec((1, wide), lambda step: (0, chunk(step)))]
            + halves(wide, first_up + chunks)
            + [
                pl.BlockSpec((HALF, wide), lambda step: (0, first_up + chunk(step))),
                pl.BlockSpec((HALF, wide), lambda step: (1, first_up + chunk(step))),
                down_spec,
            ],
            outs,
            middle_shapes,
            [
                pltpu.VMEM((D, D), bf16),
                pltpu.VMEM((D, wide), bf16),
                pltpu.VMEM((height, D), bf16),
                pltpu.VMEM((height, D), bf16),
                pltpu.VMEM((D, height), bf16),
                pltpu.VMEM((height, 1), f32),
                pltpu.VMEM((height, D), f32),
                pltpu.VMEM((height, D), f32),
                pltpu.VMEM((D, height), bf16),
                pltpu.VMEM((D, wide), f32),
                pltpu.VMEM((D, wide), f32),
                pltpu.VMEM((2, D, wide), bf16),
                pltpu.VMEM((2, down_rows, down_width), bf16),
                pltpu.VMEM((D, wide), bf16),
                pltpu.VMEM((height, D), bf16),
                pltpu.SemaphoreType.DMA((2, 2)),
            ],
            29 * 10**9,
        )(row_blocks, *inputs, up_bias, *[w_late] * 4, w_down)

    def middle_stem():
        made = list(blank(middle_shapes))
        made[5] = jnp.zeros(middle_shapes[5].shape, bf16)
        return tuple(made)

    (
        out_lo, out_hi, own_lo, own_hi, grad_two, late_term, g_a, g_b, grads_three, grad_up_bias,
    ) = lax.cond(is_stem, middle_stem, middle_text)
    if lines.by_hand:
        late_grad = lax.psum_scatter(late_term, BOTH, scatter_dimension=0, tiled=True)
    else:
        late_grad = lax.psum_scatter(
            late_term[:, : CH + FF], BOTH, scatter_dimension=0, tiled=True
        )
        down_turned = lax.psum_scatter(
            late_term[:, CH + FF :], BOTH, scatter_dimension=1, tiled=True
        )
    g_here = to_cores(g_a, g_b)
    out_here = to_cores(out_lo, out_hi)
    g_here, out_here = barrier((g_here, out_here))
    got_out = send(out_here.reshape(dp, capacity * LONGEST, HALF)).reshape(slots * LONGEST, HALF)

    def cross_back(kv):
        return tuple(
            call(
                cross_backward,
                1,
                [whole(q_here), whole(g_here), whole(kv)],
                [whole(q_here), whole(kv)],
                [slot_shape, rows_shape],
                [],
                0,
            )(q_here, g_here, kv)
        )

    grad_here, grad_kv = lax.cond(is_stem, lambda: cross_back(kv_lo), lambda: cross_back(kv_moved))
    grad_here, grad_kv, got_out = barrier((grad_here, grad_kv, got_out))
    grad_kv_moved = lax.ppermute(grad_kv, "section", [(1, 0)])

    stem_kv_shapes = [
        rows_shape,
        shape((HALF, 2 * D), bf16),
        shape((HALF, 2 * D), bf16),
        shape((1, D), f32),
    ]

    def stem_kv():
        return tuple(
            call(
                stem_backward_kv,
                blocks,
                kv_specs + [rows_spec(D)] * 3,
                [rows_spec(D)] + [at(o.shape, 0, 0) for o in stem_kv_shapes[1:]],
                stem_kv_shapes,
                [pltpu.VMEM((D, 2 * D), bf16), pltpu.VMEM((D, 2 * D), f32)],
                23 * 10**9,
            )(*kv_inputs, patches, grad_kv, grad_kv_moved)
        )

    grad_b = grad_here
    grad_rows, kv_w_lo, kv_w_hi, patch_bias_sum = lax.cond(
        is_stem, stem_kv, lambda: tuple(blank(stem_kv_shapes))
    )
    grad_a = lax.ppermute(grad_b, "section", [(0, 1)])
    grad_a, grad_rows = barrier((grad_a, grad_rows))

    row_shape = shape((half_room, D), bf16)
    text_last_shapes = [
        shape((height, D), bf16),
        row_shape,
        row_shape,
        shape((HALF, 5 * D), bf16),
        shape((HALF, 5 * D), bf16),
        shape((4, D), f32),
    ]
    half_channels = CH // 2
    stem_last_shapes = [
        shape((image_rows, half_channels), bf16),
        shape((image_rows, half_channels), bf16),
        shape((CH, D), bf16),
        shape((2, CH), f32),
    ]

    def last_text():
        inputs = [
            grad_a, grad_b, take, place[None, :], grad_two, resid_one, embed,
            qkv_rows, mix_rows, start, vecs_outer,
        ]
        done = call(
            text_last,
            1,
            [blocks_spec] + [whole(a) for a in inputs] + qkv_specs,
            [whole(o) for o in text_last_shapes],
            text_last_shapes,
            [
                pltpu.VMEM((height, D), bf16),
                pltpu.VMEM((height, D), bf16),
                pltpu.VMEM((height, 2 * D), f32),
                pltpu.VMEM((D, 3 * D), f32),
                pltpu.VMEM((height, D), f32),
            ],
            0,
        )(row_blocks, *inputs, *qkv_inputs)
        return (*done, *blank(stem_last_shapes))

    def last_stem():
        done = call(
            stem_backward,
            blocks,
            [rows_spec(CH), whole(bn), patch_spec, rows_spec(D)],
            [rows_spec(half_channels)] * 2 + [at(o.shape, 0, 0) for o in stem_last_shapes[2:]],
            stem_last_shapes,
            [pltpu.VMEM((CH, D), f32)],
            0,
        )(features, bn, w_patch, grad_rows)
        return (*blank(text_last_shapes), *done)

    (
        grad_embed, rows_low, rows_high, grad_w_lo, grad_w_hi, grads_outer,
        grad_lo, grad_hi, grad_patch_w, bn_sums,
    ) = lax.cond(is_stem, last_stem, last_text)

    def row_sums(asked, rows):
        hit = (jnp.arange(table_rows, dtype=i32)[:, None] == asked[None, :]).astype(bf16)
        return mm(hit, rows.reshape(half_room, D))

    def table_more(turn, total):
        place, asked = round_of(turn)
        slot = jnp.arange(group * room, dtype=i32)
        rows = mm((slot[:, None] == place[None, :]).astype(bf16), grad_embed).astype(bf16)
        moved = lax.ppermute(rows[:half_room], "section", [(1, 0)])
        rows = jnp.where(is_stem, moved, rows[half_room:]).reshape(dp, room, D)
        return total + row_sums(send(asked).reshape(half_room), send(rows))

    def table_update(total):
        return sgd_update(total, table_momentum, table_master, table_average, 0.05)

    def table_updated(got_rows):
        return lax.cond(
            rounds > 1,
            lambda: table_update(lax.fori_loop(1, rounds, table_more, row_sums(asked, got_rows))),
            lambda: table_update(row_sums(asked, got_rows)),
        )

    gone = jnp.zeros((), f32)
    vector_term = jnp.concatenate(
        [
            jnp.where(is_stem, bn_sums.reshape(-1), gone),
            jnp.where(is_stem, patch_bias_sum.reshape(-1), gone),
            jnp.where(
                is_stem,
                gone,
                jnp.concatenate(
                    [
                        grads_outer.reshape(-1),
                        grads_three.reshape(-1),
                        grad_up_bias.reshape(-1),
                        cot_sum,
                    ]
                ),
            ),
        ]
    ).reshape(-1, CH)

    def summed(vector, steps):
        for step in steps:
            vector = vector + lax.ppermute(vector, "dp", [(i, i ^ step) for i in range(dp)])
        return vector

    grad_w_lo, grad_w_hi, kv_w_lo, kv_w_hi = barrier(
        (grad_w_lo, grad_w_hi, kv_w_lo, kv_w_hi)
    )
    own_here = to_cores(own_lo, own_hi)

    def output(got_out):
        return simple(
            join_output,
            [slot_rows[None, :], got_out, own_here],
            [own_shape],
            [],
            3 * 10**9,
        )[0]

    if lines.by_hand:
        owners = CH // project_rows
        parts = grad_patch_w.reshape(owners, 2, project_rows // 2, D)
        terms = [
            (lax.ppermute(grad_w_lo, "section", [(1, 0)]), grad_w_hi),
            (kv_w_lo, lax.ppermute(kv_w_hi, "section", [(0, 1)])),
        ]
        terms = [
            tuple(w.reshape(4, 2, 2, HALF // dp, w.shape[1]) for w in term) for term in terms
        ]
        patch = (parts[:, 0], lax.ppermute(parts[:, 1], "section", [(0, 1)]))
        patch = [tuple(w.reshape(2, 2, 2, project_rows // 2, D) for w in patch)]
        terms, patch = barrier((terms, patch))
        first = lines.first_half(terms, 1)
        first, rows_low, vector_term = barrier((first, rows_low, vector_term))
        got = lines.across(first, 2, 1)
        patch_got = lines.sum_first(patch)
        vector_term = summed(vector_term, (4, 8))
        sent_rows = to_cores(rows_low, rows_high).reshape(dp, room, D)
        got_rows = send(sent_rows)
        got, patch_got, got_rows, vector_term = barrier((got, patch_got, got_rows, vector_term))
        got_two = lines.sum_second(terms, got)
        patch_got_two = lines.sum_second(patch, patch_got)
        table_new = table_updated(got_rows)
        got_two, patch_got_two, _, vector_term, grad_hi, got_out = barrier(
            (got_two, patch_got_two, table_new[0][:8, :128], vector_term, grad_hi, got_out)
        )
        line = lines.line_of(terms, got, got_two)
        patch_line = lines.line_of(patch, patch_got, patch_got_two)
        patch_got = lines.sum_low_first(patch_line)
        line, patch_got = barrier((line, patch_got))
        line_parts = lines.sum_line(line)
        vector_total = summed(vector_term, (1, 2))
        block_piece = output(got_out)
        got_hi = lax.ppermute(grad_hi, "section", [(0, 1)])
        line_parts, late_grad = barrier((line_parts, late_grad))
        tail_grad = lines.line_total(line_parts)
        patch_low = lines.sum_low_last(patch_line, patch_got)
        patch_high = lax.ppermute(patch_low, "section", [(1, 0)])
        down_grad = late_grad[:, CH + FF :].astype(f32).reshape(late_grad.shape[0], -1, 128)
        down_grad = down_grad.transpose(1, 0, 2).reshape(D, 128).T
        project_grad = down_grad + jnp.where(
            is_stem & (dp_index < owners), jnp.concatenate([patch_low, patch_high]), 0.0
        )
    else:
        vector_total = summed(vector_term, [1 << bit for bit in range(dp.bit_length() - 1)])
        got_rows = send(to_cores(rows_low, rows_high).reshape(dp, room, D))
        block_piece = output(got_out)
        got_hi = lax.ppermute(grad_hi, "section", [(0, 1)])
        table_new = table_updated(got_rows)
        tail_grad, patch_grad = lines.scatter_plain(
            grad_w_lo, grad_w_hi, kv_w_lo, kv_w_hi, grad_patch_w
        )
        project_grad = down_turned.astype(f32).T + patch_grad
    late_grad = late_grad.astype(f32)
    block_grad = jnp.concatenate(
        [tail_grad, late_grad[:, FF : FF + D], late_grad[:, :FF]], axis=1
    )
    vector_total = vector_total + lax.ppermute(vector_total, "section", [(0, 1), (1, 0)])
    vector_grad = lax.dynamic_slice_in_dim(
        vector_total.reshape(-1), me * vector_master.shape[0], vector_master.shape[0]
    )

    own_pre = jnp.where(is_stem, grad_lo, got_hi).astype(f32)
    first_channel = section * half_channels

    def own_half(array):
        return lax.dynamic_slice_in_dim(array, first_channel, half_channels, axis=array.ndim - 1)

    own_normed = (own_half(features).astype(f32) - own_half(center)) * own_half(factor)
    own_gain = own_half(bn_gain)
    feature_grad = own_half(factor) * (
        own_pre * own_gain
        - own_gain * own_half(vector_total[1]) / every_patch
        - own_normed * (own_gain * own_half(vector_total[0]) / every_patch)
    )

    root_tokens = math.sqrt(tokens * dp)
    block_new = sgd_update(
        block_grad, block_momentum, block_master, block_average, 0.5 * D ** (-0.5) / root_tokens
    )
    project_new = sgd_update(
        project_grad,
        project_momentum,
        project_master,
        project_average,
        0.5 * FF ** (-0.5) / root_tokens,
    )
    vector_new = sgd_update(
        vector_grad, vector_momentum, vector_master, vector_average, 0.1 / root_tokens
    )
    return (block_piece, feature_grad, *table_new, *block_new, *project_new, *vector_new)


def solution(mesh):
    rows = P(BOTH, None)
    flat = P(BOTH)
    placed = (
        (P("dp", None), P(), P("dp"), P("dp", None), P("dp", None))
        + (rows,) * 9
        + (flat,) * 3
    )
    return jax.shard_map(
        per_device,
        mesh=mesh,
        in_specs=placed,
        out_specs=(P("dp", "section"), P("dp", "section")) + (rows,) * 15 + (flat,) * 5,
        check_vma=False,
    )
```
